32 devices in a mesh: dp: 8 (over z, core), tensor: 4 (over y, x).
Axes of the slice: x: 2, y: 2, z: 4, core: 2. Of those that a mesh axis runs over, the one named last changes fastest.
Arguments:
- hidden_in: float32 [8192, 2048], P('dp'), may hold values from -16 to 16
- cotangent: bfloat16 [8192, 2048], P('dp'), may hold values from -6 to 6
- doc_lengths: int32 [8], replicated, may hold values from 1 to 7680, 8192 in all
- valid_mask: int32 [8192], P('dp'), may hold values from 0 to 1, as said below
- w_qkv: float32 [2048, 4096], P('dp', 'tensor'), may hold values from -0.125 to 0.125
- w_out: float32 [2048, 2048], P('tensor', 'dp'), may hold values from -1 to 1
- w_gate_up: float32 [2, 2048, 6144], P(None, 'dp', 'tensor'), may hold values from -0.125 to 0.125
- w_down: float32 [6144, 2048], P('tensor', 'dp'), may hold values from -0.078125 to 0.078125
- norm_gains: float32 [4352], replicated, may hold values from 0.3 to 2.8
- m_qkv: float32 [2048, 4096], P('dp', 'tensor'), may hold values from -256 to 256
- m_out: float32 [2048, 2048], P('tensor', 'dp'), may hold values from -256 to 256
- m_gate_up: float32 [2, 2048, 6144], P(None, 'dp', 'tensor'), may hold values from -256 to 256
- m_down: float32 [6144, 2048], P('tensor', 'dp'), may hold values from -256 to 256
- m_gains: float32 [4352], replicated, may hold values from -128 to 128
- a_qkv: float32 [2048, 4096], P('dp', 'tensor'), may hold values from -0.125 to 0.125
- a_out: float32 [2048, 2048], P('tensor', 'dp'), may hold values from -1 to 1
- a_gate_up: float32 [2, 2048, 6144], P(None, 'dp', 'tensor'), may hold values from -0.125 to 0.125
- a_down: float32 [6144, 2048], P('tensor', 'dp'), may hold values from -0.078125 to 0.078125
- a_gains: float32 [4352], replicated, may hold values from 0.3 to 2.8
Outputs:
- mixed_out: float32 [8192, 2048], P('dp', 'tensor')
- grad_input: float32 [8192, 2048], P('dp', 'tensor')
- branch_rms: float32 [3], replicated
- qkv_new: float32 [2048, 4096], P('dp', 'tensor')
- qkv_moment: float32 [2048, 4096], P('dp', 'tensor')
- qkv_average: float32 [2048, 4096], P('dp', 'tensor')
- qkv_average_b: bfloat16 [2048, 4096], P('dp', 'tensor')
- out_new: float32 [2048, 2048], P('tensor', 'dp')
- out_moment: float32 [2048, 2048], P('tensor', 'dp')
- out_average: float32 [2048, 2048], P('tensor', 'dp')
- out_average_b: bfloat16 [2048, 2048], P('tensor', 'dp')
- gate_up_new: float32 [2, 2048, 6144], P(None, 'dp', 'tensor')
- gate_up_moment: float32 [2, 2048, 6144], P(None, 'dp', 'tensor')
- gate_up_average: float32 [2, 2048, 6144], P(None, 'dp', 'tensor')
- gate_up_average_b: bfloat16 [2, 2048, 6144], P(None, 'dp', 'tensor')
- down_new: float32 [6144, 2048], P('tensor', 'dp')
- down_moment: float32 [6144, 2048], P('tensor', 'dp')
- down_average: float32 [6144, 2048], P('tensor', 'dp')
- down_average_b: bfloat16 [6144, 2048], P('tensor', 'dp')
- gains_new: float32 [4352], replicated
- gains_moment: float32 [4352], replicated
- gains_average: float32 [4352], replicated
- gains_average_b: bfloat16 [4352], replicated
The draws below stay inside these ranges and needn't reach their ends.
Inputs may be any that keep to these rules, and one draw needn't show every extreme that they name: `doc_lengths`: the documents tile the stream of 8192 tokens in order; the longest has exactly 7680 tokens. `valid_mask`: the valid tokens form a prefix of the stream of at least 2048 tokens.
All inputs are finite; a program needn't handle non-finite values.
Results may differ from the reference program's by a relative error of at most 0.04.
Values may be sent and summed in bfloat16 or wider, within the bound.
A program may use at most 256 MiB of HBM per device.

```python
import math
import jax
import jax.numpy as jnp
import numpy as np
from jax import lax

D = 2048
QH = 16
KVH = 8
HD = 128
FF = 6144
DOCS = 8
TOK_DEV = 1024
TOKENS = 8192


def draw_hidden_in(key, part):
    key = jax.random.fold_in(key, 5)
    position = jnp.arange(TOKENS, dtype=jnp.float32) / TOKENS
    rows = (0.5 + 1.5 * position)[:, None]
    values = jnp.clip(jax.random.normal(key, (TOKENS, D), jnp.float32), -6.0, 6.0)
    return (rows * values).astype(jnp.float32)


def draw_valid_mask(key, part):
    key = jax.random.fold_in(key, 7)
    places = jnp.arange(TOKENS, dtype=jnp.int32)
    kept = jax.random.randint(key, (), TOKENS // 4, TOKENS + 1, dtype=jnp.int32)
    return (places < kept).astype(jnp.int32)


def draw_norm_gains(key, part):
    key = jax.random.fold_in(key, 11)
    width = 2 * D + 2 * HD
    stretch = D // HD
    position = jnp.concatenate([jnp.arange(D), jnp.arange(D), jnp.arange(HD) * stretch, jnp.arange(HD) * stretch]).astype(jnp.float32) / D
    rising = 0.6 + 1.2 * position
    factor = jax.random.uniform(key, (width,), jnp.float32, 0.8, 1.2)
    return (rising * factor).astype(jnp.float32)


def level_of(key, extent, pieces, least, high):
    def one(axis_at, shards_of):
        draws = jax.random.uniform(jax.random.fold_in(jax.random.fold_in(key, 6), axis_at), (shards_of,), jnp.float32, least / len(pieces), high / len(pieces))
        return jnp.repeat(jnp.exp(draws), extent[axis_at] // shards_of).reshape((-1,) + (1,) * (len(extent) - axis_at - 1))

    gain = one(*pieces[0])
    for cut in pieces[1:]:
        gain = gain * one(*cut)
    return gain


def split_up(amount, total, bound, lean):
    weights = [(1 << 20) // math.isqrt(standing ** lean) + 1 for standing in range(2, amount + 1)]
    spare, given = total - bound - (amount - 1), [1] * (amount - 1)
    while spare > 0:
        candidates = [i for i in range(amount - 1) if given[i] < bound]
        mass, left = sum([weights[i] for i in candidates]), spare
        for i in candidates:
            more = min(bound - given[i], max(1, left * weights[i] // mass), spare)
            given[i] = given[i] + more
            spare = spare - more
    return np.array([bound] + given)


def uneven(key, number_of, total, bound, lean):
    if number_of == 2:
        one = jax.random.randint(key, (), max(1, total - bound), min(bound, total - 1) + 1)
        return jnp.stack([one, total - one])
    lengths = jnp.asarray(split_up(number_of, total, bound, lean), jnp.int32)
    twos = (number_of - 1) // 2
    source_of, sink = lengths[1:1 + 2 * twos:2], lengths[2:2 + 2 * twos:2]
    slack = jnp.minimum(source_of - 1, bound - sink)
    passed = jax.random.randint(jax.random.fold_in(key, 1), (twos,), 0, 1 << 20) % (slack + 1)
    lengths = lengths.at[1:1 + 2 * twos:2].set(source_of - passed).at[2:2 + 2 * twos:2].set(sink + passed)
    return lengths[jax.random.permutation(jax.random.fold_in(key, 2), number_of)]


def bell_draw(stream_key, dims, scale, bound, split=(), kind=jnp.bfloat16):
    values = scale * jax.random.normal(stream_key, dims, jnp.float32)
    if split:
        values = values * level_of(stream_key, dims, split, -0.22, 0.18)
    return jnp.clip(values, -bound, bound).astype(kind)


def setup_inputs(seed: int = 0) -> dict:
    streams_of = jax.random.split(jax.random.key(seed), 20)
    hidden_in = draw_hidden_in(jax.random.fold_in(streams_of[19], 71), 0)
    cotangent = bell_draw(streams_of[1], (TOKENS, D), 1.0, 6.0, ((0, 8),))
    doc_lengths = uneven(streams_of[2], DOCS, TOKENS, TOKENS - TOK_DEV // 2, 2).astype(jnp.int32)
    valid_mask = draw_valid_mask(jax.random.fold_in(streams_of[19], 71), 0)
    w_qkv = bell_draw(streams_of[4], (D, KVH * 4 * HD), D ** -0.5, 0.125, ((0, 8), (1, 4)), jnp.float32)
    w_out = bell_draw(streams_of[5], (QH * HD, D), 32 ** -0.5, 1.0, ((0, 4), (1, 8)), jnp.float32)
    w_gate_up = bell_draw(streams_of[6], (2, D, FF), D ** -0.5, 0.125, ((1, 8), (2, 4)), jnp.float32)
    w_down = bell_draw(streams_of[7], (FF, D), FF ** -0.5, 0.078125, ((0, 4), (1, 8)), jnp.float32)
    norm_gains = draw_norm_gains(jax.random.fold_in(streams_of[19], 71), 0)
    m_qkv = bell_draw(streams_of[9], (D, KVH * 4 * HD), (0.5 * TOKENS ** 0.5), 256.0, ((0, 8), (1, 4)), jnp.float32)
    m_out = bell_draw(streams_of[10], (QH * HD, D), (0.5 * TOKENS ** 0.5), 256.0, ((0, 4), (1, 8)), jnp.float32)
    m_gate_up = bell_draw(streams_of[11], (2, D, FF), (0.5 * TOKENS ** 0.5), 256.0, ((1, 8), (2, 4)), jnp.float32)
    m_down = bell_draw(streams_of[12], (FF, D), (0.5 * TOKENS ** 0.5), 256.0, ((0, 4), (1, 8)), jnp.float32)
    m_gains = bell_draw(streams_of[13], (2 * D + 2 * HD,), (0.25 * TOKENS ** 0.5), 128.0, (), jnp.float32)
    a_qkv = bell_draw(streams_of[14], (D, KVH * 4 * HD), D ** -0.5, 0.125, ((0, 8), (1, 4)), jnp.float32)
    a_out = bell_draw(streams_of[15], (QH * HD, D), 32 ** -0.5, 1.0, ((0, 4), (1, 8)), jnp.float32)
    a_gate_up = bell_draw(streams_of[16], (2, D, FF), D ** -0.5, 0.125, ((1, 8), (2, 4)), jnp.float32)
    a_down = bell_draw(streams_of[17], (FF, D), FF ** -0.5, 0.078125, ((0, 4), (1, 8)), jnp.float32)
    a_gains = jnp.clip(jax.random.uniform(streams_of[18], (2 * D + 2 * HD,), jnp.float32, 0.3, 2.8), 0.3, 2.8)
    return {"hidden_in": hidden_in, "cotangent": cotangent, "doc_lengths": doc_lengths, "valid_mask": valid_mask, "w_qkv": w_qkv, "w_out": w_out, "w_gate_up": w_gate_up, "w_down": w_down, "norm_gains": norm_gains, "m_qkv": m_qkv, "m_out": m_out, "m_gate_up": m_gate_up, "m_down": m_down, "m_gains": m_gains, "a_qkv": a_qkv, "a_out": a_out, "a_gate_up": a_gate_up, "a_down": a_down, "a_gains": a_gains}


EPSILON = 1e-06
ROPE_BASE = 1000000.0
MOMENTUM = 0.5
EMA_DECAY = 0.5
LR_MATRIX = 0.08
LR_GAIN = 0.5
NEG_FILL = -1e+30
HIGHEST = lax.Precision.HIGHEST

@jax.custom_vjp
def low(v):
    return lax.optimization_barrier(v.astype(jnp.bfloat16)).astype(jnp.float32)

@jax.custom_vjp
def low_back(v):
    return v

def low_keep(v):
    return (low(v), None)

def low_pass(kept, grad):
    return (grad,)

def back_keep(v):
    return (v, None)

def back_low(kept, grad):
    return (low(grad),)
low.defvjp(low_keep, low_pass)
low_back.defvjp(back_keep, back_low)

def rms_scale(values_in):
    return lax.rsqrt(lax.optimization_barrier(jnp.mean(values_in * values_in, axis=-1, keepdims=True)) + EPSILON)

def rotate_half(values_in, cosine, sine):
    half_dim = values_in.shape[-1] // 2
    turned = jnp.concatenate([-values_in[..., half_dim:], values_in[..., :half_dim]], axis=-1)
    return values_in * cosine + turned * sine

def rope_tables(offsets, head_dim):
    half_dim = head_dim // 2
    frequency = 1.0 / ROPE_BASE ** (jnp.arange(half_dim, dtype=jnp.float32) * 2.0 / head_dim)
    angles = offsets.astype(jnp.float32)[:, None] * frequency[None, :]
    cosine = jnp.cos(angles)
    sine = jnp.sin(angles)
    return (jnp.concatenate([cosine, cosine], axis=-1), jnp.concatenate([sine, sine], axis=-1))

def doc_layout(doc_lengths, places):
    ends_at = jnp.cumsum(doc_lengths).astype(jnp.int32)
    starts_at = (ends_at - doc_lengths).astype(jnp.int32)
    doc_ids = lax.optimization_barrier(jnp.sum((places[:, None] >= ends_at[None, :]).astype(jnp.int32), axis=1)).astype(jnp.int32)
    owned = doc_ids[:, None] == jnp.arange(doc_lengths.shape[0], dtype=jnp.int32)[None, :]
    doc_begin = lax.optimization_barrier(jnp.sum(jnp.where(owned, starts_at[None, :], 0), axis=1)).astype(jnp.int32)
    return (doc_ids, doc_begin)

def decoder_layer(hidden_in, w_qkv, w_out, w_gate_up, w_down, norm_gains, cosine, sine, doc_ids, places):
    tokens_all = hidden_in.shape[0]
    gain_attn = norm_gains[:D]
    gain_mlp = norm_gains[D:2 * D]
    gain_query = norm_gains[2 * D:2 * D + HD]
    gain_key = norm_gains[2 * D + HD:]
    normed_one = low(hidden_in * rms_scale(hidden_in) * gain_attn)
    projected = low_back(jnp.dot(normed_one, w_qkv, precision=HIGHEST)).reshape(tokens_all, KVH, 4, HD)
    queries = projected[:, :, :2]
    keys_all = projected[:, :, 2]
    values_all = low(projected[:, :, 3])
    queries = queries * rms_scale(queries) * gain_query
    keys_all = keys_all * rms_scale(keys_all) * gain_key
    queries = low(rotate_half(queries, cosine[:, None, None, :], sine[:, None, None, :]))
    keys_all = low(rotate_half(keys_all, cosine[:, None, :], sine[:, None, :]))
    score_scale = HD ** (-0.5)
    row_block = min(512, tokens_all)

    def attend(begin_row):
        query_rows = lax.dynamic_slice_in_dim(queries, begin_row, row_block, 0)
        doc_rows = lax.dynamic_slice_in_dim(doc_ids, begin_row, row_block, 0)
        place_rows = lax.dynamic_slice_in_dim(places, begin_row, row_block, 0)
        scores = low_back(jnp.einsum('qgjd,kgd->gjqk', query_rows, keys_all, precision=HIGHEST)) * score_scale
        allowed = (doc_rows[:, None] == doc_ids[None, :]) & (place_rows[:, None] >= places[None, :])
        scores = jnp.where(allowed, scores, NEG_FILL)
        row_max = lax.optimization_barrier(jnp.max(scores, axis=-1, keepdims=True))
        row_total = lax.optimization_barrier(jnp.sum(jnp.exp(scores - row_max), axis=-1, keepdims=True))
        weights = low(jnp.exp(scores - (row_max + jnp.log(row_total))))
        return jnp.einsum('gjqk,kgd->qgjd', weights, values_all, precision=HIGHEST)
    begins = (jnp.arange(tokens_all // row_block, dtype=jnp.int32) * row_block).astype(jnp.int32)
    attended = lax.map(jax.checkpoint(attend), begins)
    mixed = attended.reshape(tokens_all, QH * HD)
    mixed = low(low_back(mixed))
    attn = low_back(jnp.dot(mixed, w_out, precision=HIGHEST))
    resid_one = hidden_in + attn
    normed_two = low(resid_one * rms_scale(resid_one) * gain_mlp)
    gate = low_back(jnp.dot(normed_two, w_gate_up[0], precision=HIGHEST))
    up_proj = low_back(jnp.dot(normed_two, w_gate_up[1], precision=HIGHEST))
    hidden_mid = low(jax.nn.silu(gate) * up_proj)
    mlp = low_back(jnp.dot(hidden_mid, w_down, precision=HIGHEST))
    return (resid_one + mlp, attn, mlp)

def nesterov(weight, moment, average, gradient, rate):
    new_moment = MOMENTUM * moment + gradient
    new_weight = weight - rate * (gradient + MOMENTUM * new_moment)
    new_average = EMA_DECAY * average + (1.0 - EMA_DECAY) * new_weight
    return (new_weight, new_moment, new_average, new_average.astype(jnp.bfloat16))

def reference(hidden_in, cotangent, doc_lengths, valid_mask, w_qkv, w_out, w_gate_up, w_down, norm_gains, m_qkv, m_out, m_gate_up, m_down, m_gains, a_qkv, a_out, a_gate_up, a_down, a_gains):
    places = jnp.arange(TOKENS, dtype=jnp.int32)
    doc_ids, doc_begin = doc_layout(doc_lengths, places)
    cosine, sine = rope_tables(places - doc_begin, HD)

    def forward(hidden, qkv_w, out_w, gate_up_w, down_w, gains_w):
        return decoder_layer(hidden, qkv_w, out_w, gate_up_w, down_w, gains_w, cosine, sine, doc_ids, places)
    outputs, pullback = jax.vjp(forward, hidden_in, w_qkv, w_out, w_gate_up, w_down, norm_gains)
    mixed_out, attn_out, mlp_out = outputs
    grads = pullback((cotangent.astype(jnp.float32), jnp.zeros_like(attn_out), jnp.zeros_like(mlp_out)))
    grad_input, grad_qkv, grad_out, grad_gate_up, grad_down, grad_gains = grads
    mask_rows = valid_mask.astype(jnp.float32)[:, None]
    counted = jnp.sum(valid_mask.astype(jnp.float32))
    branch_rms = jnp.stack([jnp.sqrt(jnp.sum(mask_rows * branch * branch) / (counted * D)) for branch in (hidden_in, attn_out, mlp_out)])
    rate_matrix = LR_MATRIX / math.sqrt(TOKENS)
    rate_gain = LR_GAIN / math.sqrt(TOKENS)
    qkv_new, qkv_moment, qkv_average, qkv_average_b = nesterov(w_qkv, m_qkv, a_qkv, grad_qkv, rate_matrix)
    out_new, out_moment, out_average, out_average_b = nesterov(w_out, m_out, a_out, grad_out, rate_matrix)
    gate_up_new, gate_up_moment, gate_up_average, gate_up_average_b = nesterov(w_gate_up, m_gate_up, a_gate_up, grad_gate_up, rate_matrix)
    down_new, down_moment, down_average, down_average_b = nesterov(w_down, m_down, a_down, grad_down, rate_matrix)
    gains_new, gains_moment, gains_average, gains_average_b = nesterov(norm_gains, m_gains, a_gains, grad_gains, rate_gain)
    return (mixed_out, grad_input, branch_rms, qkv_new, qkv_moment, qkv_average, qkv_average_b, out_new, out_moment, out_average, out_average_b, gate_up_new, gate_up_moment, gate_up_average, gate_up_average_b, down_new, down_moment, down_average, down_average_b, gains_new, gains_moment, gains_average, gains_average_b)
```

```python
import functools, math
import jax, jax.numpy as jnp
from jax import lax
from jax.experimental import pallas as pl
from jax.experimental.pallas import tpu as pltpu
NT = (((1,), (1,)), ((), ()))
NN = (((1,), (0,)), ((), ()))
TN = (((0,), (0,)), ((), ()))
NEG_FILL = -1e30
LOG2E = math.log2(math.e)
MIB = 1024 * 1024

def matmul(a, b, dims):
    return lax.dot_general(a, b, dims, preferred_element_type=jnp.float32)

def row_of(column):
    return jnp.transpose(jnp.broadcast_to(column, (column.shape[0], 128)))[:1]

def attend_kernel(head_dim, key_rows, bound_ref, query_ref, begin_ref, kv_ref, out_ref, total_ref, q_two, accum):
    rows = query_ref.shape[0]
    block = pl.program_id(0)
    first = bound_ref[0, block]
    begin_first = bound_ref[1, block]
    begin_last = bound_ref[2, block]
    scale = LOG2E * head_dim**-0.5
    q_two[:rows] = query_ref[:, :head_dim]
    q_two[rows:] = query_ref[:, head_dim:]
    places = first + lax.broadcasted_iota(jnp.int32, (1, rows), 1)
    places = jnp.concatenate([places, places], axis=1)
    begins = jnp.concatenate([begin_ref[0], begin_ref[0]], axis=1)

    def step(masked, index, carry):
        top, total = carry
        key_begin = pl.multiple_of(index * key_rows, key_rows)
        keys = kv_ref[pl.ds(key_begin, key_rows), :head_dim]
        values = kv_ref[pl.ds(key_begin, key_rows), head_dim:]
        raw = matmul(keys, q_two[...], NT) * scale
        if masked:
            key_places = key_begin + lax.broadcasted_iota(jnp.int32, (key_rows, 1), 0)
            allowed = (key_places >= begins) & (key_places <= places)
            raw = jnp.where(allowed, raw, NEG_FILL)
        new_top = jnp.maximum(top, jnp.max(raw, axis=0, keepdims=True))
        probs = jnp.exp2(raw - new_top)
        fade = jnp.exp2(top - new_top)
        total = total * fade + jnp.sum(probs, axis=0, keepdims=True)
        accum[...] = accum[...] * fade + matmul(values, probs.astype(jnp.bfloat16), TN)
        return (new_top, total)

    def either(index, carry):
        key_begin = index * key_rows
        plain = (key_begin >= begin_last) & (key_begin + key_rows - 1 <= first)
        return lax.cond(
            plain, functools.partial(step, False, index), functools.partial(step, True, index), carry
        )

    accum[...] = jnp.zeros_like(accum)
    start = (
        jnp.full((1, 2 * rows), NEG_FILL, jnp.float32),
        jnp.zeros((1, 2 * rows), jnp.float32),
    )
    low = begin_first // key_rows
    high = (first + rows - 1) // key_rows + 1
    top, total = lax.fori_loop(low, high, either, start)
    out = jnp.transpose(accum[...] / total)
    out_ref[:, :head_dim] = out[:rows].astype(out_ref.dtype)
    out_ref[:, head_dim:] = out[rows:].astype(out_ref.dtype)
    total_ref[0] = top + jnp.log2(total)

def attend(bounds, queries, begins, kv_all, head_dim, query_rows, key_rows):
    rows = queries.shape[0]
    blocks = rows // query_rows
    return pl.pallas_call(
        functools.partial(attend_kernel, head_dim, key_rows),
        out_shape=(jax.ShapeDtypeStruct(queries.shape, jnp.bfloat16), jax.ShapeDtypeStruct((blocks, 1, 2 * query_rows), jnp.float32)),
        grid_spec=pltpu.PrefetchScalarGridSpec(
            num_scalar_prefetch=1,
            grid=(blocks,),
            in_specs=[
                pl.BlockSpec((query_rows, 2 * head_dim), lambda i, *_: (i, 0)),
                pl.BlockSpec((1, 1, query_rows), lambda i, *_: (i, 0, 0)),
                pl.BlockSpec(kv_all.shape, lambda i, *_: (0, 0)),
            ],
            out_specs=[
                pl.BlockSpec((query_rows, 2 * head_dim), lambda i, *_: (i, 0)),
                pl.BlockSpec((1, 1, 2 * query_rows), lambda i, *_: (i, 0, 0)),
            ],
            scratch_shapes=[pltpu.VMEM((2 * query_rows, head_dim), jnp.bfloat16), pltpu.VMEM((head_dim, 2 * query_rows), jnp.float32)],
        ),
        compiler_params=pltpu.CompilerParams(vmem_limit_bytes=48 * MIB),
    )(bounds, queries, begins, kv_all)

def attend_back_kernel(head_dim, key_rows, bound_ref, query_ref, grad_ref, out_ref, total_ref, begin_ref, kv_ref, grad_q_ref, grad_kv_ref, q_two, g_two, dq_two, kv_sum):
    rows = query_ref.shape[0]
    block = pl.program_id(0)
    first = bound_ref[0, block]
    begin_first = bound_ref[1, block]
    begin_last = bound_ref[2, block]
    unit = head_dim**-0.5
    scale = LOG2E * unit

    @pl.when(block == 0)
    def _():
        kv_sum[...] = jnp.zeros_like(kv_sum)

    for half in range(2):
        part = slice(half * rows, (half + 1) * rows)
        cols = slice(half * head_dim, (half + 1) * head_dim)
        q_two[part] = query_ref[:, cols]
        g_two[part] = grad_ref[:, cols]
    dq_two[...] = jnp.zeros_like(dq_two)
    product = grad_ref[...].astype(jnp.float32) * out_ref[...].astype(jnp.float32)
    delta = jnp.concatenate(
        [
            row_of(jnp.sum(product[:, :head_dim], axis=1, keepdims=True)),
            row_of(jnp.sum(product[:, head_dim:], axis=1, keepdims=True)),
        ],
        axis=1,
    )
    totals = total_ref[0]
    places = first + lax.broadcasted_iota(jnp.int32, (1, rows), 1)
    places = jnp.concatenate([places, places], axis=1)
    begins = jnp.concatenate([begin_ref[0], begin_ref[0]], axis=1)

    def step(masked, index):
        key_begin = pl.multiple_of(index * key_rows, key_rows)
        place = pl.ds(key_begin, key_rows)
        keys = kv_ref[place, :head_dim]
        values = kv_ref[place, head_dim:]
        raw = matmul(keys, q_two[...], NT)
        probs = jnp.exp2(raw * scale - totals)
        if masked:
            key_places = key_begin + lax.broadcasted_iota(jnp.int32, (key_rows, 1), 0)
            allowed = (key_places >= begins) & (key_places <= places)
            probs = jnp.where(allowed, probs, 0.0)
        kv_sum[place, head_dim:] += matmul(probs.astype(jnp.bfloat16), g_two[...], NN)
        grad_probs = matmul(values, g_two[...], NT)
        grad_scores = (probs * ((grad_probs - delta) * unit)).astype(jnp.bfloat16)
        kv_sum[place, :head_dim] += matmul(grad_scores, q_two[...], NN)
        dq_two[...] += matmul(grad_scores, keys, TN)

    def either(index, carry):
        key_begin = index * key_rows
        plain = (key_begin >= begin_last) & (key_begin + key_rows - 1 <= first)

        @pl.when(plain)
        def _():
            step(False, index)

        @pl.when(jnp.logical_not(plain))
        def _():
            step(True, index)

        return carry

    low = begin_first // key_rows
    high = (first + rows - 1) // key_rows + 1
    lax.fori_loop(low, high, either, 0)
    grad_q_ref[:, :head_dim] = dq_two[:rows].astype(grad_q_ref.dtype)
    grad_q_ref[:, head_dim:] = dq_two[rows:].astype(grad_q_ref.dtype)

    @pl.when(block == pl.num_programs(0) - 1)
    def _():
        grad_kv_ref[...] = kv_sum[...].astype(grad_kv_ref.dtype)

def attend_back(bounds, queries, grads, outs, totals, begin_rows, kv_all, head_dim, query_rows, key_rows):
    rows = queries.shape[0]
    blocks = rows // query_rows
    wide = pl.BlockSpec((query_rows, 2 * head_dim), lambda i, *_: (i, 0))
    whole = pl.BlockSpec(kv_all.shape, lambda i, *_: (0, 0))
    return pl.pallas_call(
        functools.partial(attend_back_kernel, head_dim, key_rows),
        out_shape=(jax.ShapeDtypeStruct(queries.shape, jnp.float32), jax.ShapeDtypeStruct(kv_all.shape, jnp.bfloat16)),
        grid_spec=pltpu.PrefetchScalarGridSpec(
            num_scalar_prefetch=1,
            grid=(blocks,),
            in_specs=[wide, wide, wide,
                pl.BlockSpec((1, 1, 2 * query_rows), lambda i, *_: (i, 0, 0)),
                pl.BlockSpec((1, 1, query_rows), lambda i, *_: (i, 0, 0)),
                whole],
            out_specs=[wide, whole],
            scratch_shapes=[pltpu.VMEM((2 * query_rows, head_dim), jnp.bfloat16)] * 2
            + [pltpu.VMEM((2 * query_rows, head_dim), jnp.float32), pltpu.VMEM(kv_all.shape, jnp.float32)],
        ),
        compiler_params=pltpu.CompilerParams(vmem_limit_bytes=56 * MIB),
    )(bounds, queries, grads, outs, totals, begin_rows, kv_all)


from jax.sharding import PartitionSpec as P

EPSILON = 1e-06
ROPE_BASE = 1000000.0
MOMENTUM = 0.5
EMA_DECAY = 0.5
LR_MATRIX = 0.08
LR_GAIN = 0.5
FF_BLOCK = 256
CHUNKS = 3


def mlp_kernel(normed_ref, cot_ref, normed_t_ref, cot_t_ref, weight_ref, hidden_ref, gate_grad_ref, up_grad_ref, weight_grad_ref):
    ways, _, shard, width = weight_ref.shape
    rows = normed_ref.shape[0]
    depth = ways * shard
    row_tile = min(512, rows)

    @pl.loop(0, rows // row_tile)
    def _(tile):
        place = pl.ds(pl.multiple_of(tile * row_tile, row_tile), row_tile)
        x = normed_ref[place, :]
        gate = matmul(x, weight_ref[:, 0].reshape(depth, width), NN)
        up = matmul(x, weight_ref[:, 1].reshape(depth, width), NN)
        grad_hidden = matmul(cot_ref[place, :], weight_ref[:, 2].reshape(depth, width), NN)
        sigmoid = 1.0 / (1.0 + jnp.exp(-gate))
        silu = gate * sigmoid
        hidden_ref[place, :] = (silu * up).astype(hidden_ref.dtype)
        gate_grad_ref[place, :] = (
            grad_hidden * up * (sigmoid * (1.0 + gate * (1.0 - sigmoid)))
        ).astype(gate_grad_ref.dtype)
        up_grad_ref[place, :] = (grad_hidden * silu).astype(up_grad_ref.dtype)

    @pl.loop(0, ways)
    def _(way):
        place = pl.ds(pl.multiple_of(way * shard, shard), shard)
        left = normed_t_ref[place, :]
        weight_grad_ref[way, 0] = matmul(left, gate_grad_ref[...], NN).astype(weight_grad_ref.dtype)
        weight_grad_ref[way, 1] = matmul(left, up_grad_ref[...], NN).astype(weight_grad_ref.dtype)
        weight_grad_ref[way, 2] = matmul(cot_t_ref[place, :], hidden_ref[...], NN).astype(weight_grad_ref.dtype)


def mlp_chunk(normed, cotangent, normed_t, cotangent_t, weights):
    ways, kinds, shard, width = weights.shape
    rows, depth = normed.shape
    block = min(FF_BLOCK, width)

    def held(array):
        return pl.BlockSpec(array.shape, lambda i: (0, 0), pipeline_mode=pl.Buffered(1))

    weight_spec = pl.BlockSpec((ways, kinds, shard, block), lambda i: (0, 0, 0, i))
    row_spec = pl.BlockSpec((rows, block), lambda i: (0, i))
    row_shape = jax.ShapeDtypeStruct((rows, width), jnp.bfloat16)
    return pl.pallas_call(
        mlp_kernel,
        grid=(width // block,),
        in_specs=[held(normed), held(cotangent), held(normed_t), held(cotangent_t), weight_spec],
        out_specs=[row_spec, row_spec, row_spec, weight_spec],
        out_shape=(row_shape, row_shape, row_shape, jax.ShapeDtypeStruct(weights.shape, jnp.bfloat16)),
        compiler_params=pltpu.CompilerParams(vmem_limit_bytes=56 * MIB),
        cost_estimate=pl.CostEstimate(flops=12 * rows * depth * width, bytes_accessed=12 * depth * width, transcendentals=rows * width),
    )(normed, cotangent, normed_t, cotangent_t, weights)


def back_product_kernel(kinds, *refs):
    out_ref = refs[-1]
    total = None
    chunks = (len(refs) - 1) // (kinds + 1)
    for chunk in range(chunks):
        weight_ref = refs[chunk * (kinds + 1) + kinds]
        for kind in range(kinds):
            part = matmul(refs[chunk * (kinds + 1) + kind][...], weight_ref[0, kind], NT)
            total = part if total is None else total + part
    out_ref[...] = total.astype(out_ref.dtype)


def back_product(groups_of, weights, kind_begin):
    kinds = len(groups_of[0])
    ways, _, shard, width = weights[0].shape
    rows = groups_of[0][0].shape[0]
    args, specs = [], []
    for lefts, weight in zip(groups_of, weights):
        for left in lefts:
            args.append(left)
            specs.append(pl.BlockSpec(left.shape, lambda i: (0, 0), pipeline_mode=pl.Buffered(1)))
        args.append(weight)
        specs.append(pl.BlockSpec((1, kinds, shard, width), lambda i: (i, kind_begin // kinds, 0, 0)))
    return pl.pallas_call(
        functools.partial(back_product_kernel, kinds),
        grid=(ways,),
        in_specs=specs,
        out_specs=pl.BlockSpec((rows, shard), lambda i: (0, i)),
        out_shape=jax.ShapeDtypeStruct((rows, ways * shard), jnp.bfloat16),
        compiler_params=pltpu.CompilerParams(vmem_limit_bytes=56 * MIB),
        cost_estimate=pl.CostEstimate(flops=2 * len(weights) * kinds * rows * width * ways * shard, bytes_accessed=2 * len(weights) * kinds * width * ways * shard, transcendentals=0),
    )(*args)


def rms_scale(values_in):
    return lax.rsqrt(jnp.mean(values_in * values_in, axis=-1, keepdims=True) + EPSILON)


def rotate_half(values_in, cosine, sine):
    half_dim = values_in.shape[-1] // 2
    turned = jnp.concatenate([-values_in[..., half_dim:], values_in[..., :half_dim]], axis=-1)
    return values_in * cosine + turned * sine


def rotate_back(grads, cosine, sine):
    half_dim = grads.shape[-1] // 2
    scaled = grads * sine
    turned = jnp.concatenate([scaled[..., half_dim:], -scaled[..., :half_dim]], axis=-1)
    return grads * cosine + turned


def norm_back(grads, normal, scale_rows, gain):
    grad_hat = grads * gain
    return scale_rows * (grad_hat - normal * jnp.mean(grad_hat * normal, axis=-1, keepdims=True))


def rope_tables(offsets, head_dim):
    half_dim = head_dim // 2
    frequency = 1.0 / ROPE_BASE ** (jnp.arange(half_dim, dtype=jnp.float32) * 2.0 / head_dim)
    angles = offsets.astype(jnp.float32)[:, None] * frequency[None, :]
    cosine = jnp.cos(angles)
    sine = jnp.sin(angles)
    return (jnp.concatenate([cosine, cosine], axis=-1), jnp.concatenate([sine, sine], axis=-1))


def nesterov(weight, moment, average, gradient, rate):
    new_moment = MOMENTUM * moment + gradient
    new_weight = weight - rate * (gradient + MOMENTUM * new_moment)
    new_average = EMA_DECAY * average + (1.0 - EMA_DECAY) * new_weight
    return (new_weight, new_moment, new_average, new_average.astype(jnp.bfloat16))


def dot(a, b, dims):
    return lax.dot_general(a, b, dims, preferred_element_type=jnp.float32)


def after(value, *others):
    return lax.optimization_barrier((value, *others))[0]


def local(
    hidden_in,
    cotangent,
    doc_lengths,
    valid_mask,
    w_qkv,
    w_out,
    w_gate_up,
    w_down,
    norm_gains,
    m_qkv,
    m_out,
    m_gate_up,
    m_down,
    m_gains,
    a_qkv,
    a_out,
    a_gate_up,
    a_down,
    a_gains,
):
    row_count, model_dim = hidden_in.shape
    head_dim = (norm_gains.shape[0] - 2 * model_dim) // 2
    data_ways = lax.axis_size("dp")
    tensor_ways = lax.axis_size("tensor")
    tensor_at = lax.axis_index("tensor")
    tokens_all = row_count * data_ways
    width_cols = model_dim // tensor_ways
    col_begin = tensor_at * width_cols
    groups = w_qkv.shape[1] // (4 * head_dim)
    ff_local = w_down.shape[0]
    ff_chunk = ff_local // CHUNKS
    bf16 = jnp.bfloat16
    f32 = jnp.float32

    def columns_of(values_in):
        return lax.dynamic_slice_in_dim(values_in, col_begin, width_cols, values_in.ndim - 1)

    qkv_full = lax.all_gather(w_qkv.astype(bf16), "dp", axis=0, tiled=True)
    out_shard_t = after(w_out.astype(bf16).T, qkv_full)
    out_full_t = lax.all_gather(out_shard_t, "dp", axis=0, tiled=True)

    ends_at = jnp.cumsum(doc_lengths)
    starts_at = ends_at - doc_lengths
    place_begin = lax.axis_index("dp") * row_count
    places = place_begin + jnp.arange(row_count, dtype=jnp.int32)
    doc_ids = jnp.sum((places[:, None] >= ends_at[None, :]).astype(jnp.int32), axis=1)
    owned = doc_ids[:, None] == jnp.arange(doc_lengths.shape[0], dtype=jnp.int32)[None, :]
    doc_begin = jnp.sum(jnp.where(owned, starts_at[None, :], 0), axis=1)
    cosine, sine = rope_tables(places - doc_begin, head_dim)
    query_rows = min(512, row_count)
    blocks = row_count // query_rows
    bounds = jnp.stack(
        [
            place_begin + jnp.arange(blocks, dtype=jnp.int32) * query_rows,
            doc_begin[::query_rows],
            doc_begin[query_rows - 1 :: query_rows],
        ]
    ).astype(jnp.int32)
    begin_rows = doc_begin.astype(jnp.int32).reshape(blocks, 1, query_rows)

    gain_attn = norm_gains[:model_dim]
    gain_mlp = norm_gains[model_dim : 2 * model_dim]
    gain_query = norm_gains[2 * model_dim : 2 * model_dim + head_dim]
    gain_key = norm_gains[2 * model_dim + head_dim :]
    scale_one = rms_scale(hidden_in)
    normal_one = hidden_in * scale_one
    normed_one_b = (normal_one * gain_attn).astype(bf16)
    projected = dot(normed_one_b, qkv_full, NN)

    raw_queries, raw_keys, queries, kv_every = [], [], [], []
    for group in range(groups):
        base = group * 4 * head_dim
        query_raw = projected[:, base : base + 2 * head_dim].reshape(row_count, 2, head_dim)
        key_raw = projected[:, base + 2 * head_dim : base + 3 * head_dim]
        value = projected[:, base + 3 * head_dim : base + 4 * head_dim]
        query = rotate_half(
            query_raw * rms_scale(query_raw) * gain_query, cosine[:, None], sine[:, None]
        )
        key = rotate_half(key_raw * rms_scale(key_raw) * gain_key, cosine, sine)
        raw_queries.append(query_raw)
        raw_keys.append(key_raw)
        queries.append(query.reshape(row_count, 2 * head_dim).astype(bf16))
        kv_local = jnp.concatenate([key, value], axis=1).astype(bf16)
        kv_every.append(lax.all_gather(kv_local, "dp", axis=0, tiled=True))

    down_t = w_down.T
    chunk_weights = []
    previous = kv_every[-1]
    for chunk in range(CHUNKS):
        units = slice(chunk * ff_chunk, (chunk + 1) * ff_chunk)
        shard = jnp.stack(
            [w_gate_up[0, :, units], w_gate_up[1, :, units], down_t[:, units]]
        ).astype(bf16)
        previous = lax.all_gather(after(shard, previous), "dp", axis=0)
        chunk_weights.append(previous)

    mixed, totals = [], []
    for group in range(groups):
        mixed_rows, total_rows = attend(
            bounds, queries[group], begin_rows, kv_every[group], head_dim, query_rows, min(1024, tokens_all)
        )
        mixed.append(mixed_rows)
        totals.append(total_rows)
    mixed_b = jnp.concatenate(mixed, axis=1)
    attn_part = dot(mixed_b, out_full_t, NT).astype(bf16)
    attn = lax.psum(attn_part, "tensor").astype(f32)
    resid_one = hidden_in + attn
    scale_two = rms_scale(resid_one)
    normal_two = resid_one * scale_two
    normed_two_b = (normal_two * gain_mlp).astype(bf16)

    normed_two_t = normed_two_b.T
    cotangent_t = cotangent.T
    weight_grads, hiddens, back_pairs = [], [], []
    for chunk in range(CHUNKS):
        hidden_b, gate_grad, up_grad, weight_grad = mlp_chunk(
            normed_two_b, cotangent, normed_two_t, cotangent_t, chunk_weights[chunk]
        )
        hiddens.append((hidden_b,))
        back_pairs.append((gate_grad, up_grad))
        weight_grads.append(lax.psum_scatter(weight_grad, "dp", scatter_dimension=0))

    part_two = back_product(back_pairs, chunk_weights, 0)
    grad_normed_two = lax.psum(part_two, "tensor").astype(f32)
    mlp_part = back_product(hiddens, chunk_weights, 2)
    mlp_cols = lax.psum_scatter(mlp_part, "tensor", scatter_dimension=1, tiled=True).astype(f32)
    gain_mlp_part = jnp.sum(columns_of(grad_normed_two * normal_two), axis=0)
    grad_resid = cotangent.astype(f32) + norm_back(grad_normed_two, normal_two, scale_two, gain_mlp)
    grad_attn_b = grad_resid.astype(bf16)
    grad_mixed_b = dot(grad_attn_b, out_full_t, NN).astype(bf16)

    grad_queries, kv_grads = [], []
    for group in range(groups):
        cols = slice(group * 2 * head_dim, (group + 1) * 2 * head_dim)
        grad_query, kv_grad = attend_back(
            bounds,
            queries[group],
            grad_mixed_b[:, cols],
            mixed[group],
            totals[group],
            begin_rows,
            kv_every[group],
            head_dim,
            query_rows,
            min(512, tokens_all),
        )
        grad_queries.append(grad_query)
        kv_grads.append(lax.psum_scatter(kv_grad, "dp", scatter_dimension=0, tiled=True).astype(f32))
    grad_out_t = dot(grad_attn_b, mixed_b, TN).astype(bf16)
    out_shard = lax.psum_scatter(grad_out_t, "dp", scatter_dimension=0, tiled=True).astype(f32).T

    grad_parts = []
    gain_query_part = jnp.zeros((head_dim,), f32)
    gain_key_part = jnp.zeros((head_dim,), f32)
    for group in range(groups):
        query_raw = raw_queries[group]
        key_raw = raw_keys[group]
        query_scale = rms_scale(query_raw)
        query_normal = query_raw * query_scale
        key_scale = rms_scale(key_raw)
        key_normal = key_raw * key_scale
        grad_query_norm = rotate_back(
            grad_queries[group].reshape(row_count, 2, head_dim), cosine[:, None], sine[:, None]
        )
        gain_query_part += jnp.sum(grad_query_norm * query_normal, axis=(0, 1))
        grad_query_raw = norm_back(grad_query_norm, query_normal, query_scale, gain_query)
        grad_key_norm = rotate_back(kv_grads[group][:, :head_dim], cosine, sine)
        gain_key_part += jnp.sum(grad_key_norm * key_normal, axis=0)
        grad_key_raw = norm_back(grad_key_norm, key_normal, key_scale, gain_key)
        grad_parts += [
            grad_query_raw.reshape(row_count, 2 * head_dim),
            grad_key_raw,
            kv_grads[group][:, head_dim:],
        ]
    grad_projected_b = jnp.concatenate([part.astype(bf16) for part in grad_parts], axis=1)
    grad_qkv = dot(normed_one_b, grad_projected_b, TN).astype(bf16)
    qkv_shard = lax.psum_scatter(grad_qkv, "dp", scatter_dimension=0, tiled=True).astype(f32)
    part_one = dot(grad_projected_b, qkv_full, NT)
    grad_one_cols = lax.psum_scatter(
        part_one.astype(bf16), "tensor", scatter_dimension=1, tiled=True
    ).astype(f32)
    row_dots = lax.psum(
        jnp.sum(part_one * (normal_one * gain_attn), axis=1, keepdims=True), "tensor"
    )
    gain_attn_part = jnp.sum(part_one * normal_one, axis=0)

    grad_cols = columns_of(grad_resid) + scale_one * (
        grad_one_cols * columns_of(gain_attn)
        - columns_of(normal_one) * (row_dots / model_dim)
    )
    attn_cols = columns_of(attn)
    mixed_cols = columns_of(resid_one) + mlp_cols
    mask_rows = valid_mask.astype(f32)[:, None]

    def column_squares(columns):
        return jnp.sum(mask_rows * columns * columns)

    count_part = jnp.where(tensor_at == 0, jnp.sum(valid_mask.astype(f32)), 0.0)
    stats_part = jnp.stack(
        [
            column_squares(columns_of(hidden_in)),
            column_squares(attn_cols),
            column_squares(mlp_cols),
            count_part,
        ]
    )
    gain_mlp_wide = lax.dynamic_update_slice_in_dim(
        jnp.zeros((model_dim,), f32), gain_mlp_part, col_begin, 0
    )
    gains_part = jnp.concatenate(
        [gain_attn_part, gain_mlp_wide, gain_query_part, gain_key_part, stats_part]
    )
    gains_sum = lax.psum(gains_part, ("dp", "tensor"))
    grad_gains = gains_sum[: norm_gains.shape[0]]
    stats_sum = gains_sum[norm_gains.shape[0] :]
    branch_rms = jnp.sqrt(stats_sum[:3] / (stats_sum[3] * model_dim))

    rate_matrix = LR_MATRIX / math.sqrt(tokens_all)
    rate_gain = LR_GAIN / math.sqrt(tokens_all)
    gate_up_shard = jnp.concatenate([grad[:2] for grad in weight_grads], axis=2).astype(f32)
    down_shard = jnp.concatenate([grad[2] for grad in weight_grads], axis=1).astype(f32).T
    return (
        mixed_cols,
        grad_cols,
        branch_rms,
        *nesterov(w_qkv, m_qkv, a_qkv, qkv_shard, rate_matrix),
        *nesterov(w_out, m_out, a_out, out_shard, rate_matrix),
        *nesterov(w_gate_up, m_gate_up, a_gate_up, gate_up_shard, rate_matrix),
        *nesterov(w_down, m_down, a_down, down_shard, rate_matrix),
        *nesterov(norm_gains, m_gains, a_gains, grad_gains, rate_gain),
    )


def solution(mesh):
    rows = P("dp", None)
    spread = P("dp", "tensor")
    turned = P("tensor", "dp")
    stacked = P(None, "dp", "tensor")
    matrices = (spread, turned, stacked, turned, P())
    in_specs = (rows, rows, P(), P("dp"), *matrices, *matrices, *matrices)
    out_specs = (spread, spread, P(), *(spec for spec in matrices for _ in range(4)))
    return jax.shard_map(local, mesh=mesh, in_specs=in_specs, out_specs=out_specs, check_vma=False)
```

```python
import functools, math
import jax, jax.numpy as jnp
from jax import lax
from jax.experimental import pallas as pl
from jax.experimental.pallas import tpu as pltpu
NT = (((1,), (1,)), ((), ()))
NN = (((1,), (0,)), ((), ()))
TN = (((0,), (0,)), ((), ()))
NEG_FILL = -1e30
LOG2E = math.log2(math.e)
MIB = 1024 * 1024

def matmul(a, b, dims):
    return lax.dot_general(a, b, dims, preferred_element_type=jnp.float32)

def row_of(column):
    return jnp.transpose(jnp.broadcast_to(column, (column.shape[0], 128)))[:1]

def attend_kernel(head_dim, key_rows, bound_ref, query_ref, begin_ref, kv_ref, out_ref, total_ref, q_two, accum):
    rows = query_ref.shape[0]
    block = pl.program_id(0)
    first = bound_ref[0, block]
    begin_first = bound_ref[1, block]
    begin_last = bound_ref[2, block]
    scale = LOG2E * head_dim**-0.5
    q_two[:rows] = query_ref[:, :head_dim]
    q_two[rows:] = query_ref[:, head_dim:]
    places = first + lax.broadcasted_iota(jnp.int32, (1, rows), 1)
    places = jnp.concatenate([places, places], axis=1)
    begins = jnp.concatenate([begin_ref[0], begin_ref[0]], axis=1)

    def step(masked, index, carry):
        top, total = carry
        key_begin = pl.multiple_of(index * key_rows, key_rows)
        keys = kv_ref[pl.ds(key_begin, key_rows), :head_dim]
        values = kv_ref[pl.ds(key_begin, key_rows), head_dim:]
        raw = matmul(keys, q_two[...], NT) * scale
        if masked:
            key_places = key_begin + lax.broadcasted_iota(jnp.int32, (key_rows, 1), 0)
            allowed = (key_places >= begins) & (key_places <= places)
            raw = jnp.where(allowed, raw, NEG_FILL)
        new_top = jnp.maximum(top, jnp.max(raw, axis=0, keepdims=True))
        probs = jnp.exp2(raw - new_top)
        fade = jnp.exp2(top - new_top)
        total = total * fade + jnp.sum(probs, axis=0, keepdims=True)
        accum[...] = accum[...] * fade + matmul(values, probs.astype(jnp.bfloat16), TN)
        return (new_top, total)

    def either(index, carry):
        key_begin = index * key_rows
        plain = (key_begin >= begin_last) & (key_begin + key_rows - 1 <= first)
        return lax.cond(
            plain, functools.partial(step, False, index), functools.partial(step, True, index), carry
        )

    accum[...] = jnp.zeros_like(accum)
    start = (
        jnp.full((1, 2 * rows), NEG_FILL, jnp.float32),
        jnp.zeros((1, 2 * rows), jnp.float32),
    )
    low = begin_first // key_rows
    high = (first + rows - 1) // key_rows + 1
    top, total = lax.fori_loop(low, high, either, start)
    out = jnp.transpose(accum[...] / total)
    out_ref[:, :head_dim] = out[:rows].astype(out_ref.dtype)
    out_ref[:, head_dim:] = out[rows:].astype(out_ref.dtype)
    total_ref[0] = top + jnp.log2(total)

def attend(bounds, queries, begins, kv_all, head_dim, query_rows, key_rows):
    rows = queries.shape[0]
    blocks = rows // query_rows
    return pl.pallas_call(
        functools.partial(attend_kernel, head_dim, key_rows),
        out_shape=(jax.ShapeDtypeStruct(queries.shape, jnp.bfloat16), jax.ShapeDtypeStruct((blocks, 1, 2 * query_rows), jnp.float32)),
        grid_spec=pltpu.PrefetchScalarGridSpec(
            num_scalar_prefetch=1,
            grid=(blocks,),
            in_specs=[
                pl.BlockSpec((query_rows, 2 * head_dim), lambda i, *_: (i, 0)),
                pl.BlockSpec((1, 1, query_rows), lambda i, *_: (i, 0, 0)),
                pl.BlockSpec(kv_all.shape, lambda i, *_: (0, 0)),
            ],
            out_specs=[
                pl.BlockSpec((query_rows, 2 * head_dim), lambda i, *_: (i, 0)),
                pl.BlockSpec((1, 1, 2 * query_rows), lambda i, *_: (i, 0, 0)),
            ],
            scratch_shapes=[pltpu.VMEM((2 * query_rows, head_dim), jnp.bfloat16), pltpu.VMEM((head_dim, 2 * query_rows), jnp.float32)],
        ),
        compiler_params=pltpu.CompilerParams(vmem_limit_bytes=48 * MIB),
        cost_estimate=pl.CostEstimate(flops=8 * rows * kv_all.shape[0] * head_dim, bytes_accessed=2 * kv_all.size, transcendentals=2 * rows * kv_all.shape[0]),
    )(bounds, queries, begins, kv_all)

def attend_back_kernel(head_dim, key_rows, bound_ref, query_ref, grad_ref, out_ref, total_ref, begin_ref, kv_ref, grad_q_ref, grad_kv_ref, q_two, g_two, dq_two, kv_sum):
    rows = query_ref.shape[0]
    block = pl.program_id(0)
    first = bound_ref[0, block]
    begin_first = bound_ref[1, block]
    begin_last = bound_ref[2, block]
    unit = head_dim**-0.5
    scale = LOG2E * unit

    @pl.when(block == 0)
    def _():
        kv_sum[...] = jnp.zeros_like(kv_sum)

    for half in range(2):
        part = slice(half * rows, (half + 1) * rows)
        cols = slice(half * head_dim, (half + 1) * head_dim)
        q_two[part] = query_ref[:, cols]
        g_two[part] = grad_ref[:, cols]
    dq_two[...] = jnp.zeros_like(dq_two)
    product = grad_ref[...].astype(jnp.float32) * out_ref[...].astype(jnp.float32)
    delta = jnp.concatenate(
        [
            row_of(jnp.sum(product[:, :head_dim], axis=1, keepdims=True)),
            row_of(jnp.sum(product[:, head_dim:], axis=1, keepdims=True)),
        ],
        axis=1,
    )
    totals = total_ref[0]
    places = first + lax.broadcasted_iota(jnp.int32, (1, rows), 1)
    places = jnp.concatenate([places, places], axis=1)
    begins = jnp.concatenate([begin_ref[0], begin_ref[0]], axis=1)

    def step(masked, index):
        key_begin = pl.multiple_of(index * key_rows, key_rows)
        place = pl.ds(key_begin, key_rows)
        keys = kv_ref[place, :head_dim]
        values = kv_ref[place, head_dim:]
        raw = matmul(keys, q_two[...], NT)
        probs = jnp.exp2(raw * scale - totals)
        if masked:
            key_places = key_begin + lax.broadcasted_iota(jnp.int32, (key_rows, 1), 0)
            allowed = (key_places >= begins) & (key_places <= places)
            probs = jnp.where(allowed, probs, 0.0)
        kv_sum[place, head_dim:] += matmul(probs.astype(jnp.bfloat16), g_two[...], NN)
        grad_probs = matmul(values, g_two[...], NT)
        grad_scores = (probs * ((grad_probs - delta) * unit)).astype(jnp.bfloat16)
        kv_sum[place, :head_dim] += matmul(grad_scores, q_two[...], NN)
        dq_two[...] += matmul(grad_scores, keys, TN)

    def either(index, carry):
        key_begin = index * key_rows
        plain = (key_begin >= begin_last) & (key_begin + key_rows - 1 <= first)

        @pl.when(plain)
        def _():
            step(False, index)

        @pl.when(jnp.logical_not(plain))
        def _():
            step(True, index)

        return carry

    low = begin_first // key_rows
    high = (first + rows - 1) // key_rows + 1
    lax.fori_loop(low, high, either, 0)
    grad_q_ref[:, :head_dim] = dq_two[:rows].astype(grad_q_ref.dtype)
    grad_q_ref[:, head_dim:] = dq_two[rows:].astype(grad_q_ref.dtype)

    @pl.when(block == pl.num_programs(0) - 1)
    def _():
        grad_kv_ref[...] = kv_sum[...].astype(grad_kv_ref.dtype)

def attend_back(bounds, queries, grads, outs, totals, begin_rows, kv_all, head_dim, query_rows, key_rows):
    rows = queries.shape[0]
    blocks = rows // query_rows
    wide = pl.BlockSpec((query_rows, 2 * head_dim), lambda i, *_: (i, 0))
    whole = pl.BlockSpec(kv_all.shape, lambda i, *_: (0, 0))
    return pl.pallas_call(
        functools.partial(attend_back_kernel, head_dim, key_rows),
        out_shape=(jax.ShapeDtypeStruct(queries.shape, jnp.float32), jax.ShapeDtypeStruct(kv_all.shape, jnp.bfloat16)),
        grid_spec=pltpu.PrefetchScalarGridSpec(
            num_scalar_prefetch=1,
            grid=(blocks,),
            in_specs=[wide, wide, wide,
                pl.BlockSpec((1, 1, 2 * query_rows), lambda i, *_: (i, 0, 0)),
                pl.BlockSpec((1, 1, query_rows), lambda i, *_: (i, 0, 0)),
                whole],
            out_specs=[wide, whole],
            scratch_shapes=[pltpu.VMEM((2 * query_rows, head_dim), jnp.bfloat16)] * 2
            + [pltpu.VMEM((2 * query_rows, head_dim), jnp.float32), pltpu.VMEM(kv_all.shape, jnp.float32)],
        ),
        compiler_params=pltpu.CompilerParams(vmem_limit_bytes=56 * MIB),
        cost_estimate=pl.CostEstimate(flops=20 * rows * kv_all.shape[0] * head_dim, bytes_accessed=2 * kv_all.size, transcendentals=2 * rows * kv_all.shape[0]),
    )(bounds, queries, grads, outs, totals, begin_rows, kv_all)


from jax.sharding import PartitionSpec as P

EPSILON = 1e-06
ROPE_BASE = 1000000.0
MOMENTUM = 0.5
EMA_DECAY = 0.5
LR_MATRIX = 0.08
LR_GAIN = 0.5
FF_BLOCK = 256
CHUNKS = 3


def mlp_kernel(normed_ref, cot_ref, normed_t_ref, cot_t_ref, weight_ref, hidden_ref, gate_grad_ref, up_grad_ref, weight_grad_ref):
    ways, _, shard, width = weight_ref.shape
    rows = normed_ref.shape[0]
    depth = ways * shard
    row_tile = min(512, rows)

    @pl.loop(0, rows // row_tile)
    def _(tile):
        place = pl.ds(pl.multiple_of(tile * row_tile, row_tile), row_tile)
        x = normed_ref[place, :]
        gate = matmul(x, weight_ref[:, 0].reshape(depth, width), NN)
        up = matmul(x, weight_ref[:, 1].reshape(depth, width), NN)
        grad_hidden = matmul(cot_ref[place, :], weight_ref[:, 2].reshape(depth, width), NN)
        sigmoid = 1.0 / (1.0 + jnp.exp(-gate))
        silu = gate * sigmoid
        hidden_ref[place, :] = (silu * up).astype(hidden_ref.dtype)
        gate_grad_ref[place, :] = (
            grad_hidden * up * (sigmoid * (1.0 + gate * (1.0 - sigmoid)))
        ).astype(gate_grad_ref.dtype)
        up_grad_ref[place, :] = (grad_hidden * silu).astype(up_grad_ref.dtype)

    @pl.loop(0, ways)
    def _(way):
        place = pl.ds(pl.multiple_of(way * shard, shard), shard)
        left = normed_t_ref[place, :]
        weight_grad_ref[way, 0] = matmul(left, gate_grad_ref[...], NN).astype(weight_grad_ref.dtype)
        weight_grad_ref[way, 1] = matmul(left, up_grad_ref[...], NN).astype(weight_grad_ref.dtype)
        weight_grad_ref[way, 2] = matmul(cot_t_ref[place, :], hidden_ref[...], NN).astype(weight_grad_ref.dtype)


def mlp_chunk(normed, cotangent, normed_t, cotangent_t, weights):
    ways, kinds, shard, width = weights.shape
    rows, depth = normed.shape
    block = min(FF_BLOCK, width)

    def held(array):
        return pl.BlockSpec(array.shape, lambda i: (0, 0), pipeline_mode=pl.Buffered(1))

    weight_spec = pl.BlockSpec((ways, kinds, shard, block), lambda i: (0, 0, 0, i))
    row_spec = pl.BlockSpec((rows, block), lambda i: (0, i))
    row_shape = jax.ShapeDtypeStruct((rows, width), jnp.bfloat16)
    return pl.pallas_call(
        mlp_kernel,
        grid=(width // block,),
        in_specs=[held(normed), held(cotangent), held(normed_t), held(cotangent_t), weight_spec],
        out_specs=[row_spec, row_spec, row_spec, weight_spec],
        out_shape=(row_shape, row_shape, row_shape, jax.ShapeDtypeStruct(weights.shape, jnp.bfloat16)),
        compiler_params=pltpu.CompilerParams(vmem_limit_bytes=56 * MIB),
        cost_estimate=pl.CostEstimate(flops=12 * rows * depth * width, bytes_accessed=12 * depth * width, transcendentals=rows * width),
    )(normed, cotangent, normed_t, cotangent_t, weights)


def back_product_kernel(kinds, *refs):
    out_ref = refs[-1]
    total = None
    chunks = (len(refs) - 1) // (kinds + 1)
    for chunk in range(chunks):
        weight_ref = refs[chunk * (kinds + 1) + kinds]
        for kind in range(kinds):
            part = matmul(refs[chunk * (kinds + 1) + kind][...], weight_ref[0, kind], NT)
            total = part if total is None else total + part
    out_ref[0] = total.astype(out_ref.dtype)


def back_product(groups_of, weights, kind_begin, pieces):
    kinds = len(groups_of[0])
    ways, _, shard, width = weights[0].shape
    rows = groups_of[0][0].shape[0]
    per_piece = ways // pieces
    args, specs = [], []
    for lefts, weight in zip(groups_of, weights):
        for left in lefts:
            args.append(left)
            specs.append(pl.BlockSpec(left.shape, lambda i: (0, 0), pipeline_mode=pl.Buffered(1)))
        args.append(weight)
        specs.append(pl.BlockSpec((1, kinds, shard, weight.shape[3]), lambda i: (i, kind_begin // kinds, 0, 0)))
    return pl.pallas_call(
        functools.partial(back_product_kernel, kinds),
        grid=(ways,),
        in_specs=specs,
        out_specs=pl.BlockSpec((1, rows, shard), lambda i: (i // per_piece, 0, i % per_piece)),
        out_shape=jax.ShapeDtypeStruct((pieces, rows, per_piece * shard), jnp.bfloat16),
        compiler_params=pltpu.CompilerParams(vmem_limit_bytes=56 * MIB),
        cost_estimate=pl.CostEstimate(flops=2 * len(weights) * kinds * rows * width * ways * shard, bytes_accessed=2 * len(weights) * kinds * width * ways * shard, transcendentals=0),
    )(*args)


MESH = pl.DeviceIdType.MESH
SUM_BLOCKS = 4


def flip(index, bit):
    unit = 1 << bit
    return index + unit - 2 * unit * ((index // unit) % 2)


def picks(index, fixed, free):
    base = 0
    for bit in fixed:
        unit = 1 << bit
        base = base + unit * ((index // unit) % 2)
    found = []
    for choice in range(1 << len(free)):
        offset = sum((1 << bit) for at, bit in enumerate(free) if (choice >> at) & 1)
        found.append(base + offset)
    return found


def tensor_sum_kernel(bits, whole, part_ref, out_ref, sums, landed, send_sem, recv_sem, send_out, recv_out):
    row_at = lax.axis_index("dp")
    me = lax.axis_index("tensor")
    barrier = pltpu.get_barrier_semaphore()
    for bit in range(bits):
        pl.semaphore_signal(barrier, inc=1, device_id=(row_at, flip(me, bit)), device_id_type=MESH)
    pl.semaphore_wait(barrier, bits)
    tensor_sum_steps(bits, whole, part_ref, out_ref, sums, landed, send_sem, recv_sem, send_out, recv_out)


def tensor_sum_steps(bits, whole, part_ref, out_ref, sums, landed, send_sem, recv_sem, send_out, recv_out):
    row_at = lax.axis_index("dp")
    me = lax.axis_index("tensor")
    rows = part_ref.shape[1] // SUM_BLOCKS
    orders = [list(range(bits)) if b % 2 == 0 else list(range(bits))[::-1] for b in range(SUM_BLOCKS)]

    def place(block):
        return pl.ds(block * rows, rows)

    def scatter(block, step):
        order = orders[block]
        bit = order[step]
        there = flip(me, bit)
        free = order[step + 1 :]
        source = part_ref if step == 0 else sums
        base = (1 << bits) - (1 << (bits - step))
        copies = []
        for at, piece in enumerate(picks(there, order[: step + 1], free)):
            slot = base + at
            copies.append(
                pltpu.make_async_remote_copy(
                    src_ref=source.at[piece, place(block)],
                    dst_ref=landed.at[slot, place(block)],
                    send_sem=send_sem.at[slot, block],
                    recv_sem=recv_sem.at[slot, block],
                    device_id=(row_at, there),
                    device_id_type=MESH,
                )
            )
        return copies

    def gather(block, step):
        order = orders[block][::-1]
        bit = order[step]
        there = flip(me, bit)
        base = (1 << step) - 1
        copies = []
        for at, piece in enumerate(picks(me, order[step:], order[:step])):
            slot = base + at
            copies.append(
                pltpu.make_async_remote_copy(
                    src_ref=out_ref.at[piece, place(block)],
                    dst_ref=out_ref.at[piece, place(block)],
                    send_sem=send_out.at[slot, block],
                    recv_sem=recv_out.at[slot, block],
                    device_id=(row_at, there),
                    device_id_type=MESH,
                )
            )
        return copies

    every = []
    flying = []
    for block in range(SUM_BLOCKS):
        copies = scatter(block, 0)
        for copy in copies:
            copy.start()
        flying.append(copies)
    for step in range(bits):
        for block in range(SUM_BLOCKS):
            order = orders[block]
            base = (1 << bits) - (1 << (bits - step))
            for copy in flying[block]:
                copy.wait_recv()
            every += flying[block]
            source = part_ref if step == 0 else sums
            last = step == bits - 1
            for at, piece in enumerate(picks(me, order[: step + 1], order[step + 1 :])):
                total = source[piece, place(block)].astype(jnp.float32) + landed[base + at, place(block)].astype(jnp.float32)
                if not last:
                    sums[piece, place(block)] = total.astype(sums.dtype)
                elif whole:
                    out_ref[piece, place(block)] = total.astype(out_ref.dtype)
                else:
                    out_ref[place(block)] = total.astype(out_ref.dtype)
            if not last:
                flying[block] = scatter(block, step + 1)
            elif whole:
                flying[block] = gather(block, 0)
            if not last or whole:
                for copy in flying[block]:
                    copy.start()
    if whole:
        for step in range(bits):
            for block in range(SUM_BLOCKS):
                for copy in flying[block]:
                    copy.wait_recv()
                every += flying[block]
                if step < bits - 1:
                    flying[block] = gather(block, step + 1)
                    for copy in flying[block]:
                        copy.start()
    for copy in every:
        copy.wait_send()


def tensor_sum(part, collective_id, whole=True):
    ways, rows, width = part.shape
    bits = ways.bit_length() - 1
    return pl.pallas_call(
        functools.partial(tensor_sum_kernel, bits, whole),
        out_shape=jax.ShapeDtypeStruct(part.shape if whole else part.shape[1:], part.dtype),
        in_specs=[pl.BlockSpec(memory_space=pltpu.VMEM)],
        out_specs=pl.BlockSpec(memory_space=pltpu.VMEM),
        scratch_shapes=[
            pltpu.VMEM(part.shape, part.dtype),
            pltpu.VMEM((ways - 1, rows, width), part.dtype),
            *[pltpu.SemaphoreType.DMA((ways - 1, SUM_BLOCKS))] * 4,
        ],
        compiler_params=pltpu.CompilerParams(
            collective_id=collective_id, has_side_effects=True, vmem_limit_bytes=32 * MIB
        ),
        cost_estimate=pl.CostEstimate(flops=0, bytes_accessed=(256 if whole else 128) * MIB, transcendentals=0),
    )(part)


def spread_kernel(source, slots, me, ways, place, send_sem, recv_sem):
    copies = []
    for step in range(1, ways):
        there = lax.rem(me + step, ways)
        copies.append(
            pltpu.make_async_remote_copy(
                src_ref=source,
                dst_ref=slots.at[me],
                send_sem=send_sem.at[step - 1],
                recv_sem=recv_sem.at[step - 1],
                device_id=place(there),
                device_id_type=MESH,
            )
        )
    for copy in copies:
        copy.start()
    return copies


def total_of(slots, ways):
    total = slots[0]
    for at in range(1, ways):
        total = total + slots[at]
    return total


def last_sum_kernel(
    bits, ways, part_ref, dots_ref, gains_ref, out_ref, dots_out_ref, gains_out_ref,
    sums, landed, dots_land, gains_land, gains_far, gains_mid, send_sem, recv_sem, dots_send, dots_recv,
    near_send, near_recv, far_send, far_recv,
):
    row_at = lax.axis_index("dp")
    me = lax.axis_index("tensor")
    pieces = 1 << bits

    def beside(there):
        return (row_at, there)

    def along(there):
        return (there, me)

    barrier = pltpu.get_barrier_semaphore()
    for step in range(1, pieces):
        pl.semaphore_signal(barrier, inc=1, device_id=beside(lax.rem(me + step, pieces)), device_id_type=MESH)
    for step in range(1, ways):
        pl.semaphore_signal(barrier, inc=1, device_id=along(lax.rem(row_at + step, ways)), device_id_type=MESH)
    pl.semaphore_wait(barrier, pieces + ways - 2)
    gains_land[me] = gains_ref[...]
    dots_land[me] = dots_ref[...]
    near = spread_kernel(gains_ref, gains_land, me, pieces, beside, near_send, near_recv)
    dots = spread_kernel(dots_ref, dots_land, me, pieces, beside, dots_send, dots_recv)
    for copy in near:
        copy.wait()
    gains_mid[...] = total_of(gains_land, pieces)
    gains_far[row_at] = gains_mid[...]
    far = spread_kernel(gains_mid, gains_far, row_at, ways, along, far_send, far_recv)
    tensor_sum_steps(bits, False, part_ref, out_ref, sums, landed, send_sem, recv_sem, None, None)
    for copy in dots:
        copy.wait()
    dots_out_ref[...] = total_of(dots_land, pieces)
    for copy in far:
        copy.wait()
    gains_out_ref[...] = total_of(gains_far, ways)


def last_sum(part, dots, gains, data_ways, collective_id):
    pieces, rows, width = part.shape
    bits = pieces.bit_length() - 1
    near = pltpu.SemaphoreType.DMA((pieces - 1,))
    far = pltpu.SemaphoreType.DMA((data_ways - 1,))
    return pl.pallas_call(
        functools.partial(last_sum_kernel, bits, data_ways),
        out_shape=(
            jax.ShapeDtypeStruct(part.shape[1:], part.dtype),
            jax.ShapeDtypeStruct(dots.shape, dots.dtype),
            jax.ShapeDtypeStruct(gains.shape, gains.dtype),
        ),
        in_specs=[pl.BlockSpec(memory_space=pltpu.VMEM)] * 3,
        out_specs=[pl.BlockSpec(memory_space=pltpu.VMEM)] * 3,
        scratch_shapes=[
            pltpu.VMEM(part.shape, part.dtype),
            pltpu.VMEM((pieces - 1, rows, width), part.dtype),
            pltpu.VMEM((pieces, *dots.shape), dots.dtype),
            pltpu.VMEM((pieces, *gains.shape), gains.dtype),
            pltpu.VMEM((data_ways, *gains.shape), gains.dtype),
            pltpu.VMEM(gains.shape, gains.dtype),
            *[pltpu.SemaphoreType.DMA((pieces - 1, SUM_BLOCKS))] * 2,
            near, near, near, near, far, far,
        ],
        compiler_params=pltpu.CompilerParams(
            collective_id=collective_id, has_side_effects=True, vmem_limit_bytes=32 * MIB
        ),
        cost_estimate=pl.CostEstimate(flops=0, bytes_accessed=128 * MIB, transcendentals=0),
    )(part, dots, gains)


def rms_scale(values_in):
    return lax.rsqrt(jnp.mean(values_in * values_in, axis=-1, keepdims=True) + EPSILON)


def rotate_half(values_in, cosine, sine):
    half_dim = values_in.shape[-1] // 2
    turned = jnp.concatenate([-values_in[..., half_dim:], values_in[..., :half_dim]], axis=-1)
    return values_in * cosine + turned * sine


def rotate_back(grads, cosine, sine):
    half_dim = grads.shape[-1] // 2
    scaled = grads * sine
    turned = jnp.concatenate([scaled[..., half_dim:], -scaled[..., :half_dim]], axis=-1)
    return grads * cosine + turned


def norm_back(grads, normal, scale_rows, gain):
    grad_hat = grads * gain
    return scale_rows * (grad_hat - normal * jnp.mean(grad_hat * normal, axis=-1, keepdims=True))


def rope_tables(offsets, head_dim):
    half_dim = head_dim // 2
    frequency = 1.0 / ROPE_BASE ** (jnp.arange(half_dim, dtype=jnp.float32) * 2.0 / head_dim)
    angles = offsets.astype(jnp.float32)[:, None] * frequency[None, :]
    cosine = jnp.cos(angles)
    sine = jnp.sin(angles)
    return (jnp.concatenate([cosine, cosine], axis=-1), jnp.concatenate([sine, sine], axis=-1))


def nesterov(weight, moment, average, gradient, rate):
    new_moment = MOMENTUM * moment + gradient
    new_weight = weight - rate * (gradient + MOMENTUM * new_moment)
    new_average = EMA_DECAY * average + (1.0 - EMA_DECAY) * new_weight
    return (new_weight, new_moment, new_average, new_average.astype(jnp.bfloat16))


def dot(a, b, dims):
    return lax.dot_general(a, b, dims, preferred_element_type=jnp.float32)


def tie(*values):
    return lax.optimization_barrier(values)


def local(
    hidden_in,
    cotangent,
    doc_lengths,
    valid_mask,
    w_qkv,
    w_out,
    w_gate_up,
    w_down,
    norm_gains,
    m_qkv,
    m_out,
    m_gate_up,
    m_down,
    m_gains,
    a_qkv,
    a_out,
    a_gate_up,
    a_down,
    a_gains,
):
    row_count, model_dim = hidden_in.shape
    head_dim = (norm_gains.shape[0] - 2 * model_dim) // 2
    data_ways = lax.axis_size("dp")
    tensor_ways = lax.axis_size("tensor")
    tensor_at = lax.axis_index("tensor")
    tokens_all = row_count * data_ways
    width_cols = model_dim // tensor_ways
    col_begin = tensor_at * width_cols
    groups = w_qkv.shape[1] // (4 * head_dim)
    ff_local = w_down.shape[0]
    ff_chunk = ff_local // CHUNKS
    bf16 = jnp.bfloat16
    f32 = jnp.float32

    def columns_of(values_in):
        return lax.dynamic_slice_in_dim(values_in, col_begin, width_cols, values_in.ndim - 1)

    def across(pieces):
        return jnp.concatenate([pieces[piece] for piece in range(tensor_ways)], axis=1)

    qkv_full = lax.all_gather(w_qkv.astype(bf16), "dp", axis=0, tiled=True)

    out_turned, qkv_full = tie(w_out.astype(bf16).T, qkv_full)
    out_blocks = lax.all_gather(out_turned, "dp", axis=0)

    ends_at = jnp.cumsum(doc_lengths)
    starts_at = ends_at - doc_lengths
    place_begin = lax.axis_index("dp") * row_count
    places = place_begin + jnp.arange(row_count, dtype=jnp.int32)
    doc_ids = jnp.sum((places[:, None] >= ends_at[None, :]).astype(jnp.int32), axis=1)
    owned = doc_ids[:, None] == jnp.arange(doc_lengths.shape[0], dtype=jnp.int32)[None, :]
    doc_begin = jnp.sum(jnp.where(owned, starts_at[None, :], 0), axis=1)
    cosine, sine = rope_tables(places - doc_begin, head_dim)
    query_rows = min(512, row_count)
    blocks = row_count // query_rows
    bounds = jnp.stack(
        [
            place_begin + jnp.arange(blocks, dtype=jnp.int32) * query_rows,
            doc_begin[::query_rows],
            doc_begin[query_rows - 1 :: query_rows],
        ]
    ).astype(jnp.int32)
    begin_rows = doc_begin.astype(jnp.int32).reshape(blocks, 1, query_rows)

    gain_attn = norm_gains[:model_dim]
    gain_mlp = norm_gains[model_dim : 2 * model_dim]
    gain_query = norm_gains[2 * model_dim : 2 * model_dim + head_dim]
    gain_key = norm_gains[2 * model_dim + head_dim :]
    scale_one = rms_scale(hidden_in)
    normal_one = hidden_in * scale_one
    normed_one_b = (normal_one * gain_attn).astype(bf16)
    projected = dot(normed_one_b, qkv_full, NN)

    raw_queries, raw_keys, queries, kv_every = [], [], [], []
    for group in range(groups):
        base = group * 4 * head_dim
        query_raw = projected[:, base : base + 2 * head_dim].reshape(row_count, 2, head_dim)
        key_raw = projected[:, base + 2 * head_dim : base + 3 * head_dim]
        value = projected[:, base + 3 * head_dim : base + 4 * head_dim]
        query = rotate_half(
            query_raw * rms_scale(query_raw) * gain_query, cosine[:, None], sine[:, None]
        )
        key = rotate_half(key_raw * rms_scale(key_raw) * gain_key, cosine, sine)
        raw_queries.append(query_raw)
        raw_keys.append(key_raw)
        queries.append(query.reshape(row_count, 2 * head_dim).astype(bf16))
        kv_local = jnp.concatenate([key, value], axis=1).astype(bf16)
        if group:
            kv_local, kv_every[-1] = tie(kv_local, kv_every[-1])
        else:
            kv_local, out_blocks = tie(kv_local, out_blocks)
        kv_every.append(lax.all_gather(kv_local, "dp", axis=0, tiled=True))

    down_t = w_down.T
    chunk_weights = []
    out_full_t = out_blocks.reshape(model_dim, w_out.shape[0])

    def chunk_shard(chunk):
        units = slice(chunk * ff_chunk, (chunk + 1) * ff_chunk)
        return jnp.stack([w_gate_up[0, :, units], w_gate_up[1, :, units], down_t[:, units]]).astype(bf16)

    def chunk_gather(shard):
        return lax.all_gather(shard, "dp", axis=0)

    shard, kv_every[-1] = tie(chunk_shard(0), kv_every[-1])
    chunk_weights.append(chunk_gather(shard))
    mixed, totals = [], []
    for group in range(groups):
        mixed_rows, total_rows = attend(
            bounds, queries[group], begin_rows, kv_every[group], head_dim, query_rows, min(1024, tokens_all)
        )
        mixed.append(mixed_rows)
        totals.append(total_rows)
    mixed_b = jnp.concatenate(mixed, axis=1)
    shard, chunk_weights[0], mixed_b = tie(chunk_shard(1), chunk_weights[0], mixed_b)
    chunk_weights.append(chunk_gather(shard))
    attn_part = back_product([(mixed_b,)], [out_blocks[:, None]], 0, tensor_ways)
    attn_sum = tensor_sum(attn_part, 0)
    shard, chunk_weights[1], attn_sum = tie(chunk_shard(2), chunk_weights[1], attn_sum)
    chunk_weights.append(chunk_gather(shard))
    attn = across(attn_sum).astype(f32)
    resid_one = hidden_in + attn
    scale_two = rms_scale(resid_one)
    normal_two = resid_one * scale_two
    normed_two_b = (normal_two * gain_mlp).astype(bf16)

    normed_two_t = normed_two_b.T
    cotangent_t = cotangent.T
    weight_grads, hiddens, back_pairs = [], [], []
    for chunk in range(CHUNKS):
        hidden_b, gate_grad, up_grad, weight_grad = mlp_chunk(
            normed_two_b, cotangent, normed_two_t, cotangent_t, chunk_weights[chunk]
        )
        hiddens.append((hidden_b,))
        back_pairs.append((gate_grad, up_grad))
        weight_grads.append(lax.psum_scatter(weight_grad, "dp", scatter_dimension=0))

    part_two = back_product(back_pairs, chunk_weights, 0, tensor_ways)
    part_two, weight_grads[0] = tie(part_two, weight_grads[0])
    grad_normed_two = across(tensor_sum(part_two, 1)).astype(f32)
    gain_mlp_part = jnp.sum(columns_of(grad_normed_two * normal_two), axis=0)
    grad_resid = cotangent.astype(f32) + norm_back(grad_normed_two, normal_two, scale_two, gain_mlp)
    grad_attn_b = grad_resid.astype(bf16)
    grad_mixed_b = dot(grad_attn_b, out_full_t, NN).astype(bf16)

    grad_queries, kv_grads = [], []
    for group in range(groups):
        cols = slice(group * 2 * head_dim, (group + 1) * 2 * head_dim)
        grad_rows, weight_grads[group + 1] = tie(grad_mixed_b[:, cols], weight_grads[group + 1])
        grad_query, kv_grad = attend_back(
            bounds,
            queries[group],
            grad_rows,
            mixed[group],
            totals[group],
            begin_rows,
            kv_every[group],
            head_dim,
            query_rows,
            min(512, tokens_all),
        )
        grad_queries.append(grad_query)
        kv_grads.append(lax.psum_scatter(kv_grad, "dp", scatter_dimension=0, tiled=True).astype(f32))
    grad_out_t = dot(grad_attn_b, mixed_b, TN).astype(bf16)
    grad_out_t, kv_grads[-1] = tie(grad_out_t, kv_grads[-1])
    out_shard = lax.psum_scatter(grad_out_t, "dp", scatter_dimension=0, tiled=True).astype(f32).T

    hidden_first, grad_queries[-1] = tie(hiddens[0][0], grad_queries[-1])
    hiddens[0] = (hidden_first,)
    mlp_part = back_product(hiddens, chunk_weights, 2, tensor_ways)
    mlp_cols = tensor_sum(mlp_part, 2, False).astype(f32)

    grad_parts = []
    gain_query_part = jnp.zeros((head_dim,), f32)
    gain_key_part = jnp.zeros((head_dim,), f32)
    for group in range(groups):
        query_raw = raw_queries[group]
        key_raw = raw_keys[group]
        query_scale = rms_scale(query_raw)
        query_normal = query_raw * query_scale
        key_scale = rms_scale(key_raw)
        key_normal = key_raw * key_scale
        grad_query_norm = rotate_back(
            grad_queries[group].reshape(row_count, 2, head_dim), cosine[:, None], sine[:, None]
        )
        gain_query_part += jnp.sum(grad_query_norm * query_normal, axis=(0, 1))
        grad_query_raw = norm_back(grad_query_norm, query_normal, query_scale, gain_query)
        grad_key_norm = rotate_back(kv_grads[group][:, :head_dim], cosine, sine)
        gain_key_part += jnp.sum(grad_key_norm * key_normal, axis=0)
        grad_key_raw = norm_back(grad_key_norm, key_normal, key_scale, gain_key)
        grad_parts += [
            grad_query_raw.reshape(row_count, 2 * head_dim),
            grad_key_raw,
            kv_grads[group][:, head_dim:],
        ]
    grad_projected_b = jnp.concatenate([part.astype(bf16) for part in grad_parts], axis=1)
    grad_qkv = dot(normed_one_b, grad_projected_b, TN).astype(bf16)
    qkv_shard = lax.psum_scatter(grad_qkv, "dp", scatter_dimension=0, tiled=True).astype(f32)
    part_one = dot(grad_projected_b, qkv_full, NT)
    part_one_b = jnp.stack(
        [part_one[:, at * width_cols : (at + 1) * width_cols] for at in range(tensor_ways)]
    ).astype(bf16)
    dots_part = jnp.sum(part_one * (normal_one * gain_attn), axis=1).reshape(row_count // 128, 128)
    gain_attn_part = jnp.sum(part_one * normal_one, axis=0)

    attn_cols = columns_of(attn)
    mixed_cols = columns_of(resid_one) + mlp_cols
    mask_rows = valid_mask.astype(f32)[:, None]

    def column_squares(columns):
        return jnp.sum(mask_rows * columns * columns)

    count_part = jnp.where(tensor_at == 0, jnp.sum(valid_mask.astype(f32)), 0.0)
    stats_part = jnp.stack(
        [
            column_squares(columns_of(hidden_in)),
            column_squares(attn_cols),
            column_squares(mlp_cols),
            count_part,
        ]
    )
    gain_mlp_wide = lax.dynamic_update_slice_in_dim(
        jnp.zeros((model_dim,), f32), gain_mlp_part, col_begin, 0
    )
    gains_part = jnp.concatenate(
        [gain_attn_part, gain_mlp_wide, gain_query_part, gain_key_part, stats_part]
    )
    gains_count = gains_part.shape[0]
    gains_rows = -(-gains_count // 1024) * 8
    gains_part = jnp.pad(gains_part, (0, gains_rows * 128 - gains_count)).reshape(gains_rows, 128)
    grad_one_cols, row_dots, gains_sum = last_sum(part_one_b, dots_part, gains_part, data_ways, 3)
    gains_sum = gains_sum.reshape(-1)[:gains_count]
    grad_cols = columns_of(grad_resid) + scale_one * (
        grad_one_cols.astype(f32) * columns_of(gain_attn)
        - columns_of(normal_one) * (row_dots.reshape(row_count, 1) / model_dim)
    )
    grad_gains = gains_sum[: norm_gains.shape[0]]
    stats_sum = gains_sum[norm_gains.shape[0] :]
    branch_rms = jnp.sqrt(stats_sum[:3] / (stats_sum[3] * model_dim))

    rate_matrix = LR_MATRIX / math.sqrt(tokens_all)
    rate_gain = LR_GAIN / math.sqrt(tokens_all)
    gate_up_shard = jnp.concatenate([grad[:2] for grad in weight_grads], axis=2).astype(f32)
    down_shard = jnp.concatenate([grad[2] for grad in weight_grads], axis=1).astype(f32).T
    return (
        mixed_cols,
        grad_cols,
        branch_rms,
        *nesterov(w_qkv, m_qkv, a_qkv, qkv_shard, rate_matrix),
        *nesterov(w_out, m_out, a_out, out_shard, rate_matrix),
        *nesterov(w_gate_up, m_gate_up, a_gate_up, gate_up_shard, rate_matrix),
        *nesterov(w_down, m_down, a_down, down_shard, rate_matrix),
        *nesterov(norm_gains, m_gains, a_gains, grad_gains, rate_gain),
    )


def solution(mesh):
    rows = P("dp", None)
    spread = P("dp", "tensor")
    turned = P("tensor", "dp")
    stacked = P(None, "dp", "tensor")
    matrices = (spread, turned, stacked, turned, P())
    in_specs = (rows, rows, P(), P("dp"), *matrices, *matrices, *matrices)
    out_specs = (spread, spread, P(), *(spec for spec in matrices for _ in range(4)))
    return jax.shard_map(local, mesh=mesh, in_specs=in_specs, out_specs=out_specs, check_vma=False)
```

```python
import functools, math
import jax, jax.numpy as jnp
from jax import lax
from jax.experimental import pallas as pl
from jax.experimental.pallas import tpu as pltpu
NT = (((1,), (1,)), ((), ()))
NN = (((1,), (0,)), ((), ()))
TN = (((0,), (0,)), ((), ()))
NEG_FILL = -1e30
LOG2E = math.log2(math.e)
MIB = 1024 * 1024

def matmul(a, b, dims):
    return lax.dot_general(a, b, dims, preferred_element_type=jnp.float32)

def row_of(column):
    return jnp.transpose(jnp.broadcast_to(column, (column.shape[0], 128)))[:1]

def attend_kernel(head_dim, key_rows, bound_ref, query_ref, begin_ref, kv_ref, out_ref, total_ref, q_two, accum):
    rows = query_ref.shape[0]
    block = pl.program_id(0)
    first = bound_ref[0, block]
    begin_first = bound_ref[1, block]
    begin_last = bound_ref[2, block]
    scale = LOG2E * head_dim**-0.5
    q_two[:rows] = query_ref[:, :head_dim]
    q_two[rows:] = query_ref[:, head_dim:]
    places = first + lax.broadcasted_iota(jnp.int32, (1, rows), 1)
    places = jnp.concatenate([places, places], axis=1)
    begins = jnp.concatenate([begin_ref[0], begin_ref[0]], axis=1)

    def step(masked, index, carry):
        top, total = carry
        key_begin = pl.multiple_of(index * key_rows, key_rows)
        keys = kv_ref[pl.ds(key_begin, key_rows), :head_dim]
        values = kv_ref[pl.ds(key_begin, key_rows), head_dim:]
        raw = matmul(keys, q_two[...], NT) * scale
        if masked:
            key_places = key_begin + lax.broadcasted_iota(jnp.int32, (key_rows, 1), 0)
            allowed = (key_places >= begins) & (key_places <= places)
            raw = jnp.where(allowed, raw, NEG_FILL)
        new_top = jnp.maximum(top, jnp.max(raw, axis=0, keepdims=True))
        probs = jnp.exp2(raw - new_top)
        fade = jnp.exp2(top - new_top)
        total = total * fade + jnp.sum(probs, axis=0, keepdims=True)
        accum[...] = accum[...] * fade + matmul(values, probs.astype(jnp.bfloat16), TN)
        return (new_top, total)

    def either(index, carry):
        key_begin = index * key_rows
        plain = (key_begin >= begin_last) & (key_begin + key_rows - 1 <= first)
        return lax.cond(
            plain, functools.partial(step, False, index), functools.partial(step, True, index), carry
        )

    accum[...] = jnp.zeros_like(accum)
    start = (
        jnp.full((1, 2 * rows), NEG_FILL, jnp.float32),
        jnp.zeros((1, 2 * rows), jnp.float32),
    )
    low = begin_first // key_rows
    high = (first + rows - 1) // key_rows + 1
    top, total = lax.fori_loop(low, high, either, start)
    out = jnp.transpose(accum[...] / total)
    out_ref[:, :head_dim] = out[:rows].astype(out_ref.dtype)
    out_ref[:, head_dim:] = out[rows:].astype(out_ref.dtype)
    total_ref[0] = top + jnp.log2(total)

def attend(bounds, queries, begins, kv_all, head_dim, query_rows, key_rows):
    rows = queries.shape[0]
    blocks = rows // query_rows
    return pl.pallas_call(
        functools.partial(attend_kernel, head_dim, key_rows),
        out_shape=(jax.ShapeDtypeStruct(queries.shape, jnp.bfloat16), jax.ShapeDtypeStruct((blocks, 1, 2 * query_rows), jnp.float32)),
        grid_spec=pltpu.PrefetchScalarGridSpec(
            num_scalar_prefetch=1,
            grid=(blocks,),
            in_specs=[
                pl.BlockSpec((query_rows, 2 * head_dim), lambda i, *_: (i, 0)),
                pl.BlockSpec((1, 1, query_rows), lambda i, *_: (i, 0, 0)),
                pl.BlockSpec(kv_all.shape, lambda i, *_: (0, 0)),
            ],
            out_specs=[
                pl.BlockSpec((query_rows, 2 * head_dim), lambda i, *_: (i, 0)),
                pl.BlockSpec((1, 1, 2 * query_rows), lambda i, *_: (i, 0, 0)),
            ],
            scratch_shapes=[pltpu.VMEM((2 * query_rows, head_dim), jnp.bfloat16), pltpu.VMEM((head_dim, 2 * query_rows), jnp.float32)],
        ),
        compiler_params=pltpu.CompilerParams(vmem_limit_bytes=48 * MIB),
        cost_estimate=pl.CostEstimate(flops=8 * rows * kv_all.shape[0] * head_dim, bytes_accessed=2 * kv_all.size, transcendentals=2 * rows * kv_all.shape[0]),
    )(bounds, queries, begins, kv_all)

def attend_back_kernel(head_dim, key_rows, bound_ref, query_ref, grad_ref, out_ref, total_ref, begin_ref, kv_ref, grad_q_ref, grad_kv_ref, q_two, g_two, dq_two, kv_sum):
    rows = query_ref.shape[0]
    block = pl.program_id(0)
    first = bound_ref[0, block]
    begin_first = bound_ref[1, block]
    begin_last = bound_ref[2, block]
    unit = head_dim**-0.5
    scale = LOG2E * unit

    @pl.when(block == 0)
    def _():
        kv_sum[...] = jnp.zeros_like(kv_sum)

    for half in range(2):
        part = slice(half * rows, (half + 1) * rows)
        cols = slice(half * head_dim, (half + 1) * head_dim)
        q_two[part] = query_ref[:, cols]
        g_two[part] = grad_ref[:, cols]
    dq_two[...] = jnp.zeros_like(dq_two)
    product = grad_ref[...].astype(jnp.float32) * out_ref[...].astype(jnp.float32)
    delta = jnp.concatenate(
        [
            row_of(jnp.sum(product[:, :head_dim], axis=1, keepdims=True)),
            row_of(jnp.sum(product[:, head_dim:], axis=1, keepdims=True)),
        ],
        axis=1,
    )
    totals = total_ref[0]
    places = first + lax.broadcasted_iota(jnp.int32, (1, rows), 1)
    places = jnp.concatenate([places, places], axis=1)
    begins = jnp.concatenate([begin_ref[0], begin_ref[0]], axis=1)

    def step(masked, index):
        key_begin = pl.multiple_of(index * key_rows, key_rows)
        place = pl.ds(key_begin, key_rows)
        keys = kv_ref[place, :head_dim]
        values = kv_ref[place, head_dim:]
        raw = matmul(keys, q_two[...], NT)
        probs = jnp.exp2(raw * scale - totals)
        if masked:
            key_places = key_begin + lax.broadcasted_iota(jnp.int32, (key_rows, 1), 0)
            allowed = (key_places >= begins) & (key_places <= places)
            probs = jnp.where(allowed, probs, 0.0)
        kv_sum[place, head_dim:] += matmul(probs.astype(jnp.bfloat16), g_two[...], NN)
        grad_probs = matmul(values, g_two[...], NT)
        grad_scores = (probs * ((grad_probs - delta) * unit)).astype(jnp.bfloat16)
        kv_sum[place, :head_dim] += matmul(grad_scores, q_two[...], NN)
        dq_two[...] += matmul(grad_scores, keys, TN)

    def either(index, carry):
        key_begin = index * key_rows
        plain = (key_begin >= begin_last) & (key_begin + key_rows - 1 <= first)

        @pl.when(plain)
        def _():
            step(False, index)

        @pl.when(jnp.logical_not(plain))
        def _():
            step(True, index)

        return carry

    low = begin_first // key_rows
    high = (first + rows - 1) // key_rows + 1
    lax.fori_loop(low, high, either, 0)
    grad_q_ref[:, :head_dim] = dq_two[:rows].astype(grad_q_ref.dtype)
    grad_q_ref[:, head_dim:] = dq_two[rows:].astype(grad_q_ref.dtype)

    @pl.when(block == pl.num_programs(0) - 1)
    def _():
        grad_kv_ref[...] = kv_sum[...].astype(grad_kv_ref.dtype)

def attend_back(bounds, queries, grads, outs, totals, begin_rows, kv_all, head_dim, query_rows, key_rows):
    rows = queries.shape[0]
    blocks = rows // query_rows
    wide = pl.BlockSpec((query_rows, 2 * head_dim), lambda i, *_: (i, 0))
    whole = pl.BlockSpec(kv_all.shape, lambda i, *_: (0, 0))
    return pl.pallas_call(
        functools.partial(attend_back_kernel, head_dim, key_rows),
        out_shape=(jax.ShapeDtypeStruct(queries.shape, jnp.float32), jax.ShapeDtypeStruct(kv_all.shape, jnp.bfloat16)),
        grid_spec=pltpu.PrefetchScalarGridSpec(
            num_scalar_prefetch=1,
            grid=(blocks,),
            in_specs=[wide, wide, wide,
                pl.BlockSpec((1, 1, 2 * query_rows), lambda i, *_: (i, 0, 0)),
                pl.BlockSpec((1, 1, query_rows), lambda i, *_: (i, 0, 0)),
                whole],
            out_specs=[wide, whole],
            scratch_shapes=[pltpu.VMEM((2 * query_rows, head_dim), jnp.bfloat16)] * 2
            + [pltpu.VMEM((2 * query_rows, head_dim), jnp.float32), pltpu.VMEM(kv_all.shape, jnp.float32)],
        ),
        compiler_params=pltpu.CompilerParams(vmem_limit_bytes=56 * MIB),
        cost_estimate=pl.CostEstimate(flops=20 * rows * kv_all.shape[0] * head_dim, bytes_accessed=2 * kv_all.size, transcendentals=2 * rows * kv_all.shape[0]),
    )(bounds, queries, grads, outs, totals, begin_rows, kv_all)


from jax.sharding import PartitionSpec as P

EPSILON = 1e-06
ROPE_BASE = 1000000.0
MOMENTUM = 0.5
EMA_DECAY = 0.5
LR_MATRIX = 0.08
LR_GAIN = 0.5
FF_BLOCK = 256
CHUNKS = 3


def mlp_kernel(normed_ref, cot_ref, normed_t_ref, cot_t_ref, weight_ref, hidden_ref, gate_grad_ref, up_grad_ref, grads_ref, wide):
    ways, kinds, shard, _ = weight_ref.shape
    rows = normed_ref.shape[0]
    row_tile = min(512, rows)

    for at in range(ways):
        wide[:, at * shard : (at + 1) * shard, :] = weight_ref[at]

    @pl.loop(0, rows // row_tile)
    def _(tile):
        place = pl.ds(pl.multiple_of(tile * row_tile, row_tile), row_tile)
        x = normed_ref[place, :]
        gate = matmul(x, wide[0], NN)
        up = matmul(x, wide[1], NN)
        grad_hidden = matmul(cot_ref[place, :], wide[2], NN)
        sigmoid = 1.0 / (1.0 + jnp.exp(-gate))
        silu = gate * sigmoid
        hidden_ref[place, :] = (silu * up).astype(hidden_ref.dtype)
        gate_grad_ref[place, :] = (
            grad_hidden * up * (sigmoid * (1.0 + gate * (1.0 - sigmoid)))
        ).astype(gate_grad_ref.dtype)
        up_grad_ref[place, :] = (grad_hidden * silu).astype(up_grad_ref.dtype)

    for at in range(ways):
        place = slice(at * shard, (at + 1) * shard)
        left = normed_t_ref[place, :]
        grads_ref[at, 0] = matmul(left, gate_grad_ref[...], NN).astype(grads_ref.dtype)
        grads_ref[at, 1] = matmul(left, up_grad_ref[...], NN).astype(grads_ref.dtype)
        grads_ref[at, 2] = matmul(cot_t_ref[place, :], hidden_ref[...], NN).astype(grads_ref.dtype)


def mlp_chunk(normed, cotangent, normed_t, cotangent_t, weights):
    ways, _, shard, width = weights.shape
    rows, depth = normed.shape
    block = min(FF_BLOCK, width)

    def held(array):
        return pl.BlockSpec(array.shape, lambda i: (0, 0), pipeline_mode=pl.Buffered(1))

    weight_spec = pl.BlockSpec((ways, 3, shard, block), lambda i: (0, 0, 0, i))
    row_spec = pl.BlockSpec((rows, block), lambda i: (0, i))
    row_shape = jax.ShapeDtypeStruct((rows, width), jnp.bfloat16)
    return pl.pallas_call(
        mlp_kernel,
        grid=(width // block,),
        in_specs=[held(normed), held(cotangent), held(normed_t), held(cotangent_t), weight_spec],
        out_specs=[row_spec, row_spec, row_spec, weight_spec],
        out_shape=(row_shape, row_shape, row_shape, jax.ShapeDtypeStruct((ways, 3, shard, width), jnp.bfloat16)),
        scratch_shapes=[pltpu.VMEM((3, depth, block), jnp.bfloat16)],
        compiler_params=pltpu.CompilerParams(vmem_limit_bytes=56 * MIB),
        cost_estimate=pl.CostEstimate(flops=24 * rows * depth * width, bytes_accessed=12 * depth * width, transcendentals=rows * width),
    )(normed, cotangent, normed_t, cotangent_t, weights)


def back_product_kernel(kinds, *refs):
    out_ref = refs[-1]
    total = None
    chunks = (len(refs) - 1) // (kinds + 1)
    for chunk in range(chunks):
        weight_ref = refs[chunk * (kinds + 1) + kinds]
        for kind in range(kinds):
            part = matmul(refs[chunk * (kinds + 1) + kind][...], weight_ref[0, kind], NT)
            total = part if total is None else total + part
    out_ref[0] = total.astype(out_ref.dtype)


def back_product(groups_of, weights, kind_begin, pieces):
    kinds = len(groups_of[0])
    ways, _, shard, width = weights[0].shape
    rows = groups_of[0][0].shape[0]
    per_piece = ways // pieces
    args, specs = [], []
    for lefts, weight in zip(groups_of, weights):
        for left in lefts:
            args.append(left)
            specs.append(pl.BlockSpec(left.shape, lambda i: (0, 0), pipeline_mode=pl.Buffered(1)))
        args.append(weight)
        specs.append(pl.BlockSpec((1, kinds, shard, weight.shape[3]), lambda i: (i, kind_begin // kinds, 0, 0)))
    return pl.pallas_call(
        functools.partial(back_product_kernel, kinds),
        grid=(ways,),
        in_specs=specs,
        out_specs=pl.BlockSpec((1, rows, shard), lambda i: (i // per_piece, 0, i % per_piece)),
        out_shape=jax.ShapeDtypeStruct((pieces, rows, per_piece * shard), jnp.bfloat16),
        compiler_params=pltpu.CompilerParams(vmem_limit_bytes=56 * MIB),
        cost_estimate=pl.CostEstimate(flops=2 * len(weights) * kinds * rows * width * ways * shard, bytes_accessed=2 * len(weights) * kinds * width * ways * shard, transcendentals=0),
    )(*args)


MESH = pl.DeviceIdType.MESH
SUM_BLOCKS = 4


def flip(index, bit):
    unit = 1 << bit
    return index + unit - 2 * unit * ((index // unit) % 2)


def picks(index, fixed, free):
    base = 0
    for bit in fixed:
        unit = 1 << bit
        base = base + unit * ((index // unit) % 2)
    found = []
    for choice in range(1 << len(free)):
        offset = sum((1 << bit) for at, bit in enumerate(free) if (choice >> at) & 1)
        found.append(base + offset)
    return found


def tensor_sum_kernel(bits, whole, part_ref, out_ref, sums, landed, send_sem, recv_sem, send_out, recv_out):
    row_at = lax.axis_index("dp")
    me = lax.axis_index("tensor")
    barrier = pltpu.get_barrier_semaphore()
    for bit in range(bits):
        pl.semaphore_signal(barrier, inc=1, device_id=(row_at, flip(me, bit)), device_id_type=MESH)
    pl.semaphore_wait(barrier, bits)
    tensor_sum_steps(bits, whole, part_ref, out_ref, sums, landed, send_sem, recv_sem, send_out, recv_out)


def tensor_sum_steps(bits, whole, part_ref, out_ref, sums, landed, send_sem, recv_sem, send_out, recv_out):
    row_at = lax.axis_index("dp")
    me = lax.axis_index("tensor")
    rows = part_ref.shape[1] // SUM_BLOCKS
    orders = [list(range(bits)) if b % 2 == 0 else list(range(bits))[::-1] for b in range(SUM_BLOCKS)]

    def place(block):
        return pl.ds(block * rows, rows)

    def scatter(block, step):
        order = orders[block]
        bit = order[step]
        there = flip(me, bit)
        free = order[step + 1 :]
        source = part_ref if step == 0 else sums
        base = (1 << bits) - (1 << (bits - step))
        copies = []
        for at, piece in enumerate(picks(there, order[: step + 1], free)):
            slot = base + at
            copies.append(
                pltpu.make_async_remote_copy(
                    src_ref=source.at[piece, place(block)],
                    dst_ref=landed.at[slot, place(block)],
                    send_sem=send_sem.at[slot, block],
                    recv_sem=recv_sem.at[slot, block],
                    device_id=(row_at, there),
                    device_id_type=MESH,
                )
            )
        return copies

    def gather(block, step):
        order = orders[block][::-1]
        bit = order[step]
        there = flip(me, bit)
        base = (1 << step) - 1
        copies = []
        for at, piece in enumerate(picks(me, order[step:], order[:step])):
            slot = base + at
            copies.append(
                pltpu.make_async_remote_copy(
                    src_ref=out_ref.at[piece, place(block)],
                    dst_ref=out_ref.at[piece, place(block)],
                    send_sem=send_out.at[slot, block],
                    recv_sem=recv_out.at[slot, block],
                    device_id=(row_at, there),
                    device_id_type=MESH,
                )
            )
        return copies

    every = []
    flying = []
    for block in range(SUM_BLOCKS):
        copies = scatter(block, 0)
        for copy in copies:
            copy.start()
        flying.append(copies)
    for step in range(bits):
        for block in range(SUM_BLOCKS):
            order = orders[block]
            base = (1 << bits) - (1 << (bits - step))
            for copy in flying[block]:
                copy.wait_recv()
            every += flying[block]
            source = part_ref if step == 0 else sums
            last = step == bits - 1
            for at, piece in enumerate(picks(me, order[: step + 1], order[step + 1 :])):
                total = source[piece, place(block)].astype(jnp.float32) + landed[base + at, place(block)].astype(jnp.float32)
                if not last:
                    sums[piece, place(block)] = total.astype(sums.dtype)
                elif whole:
                    out_ref[piece, place(block)] = total.astype(out_ref.dtype)
                else:
                    out_ref[place(block)] = total.astype(out_ref.dtype)
            if not last:
                flying[block] = scatter(block, step + 1)
            elif whole:
                flying[block] = gather(block, 0)
            if not last or whole:
                for copy in flying[block]:
                    copy.start()
    if whole:
        for step in range(bits):
            for block in range(SUM_BLOCKS):
                for copy in flying[block]:
                    copy.wait_recv()
                every += flying[block]
                if step < bits - 1:
                    flying[block] = gather(block, step + 1)
                    for copy in flying[block]:
                        copy.start()
    for copy in every:
        copy.wait_send()


def tensor_sum(part, collective_id, whole=True):
    ways, rows, width = part.shape
    bits = ways.bit_length() - 1
    return pl.pallas_call(
        functools.partial(tensor_sum_kernel, bits, whole),
        out_shape=jax.ShapeDtypeStruct(part.shape if whole else part.shape[1:], part.dtype),
        in_specs=[pl.BlockSpec(memory_space=pltpu.VMEM)],
        out_specs=pl.BlockSpec(memory_space=pltpu.VMEM),
        scratch_shapes=[
            pltpu.VMEM(part.shape, part.dtype),
            pltpu.VMEM((ways - 1, rows, width), part.dtype),
            *[pltpu.SemaphoreType.DMA((ways - 1, SUM_BLOCKS))] * 4,
        ],
        compiler_params=pltpu.CompilerParams(
            collective_id=collective_id, has_side_effects=True, vmem_limit_bytes=32 * MIB
        ),
        cost_estimate=pl.CostEstimate(flops=0, bytes_accessed=(256 if whole else 128) * MIB, transcendentals=0),
    )(part)


def spread_kernel(source, slots, me, ways, place, send_sem, recv_sem):
    copies = []
    for step in range(1, ways):
        there = lax.rem(me + step, ways)
        copies.append(
            pltpu.make_async_remote_copy(
                src_ref=source,
                dst_ref=slots.at[me],
                send_sem=send_sem.at[step - 1],
                recv_sem=recv_sem.at[step - 1],
                device_id=place(there),
                device_id_type=MESH,
            )
        )
    for copy in copies:
        copy.start()
    return copies


def total_of(slots, ways):
    total = slots[0]
    for at in range(1, ways):
        total = total + slots[at]
    return total


def last_sum_kernel(
    bits, ways, part_ref, dots_ref, gains_ref, out_ref, dots_out_ref, gains_out_ref,
    sums, landed, dots_land, gains_land, gains_far, gains_mid, send_sem, recv_sem, dots_send, dots_recv,
    near_send, near_recv, far_send, far_recv,
):
    row_at = lax.axis_index("dp")
    me = lax.axis_index("tensor")
    pieces = 1 << bits

    def beside(there):
        return (row_at, there)

    def along(there):
        return (there, me)

    barrier = pltpu.get_barrier_semaphore()
    for step in range(1, pieces):
        pl.semaphore_signal(barrier, inc=1, device_id=beside(lax.rem(me + step, pieces)), device_id_type=MESH)
    for step in range(1, ways):
        pl.semaphore_signal(barrier, inc=1, device_id=along(lax.rem(row_at + step, ways)), device_id_type=MESH)
    pl.semaphore_wait(barrier, pieces + ways - 2)
    gains_land[me] = gains_ref[...]
    dots_land[me] = dots_ref[...]
    near = spread_kernel(gains_ref, gains_land, me, pieces, beside, near_send, near_recv)
    dots = spread_kernel(dots_ref, dots_land, me, pieces, beside, dots_send, dots_recv)
    for copy in near:
        copy.wait()
    gains_mid[...] = total_of(gains_land, pieces)
    gains_far[row_at] = gains_mid[...]
    far = spread_kernel(gains_mid, gains_far, row_at, ways, along, far_send, far_recv)
    tensor_sum_steps(bits, False, part_ref, out_ref, sums, landed, send_sem, recv_sem, None, None)
    for copy in dots:
        copy.wait()
    dots_out_ref[...] = total_of(dots_land, pieces)
    for copy in far:
        copy.wait()
    gains_out_ref[...] = total_of(gains_far, ways)


def last_sum(part, dots, gains, data_ways, collective_id):
    pieces, rows, width = part.shape
    bits = pieces.bit_length() - 1
    near = pltpu.SemaphoreType.DMA((pieces - 1,))
    far = pltpu.SemaphoreType.DMA((data_ways - 1,))
    return pl.pallas_call(
        functools.partial(last_sum_kernel, bits, data_ways),
        out_shape=(
            jax.ShapeDtypeStruct(part.shape[1:], part.dtype),
            jax.ShapeDtypeStruct(dots.shape, dots.dtype),
            jax.ShapeDtypeStruct(gains.shape, gains.dtype),
        ),
        in_specs=[pl.BlockSpec(memory_space=pltpu.VMEM)] * 3,
        out_specs=[pl.BlockSpec(memory_space=pltpu.VMEM)] * 3,
        scratch_shapes=[
            pltpu.VMEM(part.shape, part.dtype),
            pltpu.VMEM((pieces - 1, rows, width), part.dtype),
            pltpu.VMEM((pieces, *dots.shape), dots.dtype),
            pltpu.VMEM((pieces, *gains.shape), gains.dtype),
            pltpu.VMEM((data_ways, *gains.shape), gains.dtype),
            pltpu.VMEM(gains.shape, gains.dtype),
            *[pltpu.SemaphoreType.DMA((pieces - 1, SUM_BLOCKS))] * 2,
            near, near, near, near, far, far,
        ],
        compiler_params=pltpu.CompilerParams(
            collective_id=collective_id, has_side_effects=True, vmem_limit_bytes=32 * MIB
        ),
        cost_estimate=pl.CostEstimate(flops=0, bytes_accessed=128 * MIB, transcendentals=0),
    )(part, dots, gains)


def turned_by(values, signs):
    return pltpu.roll(values, values.shape[1] // 2, 1) * signs


def half_signs(head_dim, first):
    lanes = lax.broadcasted_iota(jnp.int32, (1, head_dim), 1)
    return jnp.where(lanes < head_dim // 2, first, -first)


def front_kernel(groups, head_dim, normed_ref, weight_ref, cos_ref, sin_ref, gains_ref, raw_ref, *outs):
    raw_ref[...] = matmul(normed_ref[...], weight_ref[...], NN)
    cosine = cos_ref[...]
    sine = sin_ref[...] * half_signs(head_dim, -1.0)
    for group in range(groups):
        for at in range(4):
            base = (group * 4 + at) * head_dim
            raw = raw_ref[:, base : base + head_dim]
            if at < 3:
                gain = gains_ref[at // 2 : at // 2 + 1]
                scale = lax.rsqrt(jnp.mean(raw * raw, axis=1, keepdims=True) + EPSILON)
                raw = raw * scale * gain
                raw = raw * cosine + turned_by(raw, sine)
            out = outs[group] if at < 2 else outs[groups + group]
            out[:, at % 2 * head_dim : (at % 2 + 1) * head_dim] = raw.astype(out.dtype)


def front(normed, weight, cosine, sine, gains, head_dim):
    rows, depth = normed.shape
    width = weight.shape[1]
    groups = width // (4 * head_dim)
    block = min(256, rows)
    narrow = pl.BlockSpec((block, 2 * head_dim), lambda i: (i, 0))
    table = pl.BlockSpec((block, head_dim), lambda i: (i, 0))
    found = pl.pallas_call(
        functools.partial(front_kernel, groups, head_dim),
        grid=(rows // block,),
        in_specs=[
            pl.BlockSpec((block, depth), lambda i: (i, 0)),
            pl.BlockSpec(weight.shape, lambda i: (0, 0), pipeline_mode=pl.Buffered(1)),
            table,
            table,
            pl.BlockSpec(gains.shape, lambda i: (0, 0)),
        ],
        out_specs=[pl.BlockSpec((block, width), lambda i: (i, 0))] + [narrow] * (2 * groups),
        out_shape=[jax.ShapeDtypeStruct((rows, width), jnp.float32)]
        + [jax.ShapeDtypeStruct((rows, 2 * head_dim), jnp.bfloat16)] * (2 * groups),
        compiler_params=pltpu.CompilerParams(vmem_limit_bytes=32 * MIB),
        cost_estimate=pl.CostEstimate(flops=4 * rows * depth * width, bytes_accessed=2 * depth * width, transcendentals=0),
    )(normed, weight, cosine, sine, gains)
    return found[0], found[1 : 1 + groups], found[1 + groups :]


def front_back_kernel(groups, head_dim, raw_ref, cos_ref, sin_ref, gains_ref, *refs):
    queries, keys = refs[:groups], refs[groups : 2 * groups]
    out_ref, sums_ref = refs[2 * groups :]

    @pl.when(pl.program_id(0) == 0)
    def _():
        sums_ref[...] = jnp.zeros_like(sums_ref)

    cosine = cos_ref[...]
    sine = sin_ref[...] * half_signs(head_dim, 1.0)
    for group in range(groups):
        for at in range(4):
            base = (group * 4 + at) * head_dim
            source = queries[group] if at < 2 else keys[group]
            grads = source[:, at % 2 * head_dim : (at % 2 + 1) * head_dim].astype(jnp.float32)
            if at < 3:
                gain = gains_ref[at // 2 : at // 2 + 1]
                raw = raw_ref[:, base : base + head_dim]
                scale = lax.rsqrt(jnp.mean(raw * raw, axis=1, keepdims=True) + EPSILON)
                normal = raw * scale
                grads = grads * cosine + turned_by(grads, sine)
                sums_ref[at // 2 : at // 2 + 1] += jnp.sum(grads * normal, axis=0, keepdims=True)
                grads = grads * gain
                grads = scale * (grads - normal * jnp.mean(grads * normal, axis=1, keepdims=True))
            out_ref[:, base : base + head_dim] = grads.astype(out_ref.dtype)


def front_back(raw, cosine, sine, gains, grad_queries, grad_kv, head_dim):
    rows, width = raw.shape
    groups = width // (4 * head_dim)
    block = min(256, rows)
    narrow = pl.BlockSpec((block, 2 * head_dim), lambda i: (i, 0))
    table = pl.BlockSpec((block, head_dim), lambda i: (i, 0))
    wide = pl.BlockSpec((block, width), lambda i: (i, 0))
    return pl.pallas_call(
        functools.partial(front_back_kernel, groups, head_dim),
        grid=(rows // block,),
        in_specs=[wide, table, table, pl.BlockSpec(gains.shape, lambda i: (0, 0))] + [narrow] * (2 * groups),
        out_specs=[wide, pl.BlockSpec((8, head_dim), lambda i: (0, 0))],
        out_shape=[
            jax.ShapeDtypeStruct((rows, width), jnp.bfloat16),
            jax.ShapeDtypeStruct((8, head_dim), jnp.float32),
        ],
        compiler_params=pltpu.CompilerParams(vmem_limit_bytes=32 * MIB),
        cost_estimate=pl.CostEstimate(flops=60 * rows * width, bytes_accessed=10 * rows * width, transcendentals=0),
    )(raw, cosine, sine, gains, *grad_queries, *grad_kv)


def last_product_kernel(grad_ref, weight_ref, hidden_ref, scale_ref, gain_ref, out_ref, dots_ref, gain_out_ref):
    part = matmul(grad_ref[...], weight_ref[...], NT)
    out_ref[0] = part.astype(out_ref.dtype)
    product = part * (hidden_ref[...] * scale_ref[...])
    gain_out_ref[...] = jnp.sum(product, axis=0, keepdims=True)
    dots = jnp.sum(product * gain_ref[...], axis=1, keepdims=True)

    @pl.when(pl.program_id(0) == 0)
    def _():
        dots_ref[...] = dots

    @pl.when(pl.program_id(0) > 0)
    def _():
        dots_ref[...] += dots


def last_product(grads, weight, hidden, scale, gain, pieces):
    rows, width = grads.shape
    depth = weight.shape[0]
    block = depth // pieces // 2
    return pl.pallas_call(
        last_product_kernel,
        grid=(depth // block,),
        in_specs=[
            pl.BlockSpec((rows, width), lambda i: (0, 0), pipeline_mode=pl.Buffered(1)),
            pl.BlockSpec((block, width), lambda i: (i, 0)),
            pl.BlockSpec((rows, block), lambda i: (0, i)),
            pl.BlockSpec((rows, 1), lambda i: (0, 0)),
            pl.BlockSpec((1, block), lambda i: (0, i)),
        ],
        out_specs=[
            pl.BlockSpec((1, rows, block), lambda i: (i // 2, 0, i % 2)),
            pl.BlockSpec((rows, 1), lambda i: (0, 0)),
            pl.BlockSpec((1, block), lambda i: (0, i)),
        ],
        out_shape=[
            jax.ShapeDtypeStruct((pieces, rows, depth // pieces), jnp.bfloat16),
            jax.ShapeDtypeStruct((rows, 1), jnp.float32),
            jax.ShapeDtypeStruct((1, depth), jnp.float32),
        ],
        compiler_params=pltpu.CompilerParams(vmem_limit_bytes=32 * MIB),
        cost_estimate=pl.CostEstimate(flops=4 * rows * depth * width, bytes_accessed=2 * depth * width, transcendentals=0),
    )(grads, weight, hidden, scale, gain)


def resid_kernel(sum_ref, hidden_ref, gain_ref, resid_ref, normed_ref, normed_t_ref, scale_ref):
    total = jnp.concatenate([sum_ref[at] for at in range(sum_ref.shape[0])], axis=1)
    resid = hidden_ref[...] + total.astype(jnp.float32)
    scale = lax.rsqrt(jnp.mean(resid * resid, axis=1, keepdims=True) + EPSILON)
    normed = resid * scale * gain_ref[...]
    resid_ref[...] = resid
    scale_ref[...] = scale
    normed_ref[...] = normed.astype(normed_ref.dtype)
    normed_t_ref[...] = jnp.transpose(normed).astype(normed_t_ref.dtype)


def add_and_norm(total, hidden, gain):
    pieces, rows, width = total.shape
    depth = pieces * width
    block = min(256, rows)
    wide = pl.BlockSpec((block, depth), lambda i: (i, 0))
    return pl.pallas_call(
        resid_kernel,
        grid=(rows // block,),
        in_specs=[
            pl.BlockSpec((pieces, block, width), lambda i: (0, i, 0)),
            wide,
            pl.BlockSpec((1, depth), lambda i: (0, 0)),
        ],
        out_specs=[
            wide,
            wide,
            pl.BlockSpec((depth, block), lambda i: (0, i)),
            pl.BlockSpec((block, 1), lambda i: (i, 0)),
        ],
        out_shape=[
            jax.ShapeDtypeStruct((rows, depth), jnp.float32),
            jax.ShapeDtypeStruct((rows, depth), jnp.bfloat16),
            jax.ShapeDtypeStruct((depth, rows), jnp.bfloat16),
            jax.ShapeDtypeStruct((rows, 1), jnp.float32),
        ],
        compiler_params=pltpu.CompilerParams(vmem_limit_bytes=40 * MIB),
        cost_estimate=pl.CostEstimate(flops=10 * rows * depth, bytes_accessed=18 * rows * depth, transcendentals=0),
    )(total, hidden, gain)


def resid_back_kernel(sum_ref, cot_ref, resid_ref, scale_ref, gain_ref, grad_ref, rounded_ref, gain_out_ref):
    grads = jnp.concatenate([sum_ref[at] for at in range(sum_ref.shape[0])], axis=1).astype(jnp.float32)
    scale = scale_ref[...]
    normal = resid_ref[...] * scale
    sums = jnp.sum(grads * normal, axis=0, keepdims=True)
    grads = grads * gain_ref[...]
    grads = scale * (grads - normal * jnp.mean(grads * normal, axis=1, keepdims=True))
    grads = cot_ref[...].astype(jnp.float32) + grads
    grad_ref[...] = grads
    rounded_ref[...] = grads.astype(rounded_ref.dtype)

    @pl.when(pl.program_id(0) == 0)
    def _():
        gain_out_ref[...] = sums

    @pl.when(pl.program_id(0) > 0)
    def _():
        gain_out_ref[...] += sums


def norm_and_add_back(total, cotangent, resid, scale, gain):
    pieces, rows, width = total.shape
    depth = pieces * width
    block = min(256, rows)
    wide = pl.BlockSpec((block, depth), lambda i: (i, 0))
    whole = pl.BlockSpec((1, depth), lambda i: (0, 0))
    return pl.pallas_call(
        resid_back_kernel,
        grid=(rows // block,),
        in_specs=[
            pl.BlockSpec((pieces, block, width), lambda i: (0, i, 0)),
            wide,
            wide,
            pl.BlockSpec((block, 1), lambda i: (i, 0)),
            whole,
        ],
        out_specs=[wide, wide, whole],
        out_shape=[
            jax.ShapeDtypeStruct((rows, depth), jnp.float32),
            jax.ShapeDtypeStruct((rows, depth), jnp.bfloat16),
            jax.ShapeDtypeStruct((1, depth), jnp.float32),
        ],
        compiler_params=pltpu.CompilerParams(vmem_limit_bytes=40 * MIB),
        cost_estimate=pl.CostEstimate(flops=10 * rows * depth, bytes_accessed=16 * rows * depth, transcendentals=0),
    )(total, cotangent, resid, scale, gain)


def step_of(rate, weight, moment, average, gradient, outs):
    moment = MOMENTUM * moment + gradient
    weight = weight - rate * (gradient + MOMENTUM * moment)
    average = EMA_DECAY * average + (1.0 - EMA_DECAY) * weight
    for out, value in zip(outs, (weight, moment, average, average)):
        out[...] = value.astype(out.dtype)


def mlp_step_kernel(rate, chunks, *refs):
    grads, held, outs = refs[:chunks], refs[chunks : chunks + 6], refs[chunks + 6 :]
    for chunk in range(chunks):

        @pl.when(pl.program_id(0) == chunk)
        def _():
            both = grads[chunk][:2].astype(jnp.float32)
            step_of(rate, *(ref[...] for ref in held[:3]), both, outs[:4])
            down = jnp.transpose(grads[chunk][2].astype(jnp.float32))
            step_of(rate, *(ref[...] for ref in held[3:]), down, outs[4:])


def mlp_step(rate, grads, gate_up, down):
    chunks = len(grads)
    kinds, depth, width = grads[0].shape
    gate_up_spec = pl.BlockSpec((2, depth, width), lambda i: (0, 0, i))
    down_spec = pl.BlockSpec((width, depth), lambda i: (i, 0))
    types = (jnp.float32,) * 3 + (jnp.bfloat16,)
    return pl.pallas_call(
        functools.partial(mlp_step_kernel, rate, chunks),
        grid=(chunks,),
        in_specs=[pl.BlockSpec((kinds, depth, width), lambda i: (0, 0, 0), pipeline_mode=pl.Buffered(1))] * chunks
        + [gate_up_spec] * 3
        + [down_spec] * 3,
        out_specs=[gate_up_spec] * 4 + [down_spec] * 4,
        out_shape=[jax.ShapeDtypeStruct(gate_up[0].shape, kind) for kind in types]
        + [jax.ShapeDtypeStruct(down[0].shape, kind) for kind in types],
        compiler_params=pltpu.CompilerParams(vmem_limit_bytes=40 * MIB),
        cost_estimate=pl.CostEstimate(flops=0, bytes_accessed=26 * chunks * kinds * depth * width, transcendentals=0),
    )(*grads, *gate_up, *down)


def turned_step_kernel(rate, grad_ref, *refs):
    step_of(rate, *(ref[...] for ref in refs[:3]), jnp.transpose(grad_ref[...].astype(jnp.float32)), refs[3:])


def turned_step(rate, grad_t, held):
    types = (jnp.float32,) * 3 + (jnp.bfloat16,)
    return pl.pallas_call(
        functools.partial(turned_step_kernel, rate),
        in_specs=[pl.BlockSpec(memory_space=pltpu.VMEM)] * 4,
        out_specs=[pl.BlockSpec(memory_space=pltpu.VMEM)] * 4,
        out_shape=[jax.ShapeDtypeStruct(held[0].shape, kind) for kind in types],
        compiler_params=pltpu.CompilerParams(vmem_limit_bytes=24 * MIB),
        cost_estimate=pl.CostEstimate(flops=0, bytes_accessed=28 * grad_t.size, transcendentals=0),
    )(grad_t, *held)


def rms_scale(values_in):
    return lax.rsqrt(jnp.mean(values_in * values_in, axis=-1, keepdims=True) + EPSILON)


def rope_tables(offsets, head_dim):
    half_dim = head_dim // 2
    frequency = 1.0 / ROPE_BASE ** (jnp.arange(half_dim, dtype=jnp.float32) * 2.0 / head_dim)
    angles = offsets.astype(jnp.float32)[:, None] * frequency[None, :]
    cosine = jnp.cos(angles)
    sine = jnp.sin(angles)
    return (jnp.concatenate([cosine, cosine], axis=-1), jnp.concatenate([sine, sine], axis=-1))


def nesterov(weight, moment, average, gradient, rate):
    new_moment = MOMENTUM * moment + gradient
    new_weight = weight - rate * (gradient + MOMENTUM * new_moment)
    new_average = EMA_DECAY * average + (1.0 - EMA_DECAY) * new_weight
    return (new_weight, new_moment, new_average, new_average.astype(jnp.bfloat16))


def dot(a, b, dims):
    return lax.dot_general(a, b, dims, preferred_element_type=jnp.float32)


def tie(*values):
    return lax.optimization_barrier(values)


def local(
    hidden_in,
    cotangent,
    doc_lengths,
    valid_mask,
    w_qkv,
    w_out,
    w_gate_up,
    w_down,
    norm_gains,
    m_qkv,
    m_out,
    m_gate_up,
    m_down,
    m_gains,
    a_qkv,
    a_out,
    a_gate_up,
    a_down,
    a_gains,
):
    row_count, model_dim = hidden_in.shape
    head_dim = (norm_gains.shape[0] - 2 * model_dim) // 2
    data_ways = lax.axis_size("dp")
    tensor_ways = lax.axis_size("tensor")
    tensor_at = lax.axis_index("tensor")
    tokens_all = row_count * data_ways
    width_cols = model_dim // tensor_ways
    col_begin = tensor_at * width_cols
    groups = w_qkv.shape[1] // (4 * head_dim)
    ff_local = w_down.shape[0]
    ff_chunk = ff_local // CHUNKS
    bf16 = jnp.bfloat16
    f32 = jnp.float32

    def columns_of(values_in):
        return lax.dynamic_slice_in_dim(values_in, col_begin, width_cols, values_in.ndim - 1)

    qkv_full = lax.all_gather(w_qkv.astype(bf16), "dp", axis=0, tiled=True)

    ends_at = jnp.cumsum(doc_lengths)
    starts_at = ends_at - doc_lengths
    place_begin = lax.axis_index("dp") * row_count
    places = place_begin + jnp.arange(row_count, dtype=jnp.int32)
    doc_ids = jnp.sum((places[:, None] >= ends_at[None, :]).astype(jnp.int32), axis=1)
    owned = doc_ids[:, None] == jnp.arange(doc_lengths.shape[0], dtype=jnp.int32)[None, :]
    doc_begin = jnp.sum(jnp.where(owned, starts_at[None, :], 0), axis=1)
    cosine, sine = rope_tables(places - doc_begin, head_dim)
    query_rows = min(512, row_count)
    blocks = row_count // query_rows
    bounds = jnp.stack(
        [
            place_begin + jnp.arange(blocks, dtype=jnp.int32) * query_rows,
            doc_begin[::query_rows],
            doc_begin[query_rows - 1 :: query_rows],
        ]
    ).astype(jnp.int32)
    begin_rows = doc_begin.astype(jnp.int32).reshape(blocks, 1, query_rows)

    gain_attn = norm_gains[:model_dim]
    gain_mlp = norm_gains[model_dim : 2 * model_dim]
    gain_query = norm_gains[2 * model_dim : 2 * model_dim + head_dim]
    gain_key = norm_gains[2 * model_dim + head_dim :]
    scale_one = rms_scale(hidden_in)
    normal_one = hidden_in * scale_one
    normed_one_b = (normal_one * gain_attn).astype(bf16)
    gains_two = jnp.stack([gain_query, gain_key])
    projected, queries, kv_local = front(normed_one_b, qkv_full, cosine, sine, gains_two, head_dim)
    kv_every = []
    for group in range(groups):
        value = kv_local[group]
        if group:
            value, kv_every[-1] = tie(value, kv_every[-1])
        kv_every.append(lax.all_gather(value, "dp", axis=0, tiled=True))

    down_t = w_down.T

    def chunk_shard(chunk):
        units = slice(chunk * ff_chunk, (chunk + 1) * ff_chunk)
        kinds = [w_gate_up[0, :, units], w_gate_up[1, :, units], down_t[:, units]]
        return jnp.stack(kinds + ([w_out.T] if chunk == 0 else [])).astype(bf16)

    def chunk_gather(shard):
        return lax.all_gather(shard, "dp", axis=0)

    mixed, totals, chunk_weights = [], [], []
    for group in range(groups):
        mixed_rows, total_rows = attend(
            bounds, queries[group], begin_rows, kv_every[group], head_dim, query_rows, min(1024, tokens_all)
        )
        if group == 0:
            shard, kv_every[-1], mixed_rows, cotangent_t = tie(
                chunk_shard(0), kv_every[-1], mixed_rows, cotangent.T
            )
            chunk_weights.append(chunk_gather(shard))
        mixed.append(mixed_rows)
        totals.append(total_rows)
    mixed_b = jnp.concatenate(mixed, axis=1)
    shard, chunk_weights[0], mixed_b = tie(chunk_shard(1), chunk_weights[0], mixed_b)
    chunk_weights.append(chunk_gather(shard))
    out_full_t = chunk_weights[0][:, 3].reshape(model_dim, w_out.shape[0])
    attn_part = back_product([(mixed_b,)], chunk_weights[:1], 3, tensor_ways)
    attn_sum = tensor_sum(attn_part, 0)
    shard, chunk_weights[1], attn_sum = tie(chunk_shard(2), chunk_weights[1], attn_sum)
    chunk_weights.append(chunk_gather(shard))
    resid_one, normed_two_b, normed_two_t, scale_two = add_and_norm(attn_sum, hidden_in, gain_mlp[None])

    weight_grads, hiddens, back_pairs = [], [], []
    for chunk in range(CHUNKS):
        hidden_b, gate_grad, up_grad, weight_grad = mlp_chunk(
            normed_two_b, cotangent, normed_two_t, cotangent_t, chunk_weights[chunk]
        )
        hiddens.append((hidden_b,))
        back_pairs.append((gate_grad, up_grad))
        weight_grads.append(lax.psum_scatter(weight_grad, "dp", scatter_dimension=0))

    part_two = back_product(back_pairs, chunk_weights, 0, tensor_ways)
    mlp_part = back_product(hiddens, chunk_weights, 2, tensor_ways)
    part_two, mlp_part, weight_grads[0] = tie(part_two, mlp_part, weight_grads[0])
    part_two_sum = tensor_sum(part_two, 1)
    grad_resid, grad_attn_b, gain_mlp_part = norm_and_add_back(
        part_two_sum, cotangent, resid_one, scale_two, gain_mlp[None]
    )
    grad_mixed_b = dot(grad_attn_b, out_full_t, NN).astype(bf16)

    grad_out_t = dot(grad_attn_b, mixed_b, TN).astype(bf16)
    grad_queries, kv_sums = [], []
    for group in range(groups):
        grad_rows = grad_mixed_b[:, group * 2 * head_dim : (group + 1) * 2 * head_dim]
        grad_rows, weight_grads[group + 1] = tie(grad_rows, weight_grads[group + 1])
        grad_query, kv_sum = attend_back(
            bounds,
            queries[group],
            grad_rows,
            mixed[group],
            totals[group],
            begin_rows,
            kv_every[group],
            head_dim,
            query_rows,
            min(512, tokens_all),
        )
        grad_queries.append(grad_query)
        kv_sums.append(kv_sum)
    grad_out_t, weight_grads[groups] = tie(grad_out_t, weight_grads[groups])
    out_grad = lax.psum_scatter(grad_out_t, "dp", scatter_dimension=0, tiled=True)
    kv_sums[0], out_grad = tie(kv_sums[0], out_grad)
    kv_grads = [lax.psum_scatter(kv_sum, "dp", scatter_dimension=0, tiled=True) for kv_sum in kv_sums]
    mlp_part, grad_queries[-1] = tie(mlp_part, grad_queries[-1])
    rate_matrix = LR_MATRIX / math.sqrt(tokens_all)
    mlp_sum = tensor_sum(mlp_part, 2, False)
    updates = (
        *turned_step(rate_matrix, out_grad, (w_out, m_out, a_out)),
        *mlp_step(rate_matrix, weight_grads, (w_gate_up, m_gate_up, a_gate_up), (w_down, m_down, a_down)),
    )
    mlp_cols = mlp_sum.astype(f32)
    resid_cols = columns_of(resid_one)
    attn_cols = lax.dynamic_index_in_dim(attn_sum, tensor_at, 0, False).astype(f32)
    mask_rows = valid_mask.astype(f32)[:, None]
    stats_part = [
        jnp.sum(mask_rows * columns * columns) for columns in (columns_of(hidden_in), attn_cols, mlp_cols)
    ]
    stats_part.append(jnp.where(tensor_at == 0, jnp.sum(valid_mask.astype(f32)), 0.0))
    gain_mlp_wide = lax.dynamic_update_slice_in_dim(
        jnp.zeros((model_dim,), f32), columns_of(gain_mlp_part[0]), col_begin, 0
    )
    mixed_cols, gain_mlp_wide, stats_part, kv_grads[-1], updates = tie(
        resid_cols + mlp_cols, gain_mlp_wide, jnp.stack(stats_part), kv_grads[-1], updates
    )
    grad_projected_b, gains_found = front_back(
        projected, cosine, sine, gains_two, grad_queries, kv_grads, head_dim
    )
    grad_qkv = dot(normed_one_b, grad_projected_b, TN).astype(bf16)
    qkv_shard = lax.psum_scatter(grad_qkv, "dp", scatter_dimension=0, tiled=True).astype(f32)
    part_one, dots_part, gain_attn_part = last_product(
        grad_projected_b, qkv_full, hidden_in, scale_one, gain_attn[None], tensor_ways
    )

    gains_part = jnp.concatenate(
        [gain_attn_part[0], gain_mlp_wide, gains_found[0], gains_found[1], stats_part]
    )
    gains_count = gains_part.shape[0]
    gains_rows = -(-gains_count // 1024) * 8
    gains_part = jnp.pad(gains_part, (0, gains_rows * 128 - gains_count)).reshape(gains_rows, 128)
    grad_one_cols, row_dots, gains_sum = last_sum(
        part_one, dots_part.reshape(row_count // 128, 128), gains_part, data_ways, 3
    )
    gains_sum = gains_sum.reshape(-1)[:gains_count]
    grad_cols = columns_of(grad_resid) + scale_one * (
        grad_one_cols.astype(f32) * columns_of(gain_attn)
        - columns_of(normal_one) * (row_dots.reshape(row_count, 1) / model_dim)
    )
    grad_gains = gains_sum[: norm_gains.shape[0]]
    stats_sum = gains_sum[norm_gains.shape[0] :]
    branch_rms = jnp.sqrt(stats_sum[:3] / (stats_sum[3] * model_dim))

    rate_gain = LR_GAIN / math.sqrt(tokens_all)
    return (
        mixed_cols,
        grad_cols,
        branch_rms,
        *nesterov(w_qkv, m_qkv, a_qkv, qkv_shard, rate_matrix),
        *updates,
        *nesterov(norm_gains, m_gains, a_gains, grad_gains, rate_gain),
    )


def solution(mesh):
    rows = P("dp", None)
    spread = P("dp", "tensor")
    turned = P("tensor", "dp")
    stacked = P(None, "dp", "tensor")
    matrices = (spread, turned, stacked, turned, P())
    in_specs = (rows, rows, P(), P("dp"), *matrices, *matrices, *matrices)
    out_specs = (spread, spread, P(), *(spec for spec in matrices for _ in range(4)))
    return jax.shard_map(local, mesh=mesh, in_specs=in_specs, out_specs=out_specs, check_vma=False)
```

```python
import functools, math
import jax, jax.numpy as jnp
from jax import lax
from jax.experimental import pallas as pl
from jax.experimental.pallas import tpu as pltpu
NT = (((1,), (1,)), ((), ()))
NN = (((1,), (0,)), ((), ()))
TN = (((0,), (0,)), ((), ()))
NEG_FILL = -1e30
LOG2E = math.log2(math.e)
MIB = 1024 * 1024

def matmul(a, b, dims):
    return lax.dot_general(a, b, dims, preferred_element_type=jnp.float32)

def row_of(column):
    return jnp.transpose(jnp.broadcast_to(column, (column.shape[0], 128)))[:1]

def attend_kernel(head_dim, key_rows, bound_ref, query_ref, begin_ref, kv_ref, out_ref, total_ref, q_two, accum):
    rows = query_ref.shape[0]
    block = pl.program_id(0)
    first = bound_ref[0, block]
    begin_first = bound_ref[1, block]
    begin_last = bound_ref[2, block]
    scale = LOG2E * head_dim**-0.5
    q_two[:rows] = query_ref[:, :head_dim]
    q_two[rows:] = query_ref[:, head_dim:]
    places = first + lax.broadcasted_iota(jnp.int32, (1, rows), 1)
    places = jnp.concatenate([places, places], axis=1)
    begins = jnp.concatenate([begin_ref[0], begin_ref[0]], axis=1)

    def step(masked, index, carry):
        top, total = carry
        key_begin = pl.multiple_of(index * key_rows, key_rows)
        keys = kv_ref[pl.ds(key_begin, key_rows), :head_dim]
        values = kv_ref[pl.ds(key_begin, key_rows), head_dim:]
        raw = matmul(keys, q_two[...], NT) * scale
        if masked:
            key_places = key_begin + lax.broadcasted_iota(jnp.int32, (key_rows, 1), 0)
            allowed = (key_places >= begins) & (key_places <= places)
            raw = jnp.where(allowed, raw, NEG_FILL)
        new_top = jnp.maximum(top, jnp.max(raw, axis=0, keepdims=True))
        probs = jnp.exp2(raw - new_top)
        fade = jnp.exp2(top - new_top)
        total = total * fade + jnp.sum(probs, axis=0, keepdims=True)
        accum[...] = accum[...] * fade + matmul(values, probs.astype(jnp.bfloat16), TN)
        return (new_top, total)

    def either(index, carry):
        key_begin = index * key_rows
        plain = (key_begin >= begin_last) & (key_begin + key_rows - 1 <= first)
        return lax.cond(
            plain, functools.partial(step, False, index), functools.partial(step, True, index), carry
        )

    accum[...] = jnp.zeros_like(accum)
    start = (
        jnp.full((1, 2 * rows), NEG_FILL, jnp.float32),
        jnp.zeros((1, 2 * rows), jnp.float32),
    )
    low = begin_first // key_rows
    high = (first + rows - 1) // key_rows + 1
    top, total = lax.fori_loop(low, high, either, start)
    out = jnp.transpose(accum[...] / total)
    out_ref[:, :head_dim] = out[:rows].astype(out_ref.dtype)
    out_ref[:, head_dim:] = out[rows:].astype(out_ref.dtype)
    total_ref[0] = top + jnp.log2(total)

def attend(bounds, queries, begins, kv_all, group, head_dim, query_rows, key_rows):
    rows = queries.shape[0]
    blocks = rows // query_rows
    return pl.pallas_call(
        functools.partial(attend_kernel, head_dim, key_rows),
        out_shape=(jax.ShapeDtypeStruct(queries.shape, jnp.bfloat16), jax.ShapeDtypeStruct((blocks, 1, 2 * query_rows), jnp.float32)),
        grid_spec=pltpu.PrefetchScalarGridSpec(
            num_scalar_prefetch=1,
            grid=(blocks,),
            in_specs=[
                pl.BlockSpec((query_rows, 2 * head_dim), lambda i, *_: (i, 0)),
                pl.BlockSpec((1, 1, query_rows), lambda i, *_: (i, 0, 0)),
                pl.BlockSpec((kv_all.shape[0], 2 * head_dim), lambda i, *_: (0, group)),
            ],
            out_specs=[
                pl.BlockSpec((query_rows, 2 * head_dim), lambda i, *_: (i, 0)),
                pl.BlockSpec((1, 1, 2 * query_rows), lambda i, *_: (i, 0, 0)),
            ],
            scratch_shapes=[pltpu.VMEM((2 * query_rows, head_dim), jnp.bfloat16), pltpu.VMEM((head_dim, 2 * query_rows), jnp.float32)],
        ),
        compiler_params=pltpu.CompilerParams(vmem_limit_bytes=48 * MIB),
        cost_estimate=pl.CostEstimate(flops=8 * rows * kv_all.shape[0] * head_dim, bytes_accessed=2 * kv_all.size, transcendentals=2 * rows * kv_all.shape[0]),
    )(bounds, queries, begins, kv_all)

def attend_back_kernel(head_dim, key_rows, bound_ref, query_ref, grad_ref, out_ref, total_ref, begin_ref, kv_ref, grad_q_ref, grad_kv_ref, q_two, g_two, dq_two, kv_sum):
    rows = query_ref.shape[0]
    block = pl.program_id(0)
    first = bound_ref[0, block]
    begin_first = bound_ref[1, block]
    begin_last = bound_ref[2, block]
    unit = head_dim**-0.5
    scale = LOG2E * unit

    @pl.when(block == 0)
    def _():
        kv_sum[...] = jnp.zeros_like(kv_sum)

    for half in range(2):
        part = slice(half * rows, (half + 1) * rows)
        cols = slice(half * head_dim, (half + 1) * head_dim)
        q_two[part] = query_ref[:, cols]
        g_two[part] = grad_ref[:, cols]
    dq_two[...] = jnp.zeros_like(dq_two)
    product = grad_ref[...].astype(jnp.float32) * out_ref[...].astype(jnp.float32)
    delta = jnp.concatenate(
        [
            row_of(jnp.sum(product[:, :head_dim], axis=1, keepdims=True)),
            row_of(jnp.sum(product[:, head_dim:], axis=1, keepdims=True)),
        ],
        axis=1,
    )
    totals = total_ref[0]
    places = first + lax.broadcasted_iota(jnp.int32, (1, rows), 1)
    places = jnp.concatenate([places, places], axis=1)
    begins = jnp.concatenate([begin_ref[0], begin_ref[0]], axis=1)

    def step(masked, index):
        key_begin = pl.multiple_of(index * key_rows, key_rows)
        place = pl.ds(key_begin, key_rows)
        keys = kv_ref[place, :head_dim]
        values = kv_ref[place, head_dim:]
        raw = matmul(keys, q_two[...], NT)
        probs = jnp.exp2(raw * scale - totals)
        if masked:
            key_places = key_begin + lax.broadcasted_iota(jnp.int32, (key_rows, 1), 0)
            allowed = (key_places >= begins) & (key_places <= places)
            probs = jnp.where(allowed, probs, 0.0)
        kv_sum[place, head_dim:] += matmul(probs.astype(jnp.bfloat16), g_two[...], NN)
        grad_probs = matmul(values, g_two[...], NT)
        grad_scores = (probs * ((grad_probs - delta) * unit)).astype(jnp.bfloat16)
        kv_sum[place, :head_dim] += matmul(grad_scores, q_two[...], NN)
        dq_two[...] += matmul(grad_scores, keys, TN)

    def either(index, carry):
        key_begin = index * key_rows
        plain = (key_begin >= begin_last) & (key_begin + key_rows - 1 <= first)

        @pl.when(plain)
        def _():
            step(False, index)

        @pl.when(jnp.logical_not(plain))
        def _():
            step(True, index)

        return carry

    low = begin_first // key_rows
    high = (first + rows - 1) // key_rows + 1
    lax.fori_loop(low, high, either, 0)
    grad_q_ref[:, :head_dim] = dq_two[:rows].astype(grad_q_ref.dtype)
    grad_q_ref[:, head_dim:] = dq_two[rows:].astype(grad_q_ref.dtype)

    @pl.when(block == pl.num_programs(0) - 1)
    def _():
        grad_kv_ref[...] = kv_sum[...].astype(grad_kv_ref.dtype)

def attend_back(bounds, queries, grads, outs, totals, begin_rows, kv_all, group, head_dim, query_rows, key_rows):
    rows = queries.shape[0]
    blocks = rows // query_rows
    wide = pl.BlockSpec((query_rows, 2 * head_dim), lambda i, *_: (i, 0))
    kv_shape = (kv_all.shape[0], 2 * head_dim)
    whole = pl.BlockSpec(kv_shape, lambda i, *_: (0, 0))
    return pl.pallas_call(
        functools.partial(attend_back_kernel, head_dim, key_rows),
        out_shape=(jax.ShapeDtypeStruct(queries.shape, jnp.float32), jax.ShapeDtypeStruct(kv_shape, jnp.bfloat16)),
        grid_spec=pltpu.PrefetchScalarGridSpec(
            num_scalar_prefetch=1,
            grid=(blocks,),
            in_specs=[wide, wide, wide,
                pl.BlockSpec((1, 1, 2 * query_rows), lambda i, *_: (i, 0, 0)),
                pl.BlockSpec((1, 1, query_rows), lambda i, *_: (i, 0, 0)),
                pl.BlockSpec(kv_shape, lambda i, *_: (0, group))],
            out_specs=[wide, whole],
            scratch_shapes=[pltpu.VMEM((2 * query_rows, head_dim), jnp.bfloat16)] * 2
            + [pltpu.VMEM((2 * query_rows, head_dim), jnp.float32), pltpu.VMEM(kv_shape, jnp.float32)],
        ),
        compiler_params=pltpu.CompilerParams(vmem_limit_bytes=56 * MIB),
        cost_estimate=pl.CostEstimate(flops=20 * rows * kv_all.shape[0] * head_dim, bytes_accessed=2 * kv_all.size, transcendentals=2 * rows * kv_all.shape[0]),
    )(bounds, queries, grads, outs, totals, begin_rows, kv_all)


from jax.sharding import PartitionSpec as P

EPSILON = 1e-06
ROPE_BASE = 1000000.0
MOMENTUM = 0.5
EMA_DECAY = 0.5
LR_MATRIX = 0.08
LR_GAIN = 0.5
FF_BLOCK = 256
CHUNK_ENDS = (0, 1, 3)


def mlp_kernel(normed_ref, cot_ref, normed_t_ref, cot_t_ref, weight_ref, hidden_ref, gate_grad_ref, up_grad_ref, grads_ref, wide):
    ways, kinds, shard, _ = weight_ref.shape
    rows = normed_ref.shape[0]
    row_tile = min(512, rows)

    for at in range(ways):
        wide[:, at * shard : (at + 1) * shard, :] = weight_ref[at]

    @pl.loop(0, rows // row_tile)
    def _(tile):
        place = pl.ds(pl.multiple_of(tile * row_tile, row_tile), row_tile)
        x = normed_ref[place, :]
        gate = matmul(x, wide[0], NN)
        up = matmul(x, wide[1], NN)
        grad_hidden = matmul(cot_ref[place, :], wide[2], NN)
        sigmoid = 1.0 / (1.0 + jnp.exp(-gate))
        silu = gate * sigmoid
        hidden_ref[place, :] = (silu * up).astype(hidden_ref.dtype)
        gate_grad_ref[place, :] = (
            grad_hidden * up * (sigmoid * (1.0 + gate * (1.0 - sigmoid)))
        ).astype(gate_grad_ref.dtype)
        up_grad_ref[place, :] = (grad_hidden * silu).astype(up_grad_ref.dtype)

    for at in range(ways):
        place = slice(at * shard, (at + 1) * shard)
        left = normed_t_ref[place, :]
        grads_ref[at, 0] = matmul(left, gate_grad_ref[...], NN).astype(grads_ref.dtype)
        grads_ref[at, 1] = matmul(left, up_grad_ref[...], NN).astype(grads_ref.dtype)
        grads_ref[at, 2] = matmul(cot_t_ref[place, :], hidden_ref[...], NN).astype(grads_ref.dtype)


def mlp_chunk(normed, cotangent, normed_t, cotangent_t, weights):
    ways, _, shard, width = weights.shape
    rows, depth = normed.shape
    block = min(FF_BLOCK, width)

    def held(array):
        return pl.BlockSpec(array.shape, lambda i: (0, 0), pipeline_mode=pl.Buffered(1))

    weight_spec = pl.BlockSpec((ways, 3, shard, block), lambda i: (0, 0, 0, i))
    row_spec = pl.BlockSpec((rows, block), lambda i: (0, i))
    row_shape = jax.ShapeDtypeStruct((rows, width), jnp.bfloat16)
    return pl.pallas_call(
        mlp_kernel,
        grid=(width // block,),
        in_specs=[held(normed), held(cotangent), held(normed_t), held(cotangent_t), weight_spec],
        out_specs=[row_spec, row_spec, row_spec, weight_spec],
        out_shape=(row_shape, row_shape, row_shape, jax.ShapeDtypeStruct((ways, 3, shard, width), jnp.bfloat16)),
        scratch_shapes=[pltpu.VMEM((3, depth, block), jnp.bfloat16)],
        compiler_params=pltpu.CompilerParams(vmem_limit_bytes=56 * MIB),
        cost_estimate=pl.CostEstimate(flops=24 * rows * depth * width, bytes_accessed=12 * depth * width, transcendentals=rows * width),
    )(normed, cotangent, normed_t, cotangent_t, weights)


def back_product_kernel(kinds, *refs):
    out_ref = refs[-1]
    total = None
    chunks = (len(refs) - 1) // (kinds + 1)
    for chunk in range(chunks):
        weight_ref = refs[chunk * (kinds + 1) + kinds]
        for kind in range(kinds):
            part = matmul(refs[chunk * (kinds + 1) + kind][...], weight_ref[0, kind], NT)
            total = part if total is None else total + part
    out_ref[0] = total.astype(out_ref.dtype)


def back_product(groups_of, weights, kind_begin, pieces):
    kinds = len(groups_of[0])
    ways, _, shard, width = weights[0].shape
    rows = groups_of[0][0].shape[0]
    per_piece = ways // pieces
    args, specs = [], []
    for lefts, weight in zip(groups_of, weights):
        for left in lefts:
            args.append(left)
            specs.append(pl.BlockSpec(left.shape, lambda i: (0, 0), pipeline_mode=pl.Buffered(1)))
        args.append(weight)
        specs.append(pl.BlockSpec((1, kinds, shard, weight.shape[3]), lambda i: (i, kind_begin // kinds, 0, 0)))
    return pl.pallas_call(
        functools.partial(back_product_kernel, kinds),
        grid=(ways,),
        in_specs=specs,
        out_specs=pl.BlockSpec((1, rows, shard), lambda i: (i // per_piece, 0, i % per_piece)),
        out_shape=jax.ShapeDtypeStruct((pieces, rows, per_piece * shard), jnp.bfloat16),
        compiler_params=pltpu.CompilerParams(vmem_limit_bytes=56 * MIB),
        cost_estimate=pl.CostEstimate(flops=2 * len(weights) * kinds * rows * width * ways * shard, bytes_accessed=2 * len(weights) * kinds * width * ways * shard, transcendentals=0),
    )(*args)


MESH = pl.DeviceIdType.MESH
SUM_BLOCKS = 4


def flip(index, bit):
    unit = 1 << bit
    return index + unit - 2 * unit * ((index // unit) % 2)


def picks(index, fixed, free):
    base = 0
    for bit in fixed:
        unit = 1 << bit
        base = base + unit * ((index // unit) % 2)
    found = []
    for choice in range(1 << len(free)):
        offset = sum((1 << bit) for at, bit in enumerate(free) if (choice >> at) & 1)
        found.append(base + offset)
    return found


def tensor_sum_kernel(bits, whole, part_ref, out_ref, sums, landed, send_sem, recv_sem, send_out, recv_out):
    row_at = lax.axis_index("dp")
    me = lax.axis_index("tensor")
    barrier = pltpu.get_barrier_semaphore()
    for bit in range(bits):
        pl.semaphore_signal(barrier, inc=1, device_id=(row_at, flip(me, bit)), device_id_type=MESH)
    pl.semaphore_wait(barrier, bits)
    tensor_sum_steps(bits, whole, part_ref, out_ref, sums, landed, send_sem, recv_sem, send_out, recv_out)


def tensor_sum_steps(bits, whole, part_ref, out_ref, sums, landed, send_sem, recv_sem, send_out, recv_out):
    row_at = lax.axis_index("dp")
    me = lax.axis_index("tensor")
    rows = part_ref.shape[1] // SUM_BLOCKS
    orders = [list(range(bits)) if b % 2 == 0 else list(range(bits))[::-1] for b in range(SUM_BLOCKS)]

    def place(block):
        return pl.ds(block * rows, rows)

    def scatter(block, step):
        order = orders[block]
        bit = order[step]
        there = flip(me, bit)
        free = order[step + 1 :]
        source = part_ref if step == 0 else sums
        base = (1 << bits) - (1 << (bits - step))
        copies = []
        for at, piece in enumerate(picks(there, order[: step + 1], free)):
            slot = base + at
            copies.append(
                pltpu.make_async_remote_copy(
                    src_ref=source.at[piece, place(block)],
                    dst_ref=landed.at[slot, place(block)],
                    send_sem=send_sem.at[slot, block],
                    recv_sem=recv_sem.at[slot, block],
                    device_id=(row_at, there),
                    device_id_type=MESH,
                )
            )
        return copies

    def gather(block, step):
        order = orders[block][::-1]
        bit = order[step]
        there = flip(me, bit)
        base = (1 << step) - 1
        copies = []
        for at, piece in enumerate(picks(me, order[step:], order[:step])):
            slot = base + at
            copies.append(
                pltpu.make_async_remote_copy(
                    src_ref=out_ref.at[piece, place(block)],
                    dst_ref=out_ref.at[piece, place(block)],
                    send_sem=send_out.at[slot, block],
                    recv_sem=recv_out.at[slot, block],
                    device_id=(row_at, there),
                    device_id_type=MESH,
                )
            )
        return copies

    every = []
    flying = []
    for block in range(SUM_BLOCKS):
        copies = scatter(block, 0)
        for copy in copies:
            copy.start()
        flying.append(copies)
    for step in range(bits):
        for block in range(SUM_BLOCKS):
            order = orders[block]
            base = (1 << bits) - (1 << (bits - step))
            for copy in flying[block]:
                copy.wait_recv()
            every += flying[block]
            source = part_ref if step == 0 else sums
            last = step == bits - 1
            for at, piece in enumerate(picks(me, order[: step + 1], order[step + 1 :])):
                total = source[piece, place(block)].astype(jnp.float32) + landed[base + at, place(block)].astype(jnp.float32)
                if not last:
                    sums[piece, place(block)] = total.astype(sums.dtype)
                elif whole:
                    out_ref[piece, place(block)] = total.astype(out_ref.dtype)
                else:
                    out_ref[place(block)] = total.astype(out_ref.dtype)
            if not last:
                flying[block] = scatter(block, step + 1)
            elif whole:
                flying[block] = gather(block, 0)
            if not last or whole:
                for copy in flying[block]:
                    copy.start()
    if whole:
        for step in range(bits):
            for block in range(SUM_BLOCKS):
                for copy in flying[block]:
                    copy.wait_recv()
                every += flying[block]
                if step < bits - 1:
                    flying[block] = gather(block, step + 1)
                    for copy in flying[block]:
                        copy.start()
    for copy in every:
        copy.wait_send()


def tensor_sum(part, collective_id, whole=True):
    ways, rows, width = part.shape
    bits = ways.bit_length() - 1
    return pl.pallas_call(
        functools.partial(tensor_sum_kernel, bits, whole),
        out_shape=jax.ShapeDtypeStruct(part.shape if whole else part.shape[1:], part.dtype),
        in_specs=[pl.BlockSpec(memory_space=pltpu.VMEM)],
        out_specs=pl.BlockSpec(memory_space=pltpu.VMEM),
        scratch_shapes=[
            pltpu.VMEM(part.shape, part.dtype),
            pltpu.VMEM((ways - 1, rows, width), part.dtype),
            *[pltpu.SemaphoreType.DMA((ways - 1, SUM_BLOCKS))] * 4,
        ],
        compiler_params=pltpu.CompilerParams(
            collective_id=collective_id, has_side_effects=True, vmem_limit_bytes=32 * MIB
        ),
        cost_estimate=pl.CostEstimate(flops=0, bytes_accessed=(256 if whole else 128) * MIB, transcendentals=0),
    )(part)


def spread_kernel(source, slots, me, ways, place, send_sem, recv_sem):
    copies = []
    for step in range(1, ways):
        there = lax.rem(me + step, ways)
        copies.append(
            pltpu.make_async_remote_copy(
                src_ref=source,
                dst_ref=slots.at[me],
                send_sem=send_sem.at[step - 1],
                recv_sem=recv_sem.at[step - 1],
                device_id=place(there),
                device_id_type=MESH,
            )
        )
    for copy in copies:
        copy.start()
    return copies


def total_of(slots, ways):
    total = slots[0]
    for at in range(1, ways):
        total = total + slots[at]
    return total


def last_sum_kernel(
    bits, ways, part_ref, dots_ref, gains_ref, out_ref, dots_out_ref, gains_out_ref,
    sums, landed, dots_land, gains_land, gains_far, gains_mid, send_sem, recv_sem, dots_send, dots_recv,
    near_send, near_recv, far_send, far_recv,
):
    row_at = lax.axis_index("dp")
    me = lax.axis_index("tensor")
    pieces = 1 << bits

    def beside(there):
        return (row_at, there)

    def along(there):
        return (there, me)

    barrier = pltpu.get_barrier_semaphore()
    for step in range(1, pieces):
        pl.semaphore_signal(barrier, inc=1, device_id=beside(lax.rem(me + step, pieces)), device_id_type=MESH)
    for step in range(1, ways):
        pl.semaphore_signal(barrier, inc=1, device_id=along(lax.rem(row_at + step, ways)), device_id_type=MESH)
    pl.semaphore_wait(barrier, pieces + ways - 2)
    gains_land[me] = gains_ref[...]
    dots_land[me] = dots_ref[...]
    near = spread_kernel(gains_ref, gains_land, me, pieces, beside, near_send, near_recv)
    dots = spread_kernel(dots_ref, dots_land, me, pieces, beside, dots_send, dots_recv)
    for copy in near:
        copy.wait()
    gains_mid[...] = total_of(gains_land, pieces)
    gains_far[row_at] = gains_mid[...]
    far = spread_kernel(gains_mid, gains_far, row_at, ways, along, far_send, far_recv)
    tensor_sum_steps(bits, False, part_ref, out_ref, sums, landed, send_sem, recv_sem, None, None)
    for copy in dots:
        copy.wait()
    dots_out_ref[...] = total_of(dots_land, pieces)
    for copy in far:
        copy.wait()
    gains_out_ref[...] = total_of(gains_far, ways)


def last_sum(part, dots, gains, data_ways, collective_id):
    pieces, rows, width = part.shape
    bits = pieces.bit_length() - 1
    near = pltpu.SemaphoreType.DMA((pieces - 1,))
    far = pltpu.SemaphoreType.DMA((data_ways - 1,))
    return pl.pallas_call(
        functools.partial(last_sum_kernel, bits, data_ways),
        out_shape=(
            jax.ShapeDtypeStruct(part.shape[1:], part.dtype),
            jax.ShapeDtypeStruct(dots.shape, dots.dtype),
            jax.ShapeDtypeStruct(gains.shape, gains.dtype),
        ),
        in_specs=[pl.BlockSpec(memory_space=pltpu.VMEM)] * 3,
        out_specs=[pl.BlockSpec(memory_space=pltpu.VMEM)] * 3,
        scratch_shapes=[
            pltpu.VMEM(part.shape, part.dtype),
            pltpu.VMEM((pieces - 1, rows, width), part.dtype),
            pltpu.VMEM((pieces, *dots.shape), dots.dtype),
            pltpu.VMEM((pieces, *gains.shape), gains.dtype),
            pltpu.VMEM((data_ways, *gains.shape), gains.dtype),
            pltpu.VMEM(gains.shape, gains.dtype),
            *[pltpu.SemaphoreType.DMA((pieces - 1, SUM_BLOCKS))] * 2,
            near, near, near, near, far, far,
        ],
        compiler_params=pltpu.CompilerParams(
            collective_id=collective_id, has_side_effects=True, vmem_limit_bytes=32 * MIB
        ),
        cost_estimate=pl.CostEstimate(flops=0, bytes_accessed=128 * MIB, transcendentals=0),
    )(part, dots, gains)


def turned_by(values, signs):
    return pltpu.roll(values, values.shape[1] // 2, 1) * signs


def half_signs(head_dim, first):
    lanes = lax.broadcasted_iota(jnp.int32, (1, head_dim), 1)
    return jnp.where(lanes < head_dim // 2, first, -first)


def front_kernel(groups, head_dim, normed_ref, weight_ref, cos_ref, sin_ref, gains_ref, raw_ref, *outs):
    raw_ref[...] = matmul(normed_ref[...], weight_ref[...], NN)
    cosine = cos_ref[...]
    sine = sin_ref[...] * half_signs(head_dim, -1.0)
    for group in range(groups):
        for at in range(4):
            base = (group * 4 + at) * head_dim
            raw = raw_ref[:, base : base + head_dim]
            if at < 3:
                gain = gains_ref[at // 2 : at // 2 + 1]
                scale = lax.rsqrt(jnp.mean(raw * raw, axis=1, keepdims=True) + EPSILON)
                raw = raw * scale * gain
                raw = raw * cosine + turned_by(raw, sine)
            out = outs[group] if at < 2 else outs[groups]
            place = at % 2 * head_dim + (0 if at < 2 else group * 2 * head_dim)
            out[:, place : place + head_dim] = raw.astype(out.dtype)


def front(normed, weight, width, cosine, sine, gains, head_dim):
    rows, depth = normed.shape
    groups = width // (4 * head_dim)
    block = min(256, rows)
    narrow = pl.BlockSpec((block, 2 * head_dim), lambda i: (i, 0))
    table = pl.BlockSpec((block, head_dim), lambda i: (i, 0))
    found = pl.pallas_call(
        functools.partial(front_kernel, groups, head_dim),
        grid=(rows // block,),
        in_specs=[
            pl.BlockSpec((block, depth), lambda i: (i, 0)),
            pl.BlockSpec((depth, width), lambda i: (0, 0), pipeline_mode=pl.Buffered(1)),
            table,
            table,
            pl.BlockSpec(gains.shape, lambda i: (0, 0)),
        ],
        out_specs=[pl.BlockSpec((block, width), lambda i: (i, 0))]
        + [narrow] * groups
        + [pl.BlockSpec((block, groups * 2 * head_dim), lambda i: (i, 0))],
        out_shape=[jax.ShapeDtypeStruct((rows, width), jnp.float32)]
        + [jax.ShapeDtypeStruct((rows, 2 * head_dim), jnp.bfloat16)] * groups
        + [jax.ShapeDtypeStruct((rows, groups * 2 * head_dim), jnp.bfloat16)],
        compiler_params=pltpu.CompilerParams(vmem_limit_bytes=32 * MIB),
        cost_estimate=pl.CostEstimate(flops=4 * rows * depth * width, bytes_accessed=2 * depth * width, transcendentals=0),
    )(normed, weight, cosine, sine, gains)
    return found[0], found[1 : 1 + groups], found[1 + groups]


def front_back_kernel(groups, head_dim, raw_ref, cos_ref, sin_ref, gains_ref, *refs):
    queries, keys = refs[:groups], refs[groups : 2 * groups]
    out_ref, sums_ref = refs[2 * groups :]

    @pl.when(pl.program_id(0) == 0)
    def _():
        sums_ref[...] = jnp.zeros_like(sums_ref)

    cosine = cos_ref[...]
    sine = sin_ref[...] * half_signs(head_dim, 1.0)
    for group in range(groups):
        for at in range(4):
            base = (group * 4 + at) * head_dim
            source = queries[group] if at < 2 else keys[group]
            grads = source[:, at % 2 * head_dim : (at % 2 + 1) * head_dim].astype(jnp.float32)
            if at < 3:
                gain = gains_ref[at // 2 : at // 2 + 1]
                raw = raw_ref[:, base : base + head_dim]
                scale = lax.rsqrt(jnp.mean(raw * raw, axis=1, keepdims=True) + EPSILON)
                normal = raw * scale
                grads = grads * cosine + turned_by(grads, sine)
                sums_ref[at // 2 : at // 2 + 1] += jnp.sum(grads * normal, axis=0, keepdims=True)
                grads = grads * gain
                grads = scale * (grads - normal * jnp.mean(grads * normal, axis=1, keepdims=True))
            out_ref[:, base : base + head_dim] = grads.astype(out_ref.dtype)


def front_back(raw, cosine, sine, gains, grad_queries, grad_kv, head_dim):
    rows, width = raw.shape
    groups = width // (4 * head_dim)
    block = min(256, rows)
    narrow = pl.BlockSpec((block, 2 * head_dim), lambda i: (i, 0))
    table = pl.BlockSpec((block, head_dim), lambda i: (i, 0))
    wide = pl.BlockSpec((block, width), lambda i: (i, 0))
    return pl.pallas_call(
        functools.partial(front_back_kernel, groups, head_dim),
        grid=(rows // block,),
        in_specs=[wide, table, table, pl.BlockSpec(gains.shape, lambda i: (0, 0))] + [narrow] * (2 * groups),
        out_specs=[wide, pl.BlockSpec((8, head_dim), lambda i: (0, 0))],
        out_shape=[
            jax.ShapeDtypeStruct((rows, width), jnp.bfloat16),
            jax.ShapeDtypeStruct((8, head_dim), jnp.float32),
        ],
        compiler_params=pltpu.CompilerParams(vmem_limit_bytes=32 * MIB),
        cost_estimate=pl.CostEstimate(flops=60 * rows * width, bytes_accessed=10 * rows * width, transcendentals=0),
    )(raw, cosine, sine, gains, *grad_queries, *grad_kv)


def last_product_kernel(grad_ref, weight_ref, hidden_ref, scale_ref, gain_ref, out_ref, dots_ref, gain_out_ref):
    part = matmul(grad_ref[...], weight_ref[...], NT)
    out_ref[0] = part.astype(out_ref.dtype)
    product = part * (hidden_ref[...] * scale_ref[...])
    gain_out_ref[...] = jnp.sum(product, axis=0, keepdims=True)
    dots = jnp.sum(product * gain_ref[...], axis=1, keepdims=True)

    @pl.when(pl.program_id(0) == 0)
    def _():
        dots_ref[...] = dots

    @pl.when(pl.program_id(0) > 0)
    def _():
        dots_ref[...] += dots


def last_product(grads, weight, hidden, scale, gain, pieces):
    rows, width = grads.shape
    depth = weight.shape[0]
    block = depth // pieces // 2
    return pl.pallas_call(
        last_product_kernel,
        grid=(depth // block,),
        in_specs=[
            pl.BlockSpec((rows, width), lambda i: (0, 0), pipeline_mode=pl.Buffered(1)),
            pl.BlockSpec((block, width), lambda i: (i, 0)),
            pl.BlockSpec((rows, block), lambda i: (0, i)),
            pl.BlockSpec((rows, 1), lambda i: (0, 0)),
            pl.BlockSpec((1, block), lambda i: (0, i)),
        ],
        out_specs=[
            pl.BlockSpec((1, rows, block), lambda i: (i // 2, 0, i % 2)),
            pl.BlockSpec((rows, 1), lambda i: (0, 0)),
            pl.BlockSpec((1, block), lambda i: (0, i)),
        ],
        out_shape=[
            jax.ShapeDtypeStruct((pieces, rows, depth // pieces), jnp.bfloat16),
            jax.ShapeDtypeStruct((rows, 1), jnp.float32),
            jax.ShapeDtypeStruct((1, depth), jnp.float32),
        ],
        compiler_params=pltpu.CompilerParams(vmem_limit_bytes=32 * MIB),
        cost_estimate=pl.CostEstimate(flops=4 * rows * depth * width, bytes_accessed=2 * depth * width, transcendentals=0),
    )(grads, weight, hidden, scale, gain)


def resid_kernel(sum_ref, hidden_ref, gain_ref, resid_ref, normed_ref, normed_t_ref, scale_ref):
    total = jnp.concatenate([sum_ref[at] for at in range(sum_ref.shape[0])], axis=1)
    resid = hidden_ref[...] + total.astype(jnp.float32)
    scale = lax.rsqrt(jnp.mean(resid * resid, axis=1, keepdims=True) + EPSILON)
    normed = resid * scale * gain_ref[...]
    resid_ref[...] = resid
    scale_ref[...] = scale
    normed_ref[...] = normed.astype(normed_ref.dtype)
    normed_t_ref[...] = jnp.transpose(normed).astype(normed_t_ref.dtype)


def add_and_norm(total, hidden, gain):
    pieces, rows, width = total.shape
    depth = pieces * width
    block = min(256, rows)
    wide = pl.BlockSpec((block, depth), lambda i: (i, 0))
    return pl.pallas_call(
        resid_kernel,
        grid=(rows // block,),
        in_specs=[
            pl.BlockSpec((pieces, block, width), lambda i: (0, i, 0)),
            wide,
            pl.BlockSpec((1, depth), lambda i: (0, 0)),
        ],
        out_specs=[
            wide,
            wide,
            pl.BlockSpec((depth, block), lambda i: (0, i)),
            pl.BlockSpec((block, 1), lambda i: (i, 0)),
        ],
        out_shape=[
            jax.ShapeDtypeStruct((rows, depth), jnp.float32),
            jax.ShapeDtypeStruct((rows, depth), jnp.bfloat16),
            jax.ShapeDtypeStruct((depth, rows), jnp.bfloat16),
            jax.ShapeDtypeStruct((rows, 1), jnp.float32),
        ],
        compiler_params=pltpu.CompilerParams(vmem_limit_bytes=40 * MIB),
        cost_estimate=pl.CostEstimate(flops=10 * rows * depth, bytes_accessed=18 * rows * depth, transcendentals=0),
    )(total, hidden, gain)


def resid_back_kernel(sum_ref, cot_ref, resid_ref, scale_ref, gain_ref, grad_ref, rounded_ref, gain_out_ref):
    grads = jnp.concatenate([sum_ref[at] for at in range(sum_ref.shape[0])], axis=1).astype(jnp.float32)
    scale = scale_ref[...]
    normal = resid_ref[...] * scale
    sums = jnp.sum(grads * normal, axis=0, keepdims=True)
    grads = grads * gain_ref[...]
    grads = scale * (grads - normal * jnp.mean(grads * normal, axis=1, keepdims=True))
    grads = cot_ref[...].astype(jnp.float32) + grads
    grad_ref[...] = grads
    rounded_ref[...] = grads.astype(rounded_ref.dtype)

    @pl.when(pl.program_id(0) == 0)
    def _():
        gain_out_ref[...] = sums

    @pl.when(pl.program_id(0) > 0)
    def _():
        gain_out_ref[...] += sums


def norm_and_add_back(total, cotangent, resid, scale, gain):
    pieces, rows, width = total.shape
    depth = pieces * width
    block = min(256, rows)
    wide = pl.BlockSpec((block, depth), lambda i: (i, 0))
    whole = pl.BlockSpec((1, depth), lambda i: (0, 0))
    return pl.pallas_call(
        resid_back_kernel,
        grid=(rows // block,),
        in_specs=[
            pl.BlockSpec((pieces, block, width), lambda i: (0, i, 0)),
            wide,
            wide,
            pl.BlockSpec((block, 1), lambda i: (i, 0)),
            whole,
        ],
        out_specs=[wide, wide, whole],
        out_shape=[
            jax.ShapeDtypeStruct((rows, depth), jnp.float32),
            jax.ShapeDtypeStruct((rows, depth), jnp.bfloat16),
            jax.ShapeDtypeStruct((1, depth), jnp.float32),
        ],
        compiler_params=pltpu.CompilerParams(vmem_limit_bytes=40 * MIB),
        cost_estimate=pl.CostEstimate(flops=10 * rows * depth, bytes_accessed=16 * rows * depth, transcendentals=0),
    )(total, cotangent, resid, scale, gain)


def step_of(rate, weight, moment, average, gradient, outs):
    moment = MOMENTUM * moment + gradient
    weight = weight - rate * (gradient + MOMENTUM * moment)
    average = EMA_DECAY * average + (1.0 - EMA_DECAY) * weight
    for out, value in zip(outs, (weight, moment, average, average)):
        out[...] = value.astype(out.dtype)


def mlp_step_kernel(rate, steps_of, *refs):
    chunks = len(steps_of)
    grads, held, outs = refs[:chunks], refs[chunks : chunks + 6], refs[chunks + 6 :]
    begin = 0
    for chunk, steps in enumerate(steps_of):

        @pl.when((pl.program_id(0) >= begin) & (pl.program_id(0) < begin + steps))
        def _():
            both = grads[chunk][:2].astype(jnp.float32)
            step_of(rate, *(ref[...] for ref in held[:3]), both, outs[:4])
            down = jnp.transpose(grads[chunk][2].astype(jnp.float32))
            step_of(rate, *(ref[...] for ref in held[3:]), down, outs[4:])

        begin += steps


def mlp_step(rate, grads, gate_up, down):
    kinds, depth, _ = grads[0].shape
    block = min(FF_BLOCK, grads[0].shape[2])
    steps_of = [grad.shape[2] // block for grad in grads]

    def grad_spec(chunk):
        begin, last = sum(steps_of[:chunk]), steps_of[chunk] - 1
        return pl.BlockSpec((kinds, depth, block), lambda i: (0, 0, jnp.clip(i - begin, 0, last)))

    gate_up_spec = pl.BlockSpec((2, depth, block), lambda i: (0, 0, i))
    down_spec = pl.BlockSpec((block, depth), lambda i: (i, 0))
    types = (jnp.float32,) * 3 + (jnp.bfloat16,)
    return pl.pallas_call(
        functools.partial(mlp_step_kernel, rate, steps_of),
        grid=(sum(steps_of),),
        in_specs=[grad_spec(chunk) for chunk in range(len(grads))] + [gate_up_spec] * 3 + [down_spec] * 3,
        out_specs=[gate_up_spec] * 4 + [down_spec] * 4,
        out_shape=[jax.ShapeDtypeStruct(gate_up[0].shape, kind) for kind in types]
        + [jax.ShapeDtypeStruct(down[0].shape, kind) for kind in types],
        compiler_params=pltpu.CompilerParams(vmem_limit_bytes=40 * MIB),
        cost_estimate=pl.CostEstimate(flops=0, bytes_accessed=26 * sum(grad.size for grad in grads), transcendentals=0),
    )(*grads, *gate_up, *down)


def turned_step_kernel(rate, grad_ref, *refs):
    step_of(rate, *(ref[...] for ref in refs[:3]), jnp.transpose(grad_ref[...].astype(jnp.float32)), refs[3:])


def turned_step(rate, grad_t, held):
    types = (jnp.float32,) * 3 + (jnp.bfloat16,)
    return pl.pallas_call(
        functools.partial(turned_step_kernel, rate),
        in_specs=[pl.BlockSpec(memory_space=pltpu.VMEM)] * 4,
        out_specs=[pl.BlockSpec(memory_space=pltpu.VMEM)] * 4,
        out_shape=[jax.ShapeDtypeStruct(held[0].shape, kind) for kind in types],
        compiler_params=pltpu.CompilerParams(vmem_limit_bytes=24 * MIB),
        cost_estimate=pl.CostEstimate(flops=0, bytes_accessed=28 * grad_t.size, transcendentals=0),
    )(grad_t, *held)


def out_product_kernel(left_ref, weight_ref, out_ref):
    out_ref[0] = matmul(left_ref[...], weight_ref[...], NT).astype(out_ref.dtype)


def out_product(left, weight, column, pieces):
    rows, width = left.shape
    depth = weight.shape[0]
    block = depth // pieces // 2
    return pl.pallas_call(
        out_product_kernel,
        grid=(depth // block,),
        in_specs=[
            pl.BlockSpec((rows, width), lambda i: (0, 0), pipeline_mode=pl.Buffered(1)),
            pl.BlockSpec((block, width), lambda i: (i, column)),
        ],
        out_specs=pl.BlockSpec((1, rows, block), lambda i: (i // 2, 0, i % 2)),
        out_shape=jax.ShapeDtypeStruct((pieces, rows, depth // pieces), jnp.bfloat16),
        compiler_params=pltpu.CompilerParams(vmem_limit_bytes=32 * MIB),
        cost_estimate=pl.CostEstimate(flops=2 * rows * depth * width, bytes_accessed=2 * depth * width, transcendentals=0),
    )(left, weight)


def rms_scale(values_in):
    return lax.rsqrt(jnp.mean(values_in * values_in, axis=-1, keepdims=True) + EPSILON)


def rope_tables(offsets, head_dim):
    half_dim = head_dim // 2
    frequency = 1.0 / ROPE_BASE ** (jnp.arange(half_dim, dtype=jnp.float32) * 2.0 / head_dim)
    angles = offsets.astype(jnp.float32)[:, None] * frequency[None, :]
    cosine = jnp.cos(angles)
    sine = jnp.sin(angles)
    return (jnp.concatenate([cosine, cosine], axis=-1), jnp.concatenate([sine, sine], axis=-1))


def nesterov(weight, moment, average, gradient, rate):
    new_moment = MOMENTUM * moment + gradient
    new_weight = weight - rate * (gradient + MOMENTUM * new_moment)
    new_average = EMA_DECAY * average + (1.0 - EMA_DECAY) * new_weight
    return (new_weight, new_moment, new_average, new_average.astype(jnp.bfloat16))


def dot(a, b, dims):
    return lax.dot_general(a, b, dims, preferred_element_type=jnp.float32)


def tie(*values):
    return lax.optimization_barrier(values)


def local(
    hidden_in,
    cotangent,
    doc_lengths,
    valid_mask,
    w_qkv,
    w_out,
    w_gate_up,
    w_down,
    norm_gains,
    m_qkv,
    m_out,
    m_gate_up,
    m_down,
    m_gains,
    a_qkv,
    a_out,
    a_gate_up,
    a_down,
    a_gains,
):
    row_count, model_dim = hidden_in.shape
    head_dim = (norm_gains.shape[0] - 2 * model_dim) // 2
    data_ways = lax.axis_size("dp")
    tensor_ways = lax.axis_size("tensor")
    tensor_at = lax.axis_index("tensor")
    tokens_all = row_count * data_ways
    width_cols = model_dim // tensor_ways
    col_begin = tensor_at * width_cols
    groups = w_qkv.shape[1] // (4 * head_dim)
    ff_local = w_down.shape[0]
    ff_unit = ff_local // CHUNK_ENDS[-1]
    bf16 = jnp.bfloat16
    f32 = jnp.float32

    def columns_of(values_in):
        return lax.dynamic_slice_in_dim(values_in, col_begin, width_cols, values_in.ndim - 1)

    qkv_cols, out_rows = w_qkv.shape[1], w_out.shape[0]
    qkv_out = lax.all_gather(jnp.concatenate([w_qkv, w_out.T], axis=1).astype(bf16), "dp", axis=0, tiled=True)

    ends_at = jnp.cumsum(doc_lengths)
    starts_at = ends_at - doc_lengths
    place_begin = lax.axis_index("dp") * row_count
    places = place_begin + jnp.arange(row_count, dtype=jnp.int32)
    doc_ids = jnp.sum((places[:, None] >= ends_at[None, :]).astype(jnp.int32), axis=1)
    owned = doc_ids[:, None] == jnp.arange(doc_lengths.shape[0], dtype=jnp.int32)[None, :]
    doc_begin = jnp.sum(jnp.where(owned, starts_at[None, :], 0), axis=1)
    cosine, sine = rope_tables(places - doc_begin, head_dim)
    query_rows = min(512, row_count)
    blocks = row_count // query_rows
    bounds = jnp.stack(
        [
            place_begin + jnp.arange(blocks, dtype=jnp.int32) * query_rows,
            doc_begin[::query_rows],
            doc_begin[query_rows - 1 :: query_rows],
        ]
    ).astype(jnp.int32)
    begin_rows = doc_begin.astype(jnp.int32).reshape(blocks, 1, query_rows)

    gain_attn = norm_gains[:model_dim]
    gain_mlp = norm_gains[model_dim : 2 * model_dim]
    gain_query = norm_gains[2 * model_dim : 2 * model_dim + head_dim]
    gain_key = norm_gains[2 * model_dim + head_dim :]
    scale_one = rms_scale(hidden_in)
    normal_one = hidden_in * scale_one
    normed_one_b = (normal_one * gain_attn).astype(bf16)
    gains_two = jnp.stack([gain_query, gain_key])
    projected, queries, kv_local = front(
        normed_one_b, qkv_out, qkv_cols, cosine, sine, gains_two, head_dim
    )
    kv_every = lax.all_gather(kv_local, "dp", axis=0, tiled=True)

    down_t = w_down.T

    def chunk_shard(chunk):
        units = slice(CHUNK_ENDS[chunk] * ff_unit, CHUNK_ENDS[chunk + 1] * ff_unit)
        return jnp.stack([w_gate_up[0, :, units], w_gate_up[1, :, units], down_t[:, units]]).astype(bf16)

    def chunk_gather(shard):
        return lax.all_gather(shard, "dp", axis=0)

    shard, kv_every, cotangent_t = tie(chunk_shard(0), kv_every, cotangent.T)
    chunk_weights = [chunk_gather(shard)]
    mixed, totals = [], []
    for group in range(groups):
        mixed_rows, total_rows = attend(
            bounds, queries[group], begin_rows, kv_every, group, head_dim, query_rows, min(1024, tokens_all)
        )
        mixed.append(mixed_rows)
        totals.append(total_rows)
    mixed_b = jnp.concatenate(mixed, axis=1)
    attn_part = out_product(mixed_b, qkv_out, qkv_cols // out_rows, tensor_ways)
    shard, chunk_weights[0], attn_part = tie(chunk_shard(1), chunk_weights[0], attn_part)
    chunk_weights.append(chunk_gather(shard))
    attn_sum = tensor_sum(attn_part, 0)
    resid_one, normed_two_b, normed_two_t, scale_two = add_and_norm(attn_sum, hidden_in, gain_mlp[None])

    weight_grads, hiddens, back_pairs = [], [], []
    for weights in chunk_weights:
        hidden_b, gate_grad, up_grad, weight_grad = mlp_chunk(
            normed_two_b, cotangent, normed_two_t, cotangent_t, weights
        )
        hiddens.append((hidden_b,))
        back_pairs.append((gate_grad, up_grad))
        weight_grads.append(lax.psum_scatter(weight_grad, "dp", scatter_dimension=0))

    part_two = back_product(back_pairs, chunk_weights, 0, tensor_ways)
    mlp_part = back_product(hiddens, chunk_weights, 2, tensor_ways)
    part_two, mlp_part = tie(part_two, mlp_part)
    part_two_sum, weight_grads[0] = tie(tensor_sum(part_two, 1), weight_grads[0])
    grad_resid, grad_attn_b, gain_mlp_part = norm_and_add_back(
        part_two_sum, cotangent, resid_one, scale_two, gain_mlp[None]
    )
    grad_mixed_b = dot(grad_attn_b, qkv_out[:, qkv_cols:], NN).astype(bf16)

    grad_out_t = dot(grad_attn_b, mixed_b, TN).astype(bf16)
    lines = data_ways // 2
    line_at, lane = lax.axis_index("dp") // 2, lax.axis_index("dp") % 2
    out_pieces = grad_out_t.reshape(lines, 2, model_dim // data_ways, out_rows)

    def chip_piece(step, of_lane):
        return lax.dynamic_slice(
            out_pieces, ((line_at + lines - step) % lines, of_lane, 0, 0), (1, 1, *out_pieces.shape[2:])
        )[0, 0]

    far_pieces = lax.ppermute(
        jnp.stack([chip_piece(step, 1 - lane) for step in range(lines)]),
        "dp",
        [(at, at + 1 - 2 * (at % 2)) for at in range(data_ways)],
    )

    def chip_sum(step, *others):
        return sum(value.astype(f32) for value in (chip_piece(step, lane), far_pieces[step], *others))

    def hop(step, *others):
        return lax.ppermute(
            chip_sum(step, *others).astype(bf16), "dp", [(at, (at + 2) % data_ways) for at in range(data_ways)]
        )

    out_grad = hop(1)
    grad_queries, kv_sums = [], []
    for group in range(groups):
        grad_rows = grad_mixed_b[:, group * 2 * head_dim : (group + 1) * 2 * head_dim]
        if group and group == groups - 1:
            grad_rows, weight_grads[1], out_grad, kv_sums[-1] = tie(
                grad_rows, weight_grads[1], out_grad, kv_sums[-1]
            )
        if group == groups - 1:
            for step in range(2, lines - 1):
                out_grad = hop(step, out_grad)
        grad_query, kv_sum = attend_back(
            bounds,
            queries[group],
            grad_rows,
            mixed[group],
            totals[group],
            begin_rows,
            kv_every,
            group,
            head_dim,
            query_rows,
            min(512, tokens_all),
        )
        grad_queries.append(grad_query)
        kv_sums.append(kv_sum)
    out_grad, kv_sums[-1] = tie(out_grad, kv_sums[-1])
    if lines > 2:
        out_grad = hop(lines - 1, out_grad)
    out_grad = chip_sum(0, out_grad).astype(bf16)
    kv_grads = []
    for group in range(groups):
        if group:
            kv_grads[-1], kv_sums[group] = tie(kv_grads[-1], kv_sums[group])
        kv_grads.append(lax.psum_scatter(kv_sums[group], "dp", scatter_dimension=0, tiled=True))
    mlp_part, grad_queries[-1] = tie(mlp_part, grad_queries[-1])
    rate_matrix = LR_MATRIX / math.sqrt(tokens_all)
    mlp_sum = tensor_sum(mlp_part, 2, False)
    updates = (
        *turned_step(rate_matrix, out_grad, (w_out, m_out, a_out)),
        *mlp_step(rate_matrix, weight_grads, (w_gate_up, m_gate_up, a_gate_up), (w_down, m_down, a_down)),
    )
    mlp_cols = mlp_sum.astype(f32)
    resid_cols = columns_of(resid_one)
    attn_cols = lax.dynamic_index_in_dim(attn_sum, tensor_at, 0, False).astype(f32)
    mask_rows = valid_mask.astype(f32)[:, None]
    stats_part = [
        jnp.sum(mask_rows * columns * columns) for columns in (columns_of(hidden_in), attn_cols, mlp_cols)
    ]
    stats_part.append(jnp.where(tensor_at == 0, jnp.sum(valid_mask.astype(f32)), 0.0))
    gain_mlp_wide = lax.dynamic_update_slice_in_dim(
        jnp.zeros((model_dim,), f32), columns_of(gain_mlp_part[0]), col_begin, 0
    )
    mixed_cols, gain_mlp_wide, stats_part, kv_grads[-1], updates = tie(
        resid_cols + mlp_cols, gain_mlp_wide, jnp.stack(stats_part), kv_grads[-1], updates
    )
    grad_projected_b, gains_found = front_back(
        projected, cosine, sine, gains_two, grad_queries, kv_grads, head_dim
    )
    grad_qkv = dot(normed_one_b, grad_projected_b, TN).astype(bf16)
    qkv_shard = lax.psum_scatter(grad_qkv, "dp", scatter_dimension=0, tiled=True).astype(f32)
    part_one, dots_part, gain_attn_part = last_product(
        grad_projected_b, qkv_out, hidden_in, scale_one, gain_attn[None], tensor_ways
    )

    gains_part = jnp.concatenate(
        [gain_attn_part[0], gain_mlp_wide, gains_found[0], gains_found[1], stats_part]
    )
    gains_count = gains_part.shape[0]
    gains_rows = -(-gains_count // 1024) * 8
    gains_part = jnp.pad(gains_part, (0, gains_rows * 128 - gains_count)).reshape(gains_rows, 128)
    grad_one_cols, row_dots, gains_sum = last_sum(
        part_one, dots_part.reshape(row_count // 128, 128), gains_part, data_ways, 3
    )
    gains_sum = gains_sum.reshape(-1)[:gains_count]
    grad_cols = columns_of(grad_resid) + scale_one * (
        grad_one_cols.astype(f32) * columns_of(gain_attn)
        - columns_of(normal_one) * (row_dots.reshape(row_count, 1) / model_dim)
    )
    grad_gains = gains_sum[: norm_gains.shape[0]]
    stats_sum = gains_sum[norm_gains.shape[0] :]
    branch_rms = jnp.sqrt(stats_sum[:3] / (stats_sum[3] * model_dim))

    rate_gain = LR_GAIN / math.sqrt(tokens_all)
    return (
        mixed_cols,
        grad_cols,
        branch_rms,
        *nesterov(w_qkv, m_qkv, a_qkv, qkv_shard, rate_matrix),
        *updates,
        *nesterov(norm_gains, m_gains, a_gains, grad_gains, rate_gain),
    )


def solution(mesh):
    rows = P("dp", None)
    spread = P("dp", "tensor")
    turned = P("tensor", "dp")
    stacked = P(None, "dp", "tensor")
    matrices = (spread, turned, stacked, turned, P())
    in_specs = (rows, rows, P(), P("dp"), *matrices, *matrices, *matrices)
    out_specs = (spread, spread, P(), *(spec for spec in matrices for _ in range(4)))
    return jax.shard_map(local, mesh=mesh, in_specs=in_specs, out_specs=out_specs, check_vma=False)
```

```python
import functools, math
import jax, jax.numpy as jnp
from jax import lax
from jax.experimental import pallas as pl
from jax.experimental.pallas import tpu as pltpu
NT = (((1,), (1,)), ((), ()))
NN = (((1,), (0,)), ((), ()))
TN = (((0,), (0,)), ((), ()))
NEG_FILL = -1e30
LOG2E = math.log2(math.e)
MIB = 1024 * 1024

def matmul(a, b, dims):
    return lax.dot_general(a, b, dims, preferred_element_type=jnp.float32)

def row_of(column):
    return jnp.transpose(jnp.broadcast_to(column, (column.shape[0], 128)))[:1]

def attend_kernel(head_dim, key_rows, bound_ref, query_ref, begin_ref, kv_ref, out_ref, total_ref, q_two, accum):
    rows = query_ref.shape[0]
    block = pl.program_id(0)
    first = bound_ref[0, block]
    begin_first = bound_ref[1, block]
    begin_last = bound_ref[2, block]
    scale = LOG2E * head_dim**-0.5
    q_two[:rows] = query_ref[:, :head_dim]
    q_two[rows:] = query_ref[:, head_dim:]
    places = first + lax.broadcasted_iota(jnp.int32, (1, rows), 1)
    places = jnp.concatenate([places, places], axis=1)
    begins = jnp.concatenate([begin_ref[0], begin_ref[0]], axis=1)

    def step(masked, index, carry):
        top, total = carry
        key_begin = pl.multiple_of(index * key_rows, key_rows)
        keys = kv_ref[pl.ds(key_begin, key_rows), :head_dim]
        values = kv_ref[pl.ds(key_begin, key_rows), head_dim:]
        raw = matmul(keys, q_two[...], NT) * scale
        if masked:
            key_places = key_begin + lax.broadcasted_iota(jnp.int32, (key_rows, 1), 0)
            allowed = (key_places >= begins) & (key_places <= places)
            raw = jnp.where(allowed, raw, NEG_FILL)
        new_top = jnp.maximum(top, jnp.max(raw, axis=0, keepdims=True))
        probs = jnp.exp2(raw - new_top)
        fade = jnp.exp2(top - new_top)
        total = total * fade + jnp.sum(probs, axis=0, keepdims=True)
        accum[...] = accum[...] * fade + matmul(values, probs.astype(jnp.bfloat16), TN)
        return (new_top, total)

    def either(index, carry):
        key_begin = index * key_rows
        plain = (key_begin >= begin_last) & (key_begin + key_rows - 1 <= first)
        return lax.cond(
            plain, functools.partial(step, False, index), functools.partial(step, True, index), carry
        )

    accum[...] = jnp.zeros_like(accum)
    start = (
        jnp.full((1, 2 * rows), NEG_FILL, jnp.float32),
        jnp.zeros((1, 2 * rows), jnp.float32),
    )
    low = begin_first // key_rows
    high = (first + rows - 1) // key_rows + 1
    top, total = lax.fori_loop(low, high, either, start)
    out = jnp.transpose(accum[...] / total)
    out_ref[:, :head_dim] = out[:rows].astype(out_ref.dtype)
    out_ref[:, head_dim:] = out[rows:].astype(out_ref.dtype)
    total_ref[0] = top + jnp.log2(total)

def attend(bounds, queries, begins, kv_all, group, head_dim, query_rows, key_rows):
    rows = queries.shape[0]
    blocks = rows // query_rows
    return pl.pallas_call(
        functools.partial(attend_kernel, head_dim, key_rows),
        out_shape=(jax.ShapeDtypeStruct(queries.shape, jnp.bfloat16), jax.ShapeDtypeStruct((blocks, 1, 2 * query_rows), jnp.float32)),
        grid_spec=pltpu.PrefetchScalarGridSpec(
            num_scalar_prefetch=1,
            grid=(blocks,),
            in_specs=[
                pl.BlockSpec((query_rows, 2 * head_dim), lambda i, *_: (i, 0)),
                pl.BlockSpec((1, 1, query_rows), lambda i, *_: (i, 0, 0)),
                pl.BlockSpec((kv_all.shape[0], 2 * head_dim), lambda i, *_: (0, group)),
            ],
            out_specs=[
                pl.BlockSpec((query_rows, 2 * head_dim), lambda i, *_: (i, 0)),
                pl.BlockSpec((1, 1, 2 * query_rows), lambda i, *_: (i, 0, 0)),
            ],
            scratch_shapes=[pltpu.VMEM((2 * query_rows, head_dim), jnp.bfloat16), pltpu.VMEM((head_dim, 2 * query_rows), jnp.float32)],
        ),
        compiler_params=pltpu.CompilerParams(vmem_limit_bytes=60 * MIB),
        cost_estimate=pl.CostEstimate(flops=8 * rows * kv_all.shape[0] * head_dim, bytes_accessed=2 * kv_all.size, transcendentals=2 * rows * kv_all.shape[0]),
    )(bounds, queries, begins, kv_all)

def attend_back_kernel(head_dim, key_rows, bound_ref, query_ref, grad_ref, out_ref, total_ref, begin_ref, kv_ref, grad_q_ref, grad_kv_ref, q_two, g_two, dq_two, kv_sum):
    rows = query_ref.shape[0]
    block = pl.program_id(0)
    first = bound_ref[0, block]
    begin_first = bound_ref[1, block]
    begin_last = bound_ref[2, block]
    unit = head_dim**-0.5
    scale = LOG2E * unit

    @pl.when(block == 0)
    def _():
        kv_sum[...] = jnp.zeros_like(kv_sum)

    for half in range(2):
        part = slice(half * rows, (half + 1) * rows)
        cols = slice(half * head_dim, (half + 1) * head_dim)
        q_two[part] = query_ref[:, cols]
        g_two[part] = grad_ref[:, cols]
    dq_two[...] = jnp.zeros_like(dq_two)
    product = grad_ref[...].astype(jnp.float32) * out_ref[...].astype(jnp.float32)
    delta = jnp.concatenate(
        [
            row_of(jnp.sum(product[:, :head_dim], axis=1, keepdims=True)),
            row_of(jnp.sum(product[:, head_dim:], axis=1, keepdims=True)),
        ],
        axis=1,
    )
    totals = total_ref[0]
    places = first + lax.broadcasted_iota(jnp.int32, (1, rows), 1)
    places = jnp.concatenate([places, places], axis=1)
    begins = jnp.concatenate([begin_ref[0], begin_ref[0]], axis=1)

    def step(masked, index):
        key_begin = pl.multiple_of(index * key_rows, key_rows)
        place = pl.ds(key_begin, key_rows)
        keys = kv_ref[place, :head_dim]
        values = kv_ref[place, head_dim:]
        raw = matmul(keys, q_two[...], NT)
        probs = jnp.exp2(raw * scale - totals)
        if masked:
            key_places = key_begin + lax.broadcasted_iota(jnp.int32, (key_rows, 1), 0)
            allowed = (key_places >= begins) & (key_places <= places)
            probs = jnp.where(allowed, probs, 0.0)
        kv_sum[place, head_dim:] += matmul(probs.astype(jnp.bfloat16), g_two[...], NN)
        grad_probs = matmul(values, g_two[...], NT)
        grad_scores = (probs * (grad_probs - delta)).astype(jnp.bfloat16)
        kv_sum[place, :head_dim] += matmul(grad_scores, q_two[...], NN)
        dq_two[...] += matmul(grad_scores, keys, TN)

    def either(index, carry):
        key_begin = index * key_rows
        plain = (key_begin >= begin_last) & (key_begin + key_rows - 1 <= first)

        @pl.when(plain)
        def _():
            step(False, index)

        @pl.when(jnp.logical_not(plain))
        def _():
            step(True, index)

        return carry

    low = begin_first // key_rows
    high = (first + rows - 1) // key_rows + 1
    lax.fori_loop(low, high, either, 0)
    grad_q_ref[:, :head_dim] = (dq_two[:rows] * unit).astype(grad_q_ref.dtype)
    grad_q_ref[:, head_dim:] = (dq_two[rows:] * unit).astype(grad_q_ref.dtype)

    @pl.when(block == pl.num_programs(0) - 1)
    def _():
        grad_kv_ref[:, :head_dim] = (kv_sum[:, :head_dim] * unit).astype(grad_kv_ref.dtype)
        grad_kv_ref[:, head_dim:] = kv_sum[:, head_dim:].astype(grad_kv_ref.dtype)

def attend_back(bounds, queries, grads, outs, totals, begin_rows, kv_all, group, head_dim, query_rows, key_rows):
    rows = queries.shape[0]
    blocks = rows // query_rows
    wide = pl.BlockSpec((query_rows, 2 * head_dim), lambda i, *_: (i, 0))
    kv_shape = (kv_all.shape[0], 2 * head_dim)
    whole = pl.BlockSpec(kv_shape, lambda i, *_: (0, 0))
    return pl.pallas_call(
        functools.partial(attend_back_kernel, head_dim, key_rows),
        out_shape=(jax.ShapeDtypeStruct(queries.shape, jnp.float32), jax.ShapeDtypeStruct(kv_shape, jnp.bfloat16)),
        grid_spec=pltpu.PrefetchScalarGridSpec(
            num_scalar_prefetch=1,
            grid=(blocks,),
            in_specs=[wide, wide, wide,
                pl.BlockSpec((1, 1, 2 * query_rows), lambda i, *_: (i, 0, 0)),
                pl.BlockSpec((1, 1, query_rows), lambda i, *_: (i, 0, 0)),
                pl.BlockSpec(kv_shape, lambda i, *_: (0, group))],
            out_specs=[wide, whole],
            scratch_shapes=[pltpu.VMEM((2 * query_rows, head_dim), jnp.bfloat16)] * 2
            + [pltpu.VMEM((2 * query_rows, head_dim), jnp.float32), pltpu.VMEM(kv_shape, jnp.float32)],
        ),
        compiler_params=pltpu.CompilerParams(vmem_limit_bytes=60 * MIB),
        cost_estimate=pl.CostEstimate(flops=20 * rows * kv_all.shape[0] * head_dim, bytes_accessed=2 * kv_all.size, transcendentals=2 * rows * kv_all.shape[0]),
    )(bounds, queries, grads, outs, totals, begin_rows, kv_all)


from jax.sharding import PartitionSpec as P

EPSILON = 1e-06
ROPE_BASE = 1000000.0
MOMENTUM = 0.5
EMA_DECAY = 0.5
LR_MATRIX = 0.08
LR_GAIN = 0.5
FF_BLOCK = 256
CHUNK_ENDS = (0, 1, 3)


def mlp_kernel(normed_ref, cot_ref, normed_t_ref, cot_t_ref, weight_ref, hidden_ref, gate_grad_ref, up_grad_ref, grads_ref, wide):
    ways, kinds, shard, _ = weight_ref.shape
    rows = normed_ref.shape[0]
    row_tile = min(512, rows)

    for at in range(ways):
        wide[:, at * shard : (at + 1) * shard, :] = weight_ref[at]

    @pl.loop(0, rows // row_tile)
    def _(tile):
        place = pl.ds(pl.multiple_of(tile * row_tile, row_tile), row_tile)
        x = normed_ref[place, :]
        gate = matmul(x, wide[0], NN)
        up = matmul(x, wide[1], NN)
        grad_hidden = matmul(cot_ref[place, :], wide[2], NN)
        sigmoid = 1.0 / (1.0 + jnp.exp(-gate))
        silu = gate * sigmoid
        hidden_ref[place, :] = (silu * up).astype(hidden_ref.dtype)
        gate_grad_ref[place, :] = (
            grad_hidden * up * (sigmoid * (1.0 + gate * (1.0 - sigmoid)))
        ).astype(gate_grad_ref.dtype)
        up_grad_ref[place, :] = (grad_hidden * silu).astype(up_grad_ref.dtype)

    for at in range(ways):
        place = slice(at * shard, (at + 1) * shard)
        left = normed_t_ref[place, :]
        grads_ref[at, 0] = matmul(left, gate_grad_ref[...], NN).astype(grads_ref.dtype)
        grads_ref[at, 1] = matmul(left, up_grad_ref[...], NN).astype(grads_ref.dtype)
        grads_ref[at, 2] = matmul(cot_t_ref[place, :], hidden_ref[...], NN).astype(grads_ref.dtype)


def mlp_chunk(normed, cotangent, normed_t, cotangent_t, weights):
    ways, _, shard, width = weights.shape
    rows, depth = normed.shape
    block = min(FF_BLOCK, width)

    def held(array):
        return pl.BlockSpec(array.shape, lambda i: (0, 0), pipeline_mode=pl.Buffered(1))

    weight_spec = pl.BlockSpec((ways, 3, shard, block), lambda i: (0, 0, 0, i))
    row_spec = pl.BlockSpec((rows, block), lambda i: (0, i))
    row_shape = jax.ShapeDtypeStruct((rows, width), jnp.bfloat16)
    return pl.pallas_call(
        mlp_kernel,
        grid=(width // block,),
        in_specs=[held(normed), held(cotangent), held(normed_t), held(cotangent_t), weight_spec],
        out_specs=[row_spec, row_spec, row_spec, weight_spec],
        out_shape=(row_shape, row_shape, row_shape, jax.ShapeDtypeStruct((ways, 3, shard, width), jnp.bfloat16)),
        scratch_shapes=[pltpu.VMEM((3, depth, block), jnp.bfloat16)],
        compiler_params=pltpu.CompilerParams(vmem_limit_bytes=60 * MIB),
        cost_estimate=pl.CostEstimate(flops=24 * rows * depth * width, bytes_accessed=12 * depth * width, transcendentals=rows * width),
    )(normed, cotangent, normed_t, cotangent_t, weights)


def back_product_kernel(kinds, *refs):
    out_ref = refs[-1]
    total = None
    chunks = (len(refs) - 1) // (kinds + 1)
    for chunk in range(chunks):
        weight_ref = refs[chunk * (kinds + 1) + kinds]
        for kind in range(kinds):
            part = matmul(refs[chunk * (kinds + 1) + kind][...], weight_ref[0, kind], NT)
            total = part if total is None else total + part
    out_ref[0] = total.astype(out_ref.dtype)


def back_product(groups_of, weights, kind_begin, pieces):
    kinds = len(groups_of[0])
    ways, _, shard, width = weights[0].shape
    rows = groups_of[0][0].shape[0]
    per_piece = ways // pieces
    args, specs = [], []
    for lefts, weight in zip(groups_of, weights):
        for left in lefts:
            args.append(left)
            specs.append(pl.BlockSpec(left.shape, lambda i: (0, 0), pipeline_mode=pl.Buffered(1)))
        args.append(weight)
        specs.append(pl.BlockSpec((1, kinds, shard, weight.shape[3]), lambda i: (i, kind_begin // kinds, 0, 0)))
    return pl.pallas_call(
        functools.partial(back_product_kernel, kinds),
        grid=(ways,),
        in_specs=specs,
        out_specs=pl.BlockSpec((1, rows, shard), lambda i: (i // per_piece, 0, i % per_piece)),
        out_shape=jax.ShapeDtypeStruct((pieces, rows, per_piece * shard), jnp.bfloat16),
        compiler_params=pltpu.CompilerParams(vmem_limit_bytes=60 * MIB),
        cost_estimate=pl.CostEstimate(flops=2 * len(weights) * kinds * rows * width * ways * shard, bytes_accessed=2 * len(weights) * kinds * width * ways * shard, transcendentals=0),
    )(*args)


MESH = pl.DeviceIdType.MESH
SUM_BLOCKS = 4


def flip(index, bit):
    unit = 1 << bit
    return index + unit - 2 * unit * ((index // unit) % 2)


def picks(index, fixed, free):
    base = 0
    for bit in fixed:
        unit = 1 << bit
        base = base + unit * ((index // unit) % 2)
    found = []
    for choice in range(1 << len(free)):
        offset = sum((1 << bit) for at, bit in enumerate(free) if (choice >> at) & 1)
        found.append(base + offset)
    return found


def tensor_sum_kernel(bits, whole, part_ref, out_ref, sums, landed, send_sem, recv_sem, send_out, recv_out):
    row_at = lax.axis_index("dp")
    me = lax.axis_index("tensor")
    barrier = pltpu.get_barrier_semaphore()
    for bit in range(bits):
        pl.semaphore_signal(barrier, inc=1, device_id=(row_at, flip(me, bit)), device_id_type=MESH)
    pl.semaphore_wait(barrier, bits)
    tensor_sum_steps(bits, whole, part_ref, out_ref, sums, landed, send_sem, recv_sem, send_out, recv_out)


def tensor_sum_steps(bits, whole, part_ref, out_ref, sums, landed, send_sem, recv_sem, send_out, recv_out):
    row_at = lax.axis_index("dp")
    me = lax.axis_index("tensor")
    rows = part_ref.shape[1] // SUM_BLOCKS
    orders = [list(range(bits)) if b % 2 == 0 else list(range(bits))[::-1] for b in range(SUM_BLOCKS)]

    def place(block):
        return pl.ds(block * rows, rows)

    def scatter(block, step):
        order = orders[block]
        bit = order[step]
        there = flip(me, bit)
        free = order[step + 1 :]
        source = part_ref if step == 0 else sums
        base = (1 << bits) - (1 << (bits - step))
        copies = []
        for at, piece in enumerate(picks(there, order[: step + 1], free)):
            slot = base + at
            copies.append(
                pltpu.make_async_remote_copy(
                    src_ref=source.at[piece, place(block)],
                    dst_ref=landed.at[slot, place(block)],
                    send_sem=send_sem.at[slot, block],
                    recv_sem=recv_sem.at[slot, block],
                    device_id=(row_at, there),
                    device_id_type=MESH,
                )
            )
        return copies

    def gather(block, step):
        order = orders[block][::-1]
        bit = order[step]
        there = flip(me, bit)
        base = (1 << step) - 1
        copies = []
        for at, piece in enumerate(picks(me, order[step:], order[:step])):
            slot = base + at
            copies.append(
                pltpu.make_async_remote_copy(
                    src_ref=out_ref.at[piece, place(block)],
                    dst_ref=out_ref.at[piece, place(block)],
                    send_sem=send_out.at[slot, block],
                    recv_sem=recv_out.at[slot, block],
                    device_id=(row_at, there),
                    device_id_type=MESH,
                )
            )
        return copies

    every = []
    flying = []
    for block in range(SUM_BLOCKS):
        copies = scatter(block, 0)
        for copy in copies:
            copy.start()
        flying.append(copies)
    for step in range(bits):
        for block in range(SUM_BLOCKS):
            order = orders[block]
            base = (1 << bits) - (1 << (bits - step))
            for copy in flying[block]:
                copy.wait_recv()
            every += flying[block]
            source = part_ref if step == 0 else sums
            last = step == bits - 1
            for at, piece in enumerate(picks(me, order[: step + 1], order[step + 1 :])):
                total = source[piece, place(block)].astype(jnp.float32) + landed[base + at, place(block)].astype(jnp.float32)
                if not last:
                    sums[piece, place(block)] = total.astype(sums.dtype)
                elif whole:
                    out_ref[piece, place(block)] = total.astype(out_ref.dtype)
                else:
                    out_ref[place(block)] = total.astype(out_ref.dtype)
            if not last:
                flying[block] = scatter(block, step + 1)
            elif whole:
                flying[block] = gather(block, 0)
            if not last or whole:
                for copy in flying[block]:
                    copy.start()
    if whole:
        for step in range(bits):
            for block in range(SUM_BLOCKS):
                for copy in flying[block]:
                    copy.wait_recv()
                every += flying[block]
                if step < bits - 1:
                    flying[block] = gather(block, step + 1)
                    for copy in flying[block]:
                        copy.start()
    for copy in every:
        copy.wait_send()


def tensor_sum(part, collective_id, whole=True):
    ways, rows, width = part.shape
    bits = ways.bit_length() - 1
    return pl.pallas_call(
        functools.partial(tensor_sum_kernel, bits, whole),
        out_shape=jax.ShapeDtypeStruct(part.shape if whole else part.shape[1:], part.dtype),
        in_specs=[pl.BlockSpec(memory_space=pltpu.VMEM)],
        out_specs=pl.BlockSpec(memory_space=pltpu.VMEM),
        scratch_shapes=[
            pltpu.VMEM(part.shape, part.dtype),
            pltpu.VMEM((ways - 1, rows, width), part.dtype),
            *[pltpu.SemaphoreType.DMA((ways - 1, SUM_BLOCKS))] * 4,
        ],
        compiler_params=pltpu.CompilerParams(
            collective_id=collective_id, has_side_effects=True, vmem_limit_bytes=32 * MIB
        ),
        cost_estimate=pl.CostEstimate(flops=0, bytes_accessed=(256 if whole else 128) * MIB, transcendentals=0),
    )(part)


def spread_kernel(source, slots, me, ways, place, send_sem, recv_sem):
    copies = []
    for step in range(1, ways):
        there = lax.rem(me + step, ways)
        copies.append(
            pltpu.make_async_remote_copy(
                src_ref=source,
                dst_ref=slots.at[me],
                send_sem=send_sem.at[step - 1],
                recv_sem=recv_sem.at[step - 1],
                device_id=place(there),
                device_id_type=MESH,
            )
        )
    for copy in copies:
        copy.start()
    return copies


def total_of(slots, ways):
    total = slots[0]
    for at in range(1, ways):
        total = total + slots[at]
    return total


def last_sum_kernel(
    bits, ways, part_ref, dots_ref, gains_ref, out_ref, dots_out_ref, gains_out_ref,
    sums, landed, dots_land, gains_land, gains_far, gains_mid, send_sem, recv_sem, dots_send, dots_recv,
    near_send, near_recv, far_send, far_recv,
):
    row_at = lax.axis_index("dp")
    me = lax.axis_index("tensor")
    pieces = 1 << bits

    def beside(there):
        return (row_at, there)

    def along(there):
        return (there, me)

    barrier = pltpu.get_barrier_semaphore()
    for step in range(1, pieces):
        pl.semaphore_signal(barrier, inc=1, device_id=beside(lax.rem(me + step, pieces)), device_id_type=MESH)
    for step in range(1, ways):
        pl.semaphore_signal(barrier, inc=1, device_id=along(lax.rem(row_at + step, ways)), device_id_type=MESH)
    pl.semaphore_wait(barrier, pieces + ways - 2)
    gains_land[me] = gains_ref[...]
    dots_land[me] = dots_ref[...]
    near = spread_kernel(gains_ref, gains_land, me, pieces, beside, near_send, near_recv)
    dots = spread_kernel(dots_ref, dots_land, me, pieces, beside, dots_send, dots_recv)
    for copy in near:
        copy.wait()
    gains_mid[...] = total_of(gains_land, pieces)
    gains_far[row_at] = gains_mid[...]
    far = spread_kernel(gains_mid, gains_far, row_at, ways, along, far_send, far_recv)
    tensor_sum_steps(bits, False, part_ref, out_ref, sums, landed, send_sem, recv_sem, None, None)
    for copy in dots:
        copy.wait()
    dots_out_ref[...] = total_of(dots_land, pieces)
    for copy in far:
        copy.wait()
    gains_out_ref[...] = total_of(gains_far, ways)


def last_sum(part, dots, gains, data_ways, collective_id):
    pieces, rows, width = part.shape
    bits = pieces.bit_length() - 1
    near = pltpu.SemaphoreType.DMA((pieces - 1,))
    far = pltpu.SemaphoreType.DMA((data_ways - 1,))
    return pl.pallas_call(
        functools.partial(last_sum_kernel, bits, data_ways),
        out_shape=(
            jax.ShapeDtypeStruct(part.shape[1:], part.dtype),
            jax.ShapeDtypeStruct(dots.shape, dots.dtype),
            jax.ShapeDtypeStruct(gains.shape, gains.dtype),
        ),
        in_specs=[pl.BlockSpec(memory_space=pltpu.VMEM)] * 3,
        out_specs=[pl.BlockSpec(memory_space=pltpu.VMEM)] * 3,
        scratch_shapes=[
            pltpu.VMEM(part.shape, part.dtype),
            pltpu.VMEM((pieces - 1, rows, width), part.dtype),
            pltpu.VMEM((pieces, *dots.shape), dots.dtype),
            pltpu.VMEM((pieces, *gains.shape), gains.dtype),
            pltpu.VMEM((data_ways, *gains.shape), gains.dtype),
            pltpu.VMEM(gains.shape, gains.dtype),
            *[pltpu.SemaphoreType.DMA((pieces - 1, SUM_BLOCKS))] * 2,
            near, near, near, near, far, far,
        ],
        compiler_params=pltpu.CompilerParams(
            collective_id=collective_id, has_side_effects=True, vmem_limit_bytes=32 * MIB
        ),
        cost_estimate=pl.CostEstimate(flops=0, bytes_accessed=128 * MIB, transcendentals=0),
    )(part, dots, gains)


def turned_by(values, signs):
    return pltpu.roll(values, values.shape[1] // 2, 1) * signs


def half_signs(head_dim, first):
    lanes = lax.broadcasted_iota(jnp.int32, (1, head_dim), 1)
    return jnp.where(lanes < head_dim // 2, first, -first)


def front_kernel(groups, head_dim, first, normed_ref, cos_ref, sin_ref, gains_ref, *refs):
    weights, raw_ref, outs = refs[:groups], refs[groups], refs[groups + 1 :]
    cosine = cos_ref[...]
    sine = sin_ref[...] * half_signs(head_dim, -1.0)
    for group in range(groups):
        pair = slice(group * 2 * head_dim, (group + 1) * 2 * head_dim)
        raw_ref[:, pair] = matmul(normed_ref[...], weights[group][...], NN)
        for at in range(2):
            base = (group * 2 + at) * head_dim
            raw = raw_ref[:, base : base + head_dim]
            if first + at < 3:
                gain = gains_ref[first // 2 : first // 2 + 1]
                scale = lax.rsqrt(jnp.mean(raw * raw, axis=1, keepdims=True) + EPSILON)
                raw = raw * scale * gain
                raw = raw * cosine + turned_by(raw, sine)
            out, place = (outs[group], at * head_dim) if first == 0 else (outs[0], base)
            out[:, place : place + head_dim] = raw.astype(out.dtype)


def front(normed, weight, groups, first, cosine, sine, gains, head_dim):
    rows, depth = normed.shape
    block = min(256, rows)
    width = groups * 2 * head_dim
    table = pl.BlockSpec((block, head_dim), lambda i: (i, 0))
    outs = [2 * head_dim] * groups if first == 0 else [width]

    def weight_spec(group):
        return pl.BlockSpec((depth, 2 * head_dim), lambda i: (0, 2 * group + first // 2), pipeline_mode=pl.Buffered(1))

    found = pl.pallas_call(
        functools.partial(front_kernel, groups, head_dim, first),
        grid=(rows // block,),
        in_specs=[pl.BlockSpec((block, depth), lambda i: (i, 0)), table, table, pl.BlockSpec(gains.shape, lambda i: (0, 0))]
        + [weight_spec(group) for group in range(groups)],
        out_specs=[pl.BlockSpec((block, columns), lambda i: (i, 0)) for columns in [width] + outs],
        out_shape=[jax.ShapeDtypeStruct((rows, width), jnp.float32)]
        + [jax.ShapeDtypeStruct((rows, columns), jnp.bfloat16) for columns in outs],
        compiler_params=pltpu.CompilerParams(vmem_limit_bytes=60 * MIB),
        cost_estimate=pl.CostEstimate(flops=2 * rows * depth * width, bytes_accessed=2 * depth * width, transcendentals=0),
    )(normed, cosine, sine, gains, *[weight] * groups)
    return found[0], found[1:]


def front_back_kernel(groups, head_dim, raw_query_ref, raw_key_ref, cos_ref, sin_ref, gains_ref, *refs):
    queries, keys = refs[:groups], refs[groups : 2 * groups]
    out_ref, sums_ref = refs[2 * groups :]

    @pl.when(pl.program_id(0) == 0)
    def _():
        sums_ref[...] = jnp.zeros_like(sums_ref)

    cosine = cos_ref[...]
    sine = sin_ref[...] * half_signs(head_dim, 1.0)
    for group in range(groups):
        for at in range(4):
            base = (group * 4 + at) * head_dim
            source = queries[group] if at < 2 else keys[group]
            grads = source[:, at % 2 * head_dim : (at % 2 + 1) * head_dim].astype(jnp.float32)
            if at < 3:
                gain = gains_ref[at // 2 : at // 2 + 1]
                place = (group * 2 + at % 2) * head_dim
                raw = (raw_query_ref if at < 2 else raw_key_ref)[:, place : place + head_dim]
                scale = lax.rsqrt(jnp.mean(raw * raw, axis=1, keepdims=True) + EPSILON)
                normal = raw * scale
                grads = grads * cosine + turned_by(grads, sine)
                sums_ref[at // 2 : at // 2 + 1] += jnp.sum(grads * normal, axis=0, keepdims=True)
                grads = grads * gain
                grads = scale * (grads - normal * jnp.mean(grads * normal, axis=1, keepdims=True))
            out_ref[:, base : base + head_dim] = grads.astype(out_ref.dtype)


def front_back(raw_queries, raw_keys, cosine, sine, gains, grad_queries, grad_kv, head_dim):
    rows, width = raw_queries.shape[0], 2 * raw_queries.shape[1]
    groups = width // (4 * head_dim)
    block = min(256, rows)
    half = pl.BlockSpec((block, width // 2), lambda i: (i, 0))
    narrow = pl.BlockSpec((block, 2 * head_dim), lambda i: (i, 0))
    table = pl.BlockSpec((block, head_dim), lambda i: (i, 0))
    wide = pl.BlockSpec((block, width), lambda i: (i, 0))
    return pl.pallas_call(
        functools.partial(front_back_kernel, groups, head_dim),
        grid=(rows // block,),
        in_specs=[half, half, table, table, pl.BlockSpec(gains.shape, lambda i: (0, 0))] + [narrow] * (2 * groups),
        out_specs=[wide, pl.BlockSpec((8, head_dim), lambda i: (0, 0))],
        out_shape=[
            jax.ShapeDtypeStruct((rows, width), jnp.bfloat16),
            jax.ShapeDtypeStruct((8, head_dim), jnp.float32),
        ],
        compiler_params=pltpu.CompilerParams(vmem_limit_bytes=60 * MIB),
        cost_estimate=pl.CostEstimate(flops=60 * rows * width, bytes_accessed=10 * rows * width, transcendentals=0),
    )(raw_queries, raw_keys, cosine, sine, gains, *grad_queries, *grad_kv)


def last_product_kernel(grad_ref, weight_ref, hidden_ref, scale_ref, gain_ref, out_ref, dots_ref, gain_out_ref):
    part = matmul(grad_ref[...], weight_ref[...], NT)
    out_ref[0] = part.astype(out_ref.dtype)
    product = part * (hidden_ref[...] * scale_ref[...])
    gain_out_ref[...] = jnp.sum(product, axis=0, keepdims=True)
    dots = jnp.sum(product * gain_ref[...], axis=1, keepdims=True)

    @pl.when(pl.program_id(0) == 0)
    def _():
        dots_ref[...] = dots

    @pl.when(pl.program_id(0) > 0)
    def _():
        dots_ref[...] += dots


def last_product(grads, weight, hidden, scale, gain, pieces):
    rows, width = grads.shape
    depth = weight.shape[0]
    block = depth // pieces // 2
    return pl.pallas_call(
        last_product_kernel,
        grid=(depth // block,),
        in_specs=[
            pl.BlockSpec((rows, width), lambda i: (0, 0), pipeline_mode=pl.Buffered(1)),
            pl.BlockSpec((block, width), lambda i: (i, 0)),
            pl.BlockSpec((rows, block), lambda i: (0, i)),
            pl.BlockSpec((rows, 1), lambda i: (0, 0)),
            pl.BlockSpec((1, block), lambda i: (0, i)),
        ],
        out_specs=[
            pl.BlockSpec((1, rows, block), lambda i: (i // 2, 0, i % 2)),
            pl.BlockSpec((rows, 1), lambda i: (0, 0)),
            pl.BlockSpec((1, block), lambda i: (0, i)),
        ],
        out_shape=[
            jax.ShapeDtypeStruct((pieces, rows, depth // pieces), jnp.bfloat16),
            jax.ShapeDtypeStruct((rows, 1), jnp.float32),
            jax.ShapeDtypeStruct((1, depth), jnp.float32),
        ],
        compiler_params=pltpu.CompilerParams(vmem_limit_bytes=60 * MIB),
        cost_estimate=pl.CostEstimate(flops=4 * rows * depth * width, bytes_accessed=2 * depth * width, transcendentals=0),
    )(grads, weight, hidden, scale, gain)


def resid_kernel(sum_ref, hidden_ref, gain_ref, resid_ref, normed_ref, normed_t_ref, scale_ref):
    total = jnp.concatenate([sum_ref[at] for at in range(sum_ref.shape[0])], axis=1)
    resid = hidden_ref[...] + total.astype(jnp.float32)
    scale = lax.rsqrt(jnp.mean(resid * resid, axis=1, keepdims=True) + EPSILON)
    normed = resid * scale * gain_ref[...]
    resid_ref[...] = resid
    scale_ref[...] = scale
    normed_ref[...] = normed.astype(normed_ref.dtype)
    normed_t_ref[...] = jnp.transpose(normed).astype(normed_t_ref.dtype)


def add_and_norm(total, hidden, gain):
    pieces, rows, width = total.shape
    depth = pieces * width
    block = min(256, rows)
    wide = pl.BlockSpec((block, depth), lambda i: (i, 0))
    return pl.pallas_call(
        resid_kernel,
        grid=(rows // block,),
        in_specs=[
            pl.BlockSpec((pieces, block, width), lambda i: (0, i, 0)),
            wide,
            pl.BlockSpec((1, depth), lambda i: (0, 0)),
        ],
        out_specs=[
            wide,
            wide,
            pl.BlockSpec((depth, block), lambda i: (0, i)),
            pl.BlockSpec((block, 1), lambda i: (i, 0)),
        ],
        out_shape=[
            jax.ShapeDtypeStruct((rows, depth), jnp.float32),
            jax.ShapeDtypeStruct((rows, depth), jnp.bfloat16),
            jax.ShapeDtypeStruct((depth, rows), jnp.bfloat16),
            jax.ShapeDtypeStruct((rows, 1), jnp.float32),
        ],
        compiler_params=pltpu.CompilerParams(vmem_limit_bytes=60 * MIB),
        cost_estimate=pl.CostEstimate(flops=10 * rows * depth, bytes_accessed=18 * rows * depth, transcendentals=0),
    )(total, hidden, gain)


def resid_back_kernel(sum_ref, cot_ref, resid_ref, scale_ref, gain_ref, grad_ref, rounded_ref, gain_out_ref):
    grads = jnp.concatenate([sum_ref[at] for at in range(sum_ref.shape[0])], axis=1).astype(jnp.float32)
    scale = scale_ref[...]
    normal = resid_ref[...] * scale
    sums = jnp.sum(grads * normal, axis=0, keepdims=True)
    grads = grads * gain_ref[...]
    grads = scale * (grads - normal * jnp.mean(grads * normal, axis=1, keepdims=True))
    grads = cot_ref[...].astype(jnp.float32) + grads
    grad_ref[...] = grads
    rounded_ref[...] = grads.astype(rounded_ref.dtype)

    @pl.when(pl.program_id(0) == 0)
    def _():
        gain_out_ref[...] = sums

    @pl.when(pl.program_id(0) > 0)
    def _():
        gain_out_ref[...] += sums


def norm_and_add_back(total, cotangent, resid, scale, gain):
    pieces, rows, width = total.shape
    depth = pieces * width
    block = min(256, rows)
    wide = pl.BlockSpec((block, depth), lambda i: (i, 0))
    whole = pl.BlockSpec((1, depth), lambda i: (0, 0))
    return pl.pallas_call(
        resid_back_kernel,
        grid=(rows // block,),
        in_specs=[
            pl.BlockSpec((pieces, block, width), lambda i: (0, i, 0)),
            wide,
            wide,
            pl.BlockSpec((block, 1), lambda i: (i, 0)),
            whole,
        ],
        out_specs=[wide, wide, whole],
        out_shape=[
            jax.ShapeDtypeStruct((rows, depth), jnp.float32),
            jax.ShapeDtypeStruct((rows, depth), jnp.bfloat16),
            jax.ShapeDtypeStruct((1, depth), jnp.float32),
        ],
        compiler_params=pltpu.CompilerParams(vmem_limit_bytes=60 * MIB),
        cost_estimate=pl.CostEstimate(flops=10 * rows * depth, bytes_accessed=16 * rows * depth, transcendentals=0),
    )(total, cotangent, resid, scale, gain)


def step_of(rate, weight, moment, average, gradient, outs):
    moment = MOMENTUM * moment + gradient
    weight = weight - rate * (gradient + MOMENTUM * moment)
    average = EMA_DECAY * average + (1.0 - EMA_DECAY) * weight
    for out, value in zip(outs, (weight, moment, average, average)):
        out[...] = value.astype(out.dtype)


def mlp_step_kernel(rate, steps_of, *refs):
    chunks = len(steps_of)
    grads, held, outs = refs[:chunks], refs[chunks : chunks + 6], refs[chunks + 6 :]
    begin = 0
    for chunk, steps in enumerate(steps_of):

        @pl.when((pl.program_id(0) >= begin) & (pl.program_id(0) < begin + steps))
        def _():
            both = grads[chunk][:2].astype(jnp.float32)
            step_of(rate, *(ref[...] for ref in held[:3]), both, outs[:4])
            down = jnp.transpose(grads[chunk][2].astype(jnp.float32))
            step_of(rate, *(ref[...] for ref in held[3:]), down, outs[4:])

        begin += steps


def mlp_step(rate, grads, gate_up, down):
    kinds, depth, _ = grads[0].shape
    block = min(FF_BLOCK, grads[0].shape[2])
    steps_of = [grad.shape[2] // block for grad in grads]

    def grad_spec(chunk):
        begin, last = sum(steps_of[:chunk]), steps_of[chunk] - 1
        return pl.BlockSpec((kinds, depth, block), lambda i: (0, 0, jnp.clip(i - begin, 0, last)))

    gate_up_spec = pl.BlockSpec((2, depth, block), lambda i: (0, 0, i))
    down_spec = pl.BlockSpec((block, depth), lambda i: (i, 0))
    types = (jnp.float32,) * 3 + (jnp.bfloat16,)
    return pl.pallas_call(
        functools.partial(mlp_step_kernel, rate, steps_of),
        grid=(sum(steps_of),),
        in_specs=[grad_spec(chunk) for chunk in range(len(grads))] + [gate_up_spec] * 3 + [down_spec] * 3,
        out_specs=[gate_up_spec] * 4 + [down_spec] * 4,
        out_shape=[jax.ShapeDtypeStruct(gate_up[0].shape, kind) for kind in types]
        + [jax.ShapeDtypeStruct(down[0].shape, kind) for kind in types],
        compiler_params=pltpu.CompilerParams(vmem_limit_bytes=40 * MIB),
        cost_estimate=pl.CostEstimate(flops=0, bytes_accessed=26 * sum(grad.size for grad in grads), transcendentals=0),
    )(*grads, *gate_up, *down)


def turned_step_kernel(rate, grad_ref, *refs):
    step_of(rate, *(ref[...] for ref in refs[:3]), jnp.transpose(grad_ref[...].astype(jnp.float32)), refs[3:])


def turned_step(rate, grad_t, held):
    types = (jnp.float32,) * 3 + (jnp.bfloat16,)
    return pl.pallas_call(
        functools.partial(turned_step_kernel, rate),
        in_specs=[pl.BlockSpec(memory_space=pltpu.VMEM)] * 4,
        out_specs=[pl.BlockSpec(memory_space=pltpu.VMEM)] * 4,
        out_shape=[jax.ShapeDtypeStruct(held[0].shape, kind) for kind in types],
        compiler_params=pltpu.CompilerParams(vmem_limit_bytes=60 * MIB),
        cost_estimate=pl.CostEstimate(flops=0, bytes_accessed=28 * grad_t.size, transcendentals=0),
    )(grad_t, *held)


def out_product_kernel(left_ref, weight_ref, out_ref):
    out_ref[0] = matmul(left_ref[...], weight_ref[...], NT).astype(out_ref.dtype)


def out_product(left, weight, column, pieces):
    rows, width = left.shape
    depth = weight.shape[0]
    block = depth // pieces // 2
    return pl.pallas_call(
        out_product_kernel,
        grid=(depth // block,),
        in_specs=[
            pl.BlockSpec((rows, width), lambda i: (0, 0), pipeline_mode=pl.Buffered(1)),
            pl.BlockSpec((block, width), lambda i: (i, column)),
        ],
        out_specs=pl.BlockSpec((1, rows, block), lambda i: (i // 2, 0, i % 2)),
        out_shape=jax.ShapeDtypeStruct((pieces, rows, depth // pieces), jnp.bfloat16),
        compiler_params=pltpu.CompilerParams(vmem_limit_bytes=60 * MIB),
        cost_estimate=pl.CostEstimate(flops=2 * rows * depth * width, bytes_accessed=2 * depth * width, transcendentals=0),
    )(left, weight)


def weight_products_kernel(normed_ref, grad_ref, left_ref, mixed_ref, out_ref):
    width = grad_ref.shape[1]
    out_ref[:, :width] = matmul(normed_ref[...], grad_ref[...], TN).astype(out_ref.dtype)
    out_ref[:, width:] = matmul(left_ref[...], mixed_ref[...], TN).astype(out_ref.dtype)


def weight_products(normed, grads, left, mixed):
    rows, depth = normed.shape
    block = min(256, depth)
    width = grads.shape[1] + mixed.shape[1]
    column = pl.BlockSpec((rows, block), lambda i: (0, i))

    def held(array):
        return pl.BlockSpec(array.shape, lambda i: (0, 0), pipeline_mode=pl.Buffered(1))

    return pl.pallas_call(
        weight_products_kernel,
        grid=(depth // block,),
        in_specs=[column, held(grads), column, held(mixed)],
        out_specs=pl.BlockSpec((block, width), lambda i: (i, 0)),
        out_shape=jax.ShapeDtypeStruct((depth, width), jnp.bfloat16),
        compiler_params=pltpu.CompilerParams(vmem_limit_bytes=60 * MIB),
        cost_estimate=pl.CostEstimate(flops=2 * rows * depth * width, bytes_accessed=2 * depth * width, transcendentals=0),
    )(normed, grads, left, mixed)


def rms_scale(values_in):
    return lax.rsqrt(jnp.mean(values_in * values_in, axis=-1, keepdims=True) + EPSILON)


def rope_tables(offsets, head_dim):
    half_dim = head_dim // 2
    frequency = 1.0 / ROPE_BASE ** (jnp.arange(half_dim, dtype=jnp.float32) * 2.0 / head_dim)
    angles = offsets.astype(jnp.float32)[:, None] * frequency[None, :]
    cosine = jnp.cos(angles)
    sine = jnp.sin(angles)
    return (jnp.concatenate([cosine, cosine], axis=-1), jnp.concatenate([sine, sine], axis=-1))


def nesterov(weight, moment, average, gradient, rate):
    new_moment = MOMENTUM * moment + gradient
    new_weight = weight - rate * (gradient + MOMENTUM * new_moment)
    new_average = EMA_DECAY * average + (1.0 - EMA_DECAY) * new_weight
    return (new_weight, new_moment, new_average, new_average.astype(jnp.bfloat16))


def dot(a, b, dims):
    return lax.dot_general(a, b, dims, preferred_element_type=jnp.float32)


def tie(*values):
    return lax.optimization_barrier(values)


def local(
    hidden_in,
    cotangent,
    doc_lengths,
    valid_mask,
    w_qkv,
    w_out,
    w_gate_up,
    w_down,
    norm_gains,
    m_qkv,
    m_out,
    m_gate_up,
    m_down,
    m_gains,
    a_qkv,
    a_out,
    a_gate_up,
    a_down,
    a_gains,
):
    row_count, model_dim = hidden_in.shape
    head_dim = (norm_gains.shape[0] - 2 * model_dim) // 2
    data_ways = lax.axis_size("dp")
    tensor_ways = lax.axis_size("tensor")
    tensor_at = lax.axis_index("tensor")
    tokens_all = row_count * data_ways
    width_cols = model_dim // tensor_ways
    col_begin = tensor_at * width_cols
    groups = w_qkv.shape[1] // (4 * head_dim)
    ff_local = w_down.shape[0]
    ff_unit = ff_local // CHUNK_ENDS[-1]
    bf16 = jnp.bfloat16
    f32 = jnp.float32

    def columns_of(values_in):
        return lax.dynamic_slice_in_dim(values_in, col_begin, width_cols, values_in.ndim - 1)

    qkv_cols, out_rows = w_qkv.shape[1], w_out.shape[0]
    qkv_out = lax.all_gather(jnp.concatenate([w_qkv, w_out.T], axis=1).astype(bf16), "dp", axis=0, tiled=True)

    ends_at = jnp.cumsum(doc_lengths)
    starts_at = ends_at - doc_lengths
    place_begin = lax.axis_index("dp") * row_count
    places = place_begin + jnp.arange(row_count, dtype=jnp.int32)
    doc_ids = jnp.sum((places[:, None] >= ends_at[None, :]).astype(jnp.int32), axis=1)
    owned = doc_ids[:, None] == jnp.arange(doc_lengths.shape[0], dtype=jnp.int32)[None, :]
    doc_begin = jnp.sum(jnp.where(owned, starts_at[None, :], 0), axis=1)
    cosine, sine = rope_tables(places - doc_begin, head_dim)
    query_rows = min(512, row_count)
    blocks = row_count // query_rows
    bounds = jnp.stack(
        [
            place_begin + jnp.arange(blocks, dtype=jnp.int32) * query_rows,
            doc_begin[::query_rows],
            doc_begin[query_rows - 1 :: query_rows],
        ]
    ).astype(jnp.int32)
    begin_rows = doc_begin.astype(jnp.int32).reshape(blocks, 1, query_rows)

    gain_attn = norm_gains[:model_dim]
    gain_mlp = norm_gains[model_dim : 2 * model_dim]
    gain_query = norm_gains[2 * model_dim : 2 * model_dim + head_dim]
    gain_key = norm_gains[2 * model_dim + head_dim :]
    scale_one = rms_scale(hidden_in)
    normal_one = hidden_in * scale_one
    normed_one_b = (normal_one * gain_attn).astype(bf16)
    gains_two = jnp.stack([gain_query, gain_key])
    raw_keys, (kv_local,) = front(
        normed_one_b, qkv_out, groups, 2, cosine, sine, gains_two, head_dim
    )
    normed_one_b, kv_local = tie(normed_one_b, kv_local)
    kv_every = lax.all_gather(kv_local, "dp", axis=0, tiled=True)
    raw_queries, queries = front(
        normed_one_b, qkv_out, groups, 0, cosine, sine, gains_two, head_dim
    )

    down_t = w_down.T

    def chunk_shard(chunk):
        units = slice(CHUNK_ENDS[chunk] * ff_unit, CHUNK_ENDS[chunk + 1] * ff_unit)
        return jnp.stack([w_gate_up[0, :, units], w_gate_up[1, :, units], down_t[:, units]]).astype(bf16)

    def chunk_gather(shard):
        return lax.all_gather(shard, "dp", axis=0)

    shard, kv_every, cotangent_t, queries = tie(chunk_shard(0), kv_every, cotangent.T, queries)
    chunk_weights = [chunk_gather(shard)]
    mixed, totals = [], []
    for group in range(groups):
        mixed_rows, total_rows = attend(
            bounds, queries[group], begin_rows, kv_every, group, head_dim, query_rows, min(1024, tokens_all)
        )
        mixed.append(mixed_rows)
        totals.append(total_rows)
    mixed_b = jnp.concatenate(mixed, axis=1)
    attn_part = out_product(mixed_b, qkv_out, qkv_cols // out_rows, tensor_ways)
    shard, chunk_weights[0], attn_part = tie(chunk_shard(1), chunk_weights[0], attn_part)
    chunk_weights.append(chunk_gather(shard))
    attn_sum = tensor_sum(attn_part, 0)
    resid_one, normed_two_b, normed_two_t, scale_two = add_and_norm(attn_sum, hidden_in, gain_mlp[None])

    weight_grads, hiddens, back_pairs = [], [], []
    for weights in chunk_weights:
        hidden_b, gate_grad, up_grad, weight_grad = mlp_chunk(
            normed_two_b, cotangent, normed_two_t, cotangent_t, weights
        )
        hiddens.append((hidden_b,))
        back_pairs.append((gate_grad, up_grad))
        weight_grads.append(lax.psum_scatter(weight_grad, "dp", scatter_dimension=0))

    part_two = back_product(back_pairs, chunk_weights, 0, tensor_ways)
    part_two_sum, weight_grads[0] = tie(tensor_sum(part_two, 1), weight_grads[0])
    grad_resid, grad_attn_b, gain_mlp_part = norm_and_add_back(
        part_two_sum, cotangent, resid_one, scale_two, gain_mlp[None]
    )
    grad_mixed_b = dot(grad_attn_b, qkv_out[:, qkv_cols:], NN).astype(bf16)

    grad_queries, kv_sums = [], []
    for group in range(groups):
        grad_rows = grad_mixed_b[:, group * 2 * head_dim : (group + 1) * 2 * head_dim]
        if group and group == groups - 1:
            grad_rows, weight_grads[1], kv_sums[-1] = tie(grad_rows, weight_grads[1], kv_sums[-1])
        grad_query, kv_sum = attend_back(
            bounds,
            queries[group],
            grad_rows,
            mixed[group],
            totals[group],
            begin_rows,
            kv_every,
            group,
            head_dim,
            query_rows,
            min(512, tokens_all),
        )
        grad_queries.append(grad_query)
        kv_sums.append(kv_sum)
    kv_grads = []
    for group in range(groups):
        if group:
            kv_grads[-1], kv_sums[group] = tie(kv_grads[-1], kv_sums[group])
        kv_grads.append(lax.psum_scatter(kv_sums[group], "dp", scatter_dimension=0, tiled=True))
    hidden_b, grad_queries[-1] = tie(hiddens[0][0], grad_queries[-1])
    mlp_part = back_product([(hidden_b,), *hiddens[1:]], chunk_weights, 2, tensor_ways)
    rate_matrix = LR_MATRIX / math.sqrt(tokens_all)
    mlp_sum = tensor_sum(mlp_part, 2, False)
    updates = (
        *mlp_step(rate_matrix, weight_grads, (w_gate_up, m_gate_up, a_gate_up), (w_down, m_down, a_down)),
    )
    mlp_cols = mlp_sum.astype(f32)
    resid_cols = columns_of(resid_one)
    attn_cols = lax.dynamic_index_in_dim(attn_sum, tensor_at, 0, False).astype(f32)
    mask_rows = valid_mask.astype(f32)[:, None]
    stats_part = [
        jnp.sum(mask_rows * columns * columns) for columns in (columns_of(hidden_in), attn_cols, mlp_cols)
    ]
    stats_part.append(jnp.where(tensor_at == 0, jnp.sum(valid_mask.astype(f32)), 0.0))
    gain_mlp_wide = lax.dynamic_update_slice_in_dim(
        jnp.zeros((model_dim,), f32), columns_of(gain_mlp_part[0]), col_begin, 0
    )
    mixed_cols, gain_mlp_wide, stats_part, kv_grads[-1], updates = tie(
        resid_cols + mlp_cols, gain_mlp_wide, jnp.stack(stats_part), kv_grads[-1], updates
    )
    grad_projected_b, gains_found = front_back(
        raw_queries, raw_keys, cosine, sine, gains_two, grad_queries, kv_grads, head_dim
    )
    both_grads, grad_projected_b = tie(
        weight_products(normed_one_b, grad_projected_b, grad_attn_b, mixed_b), grad_projected_b
    )
    both_shard = lax.psum_scatter(both_grads, "dp", scatter_dimension=0, tiled=True)
    qkv_shard = both_shard[:, :qkv_cols].astype(f32)
    part_one, dots_part, gain_attn_part = last_product(
        grad_projected_b, qkv_out, hidden_in, scale_one, gain_attn[None], tensor_ways
    )

    gains_part = jnp.concatenate(
        [gain_attn_part[0], gain_mlp_wide, gains_found[0], gains_found[1], stats_part]
    )
    gains_count = gains_part.shape[0]
    gains_rows = -(-gains_count // 1024) * 8
    gains_part = jnp.pad(gains_part, (0, gains_rows * 128 - gains_count)).reshape(gains_rows, 128)
    grad_one_cols, row_dots, gains_sum = last_sum(
        part_one, dots_part.reshape(row_count // 128, 128), gains_part, data_ways, 3
    )
    gains_sum = gains_sum.reshape(-1)[:gains_count]
    grad_cols = columns_of(grad_resid) + scale_one * (
        grad_one_cols.astype(f32) * columns_of(gain_attn)
        - columns_of(normal_one) * (row_dots.reshape(row_count, 1) / model_dim)
    )
    grad_gains = gains_sum[: norm_gains.shape[0]]
    stats_sum = gains_sum[norm_gains.shape[0] :]
    branch_rms = jnp.sqrt(stats_sum[:3] / (stats_sum[3] * model_dim))

    rate_gain = LR_GAIN / math.sqrt(tokens_all)
    return (
        mixed_cols,
        grad_cols,
        branch_rms,
        *nesterov(w_qkv, m_qkv, a_qkv, qkv_shard, rate_matrix),
        *turned_step(rate_matrix, both_shard[:, qkv_cols:], (w_out, m_out, a_out)),
        *updates,
        *nesterov(norm_gains, m_gains, a_gains, grad_gains, rate_gain),
    )


def solution(mesh):
    rows = P("dp", None)
    spread = P("dp", "tensor")
    turned = P("tensor", "dp")
    stacked = P(None, "dp", "tensor")
    matrices = (spread, turned, stacked, turned, P())
    in_specs = (rows, rows, P(), P("dp"), *matrices, *matrices, *matrices)
    out_specs = (spread, spread, P(), *(spec for spec in matrices for _ in range(4)))
    return jax.shard_map(local, mesh=mesh, in_specs=in_specs, out_specs=out_specs, check_vma=False)
```

```python
import functools, math
import jax, jax.numpy as jnp
from jax import lax
from jax.experimental import pallas as pl
from jax.experimental.pallas import tpu as pltpu
NT = (((1,), (1,)), ((), ()))
NN = (((1,), (0,)), ((), ()))
TN = (((0,), (0,)), ((), ()))
NEG_FILL = -1e30
LOG2E = math.log2(math.e)
MIB = 1024 * 1024

def matmul(a, b, dims):
    return lax.dot_general(a, b, dims, preferred_element_type=jnp.float32)

def row_of(column):
    return jnp.transpose(jnp.broadcast_to(column, (column.shape[0], 128)))[:1]

def attend_kernel(head_dim, key_rows, bound_ref, query_ref, begin_ref, kv_ref, out_ref, total_ref, q_two, accum):
    rows = query_ref.shape[0]
    block = pl.program_id(0)
    first = bound_ref[0, block]
    begin_first = bound_ref[1, block]
    begin_last = bound_ref[2, block]
    scale = LOG2E * head_dim**-0.5
    q_two[:rows] = query_ref[:, :head_dim]
    q_two[rows:] = query_ref[:, head_dim:]
    places = first + lax.broadcasted_iota(jnp.int32, (1, rows), 1)
    places = jnp.concatenate([places, places], axis=1)
    begins = jnp.concatenate([begin_ref[0], begin_ref[0]], axis=1)

    def step(masked, index, carry):
        top, total = carry
        key_begin = pl.multiple_of(index * key_rows, key_rows)
        keys = kv_ref[pl.ds(key_begin, key_rows), :head_dim]
        values = kv_ref[pl.ds(key_begin, key_rows), head_dim:]
        raw = matmul(keys, q_two[...], NT) * scale
        if masked:
            key_places = key_begin + lax.broadcasted_iota(jnp.int32, (key_rows, 1), 0)
            allowed = (key_places >= begins) & (key_places <= places)
            raw = jnp.where(allowed, raw, NEG_FILL)
        new_top = jnp.maximum(top, jnp.max(raw, axis=0, keepdims=True))
        probs = jnp.exp2(raw - new_top)
        fade = jnp.exp2(top - new_top)
        total = total * fade + jnp.sum(probs, axis=0, keepdims=True)
        accum[...] = accum[...] * fade + matmul(values, probs.astype(jnp.bfloat16), TN)
        return (new_top, total)

    def either(index, carry):
        key_begin = index * key_rows
        plain = (key_begin >= begin_last) & (key_begin + key_rows - 1 <= first)
        return lax.cond(
            plain, functools.partial(step, False, index), functools.partial(step, True, index), carry
        )

    accum[...] = jnp.zeros_like(accum)
    start = (
        jnp.full((1, 2 * rows), NEG_FILL, jnp.float32),
        jnp.zeros((1, 2 * rows), jnp.float32),
    )
    low = begin_first // key_rows
    high = (first + rows - 1) // key_rows + 1
    top, total = lax.fori_loop(low, high, either, start)
    out = jnp.transpose(accum[...] / total)
    out_ref[:, :head_dim] = out[:rows].astype(out_ref.dtype)
    out_ref[:, head_dim:] = out[rows:].astype(out_ref.dtype)
    total_ref[0] = top + jnp.log2(total)

def attend(bounds, queries, begins, kv_all, group, head_dim, query_rows, key_rows):
    rows = queries.shape[0]
    blocks = rows // query_rows
    return pl.pallas_call(
        functools.partial(attend_kernel, head_dim, key_rows),
        out_shape=(jax.ShapeDtypeStruct(queries.shape, jnp.bfloat16), jax.ShapeDtypeStruct((blocks, 1, 2 * query_rows), jnp.float32)),
        grid_spec=pltpu.PrefetchScalarGridSpec(
            num_scalar_prefetch=1,
            grid=(blocks,),
            in_specs=[
                pl.BlockSpec((query_rows, 2 * head_dim), lambda i, *_: (i, 0)),
                pl.BlockSpec((1, 1, query_rows), lambda i, *_: (i, 0, 0)),
                pl.BlockSpec((kv_all.shape[0], 2 * head_dim), lambda i, *_: (0, group)),
            ],
            out_specs=[
                pl.BlockSpec((query_rows, 2 * head_dim), lambda i, *_: (i, 0)),
                pl.BlockSpec((1, 1, 2 * query_rows), lambda i, *_: (i, 0, 0)),
            ],
            scratch_shapes=[pltpu.VMEM((2 * query_rows, head_dim), jnp.bfloat16), pltpu.VMEM((head_dim, 2 * query_rows), jnp.float32)],
        ),
        compiler_params=pltpu.CompilerParams(vmem_limit_bytes=60 * MIB),
        cost_estimate=pl.CostEstimate(flops=8 * rows * kv_all.shape[0] * head_dim, bytes_accessed=2 * kv_all.size, transcendentals=2 * rows * kv_all.shape[0]),
    )(bounds, queries, begins, kv_all)

def attend_back_kernel(head_dim, key_rows, bound_ref, query_ref, grad_ref, out_ref, total_ref, begin_ref, kv_ref, grad_q_ref, grad_kv_ref, q_two, g_two, dq_two, kv_sum):
    rows = query_ref.shape[0]
    block = pl.program_id(0)
    first = bound_ref[0, block]
    begin_first = bound_ref[1, block]
    begin_last = bound_ref[2, block]
    unit = head_dim**-0.5
    scale = LOG2E * unit

    @pl.when(block == 0)
    def _():
        kv_sum[...] = jnp.zeros_like(kv_sum)

    for half in range(2):
        part = slice(half * rows, (half + 1) * rows)
        cols = slice(half * head_dim, (half + 1) * head_dim)
        q_two[part] = query_ref[:, cols]
        g_two[part] = grad_ref[:, cols]
    dq_two[...] = jnp.zeros_like(dq_two)
    product = grad_ref[...].astype(jnp.float32) * out_ref[...].astype(jnp.float32)
    delta = jnp.concatenate(
        [
            row_of(jnp.sum(product[:, :head_dim], axis=1, keepdims=True)),
            row_of(jnp.sum(product[:, head_dim:], axis=1, keepdims=True)),
        ],
        axis=1,
    )
    totals = total_ref[0]
    places = first + lax.broadcasted_iota(jnp.int32, (1, rows), 1)
    places = jnp.concatenate([places, places], axis=1)
    begins = jnp.concatenate([begin_ref[0], begin_ref[0]], axis=1)

    def step(masked, index):
        key_begin = pl.multiple_of(index * key_rows, key_rows)
        place = pl.ds(key_begin, key_rows)
        keys = kv_ref[place, :head_dim]
        values = kv_ref[place, head_dim:]
        raw = matmul(keys, q_two[...], NT)
        probs = jnp.exp2(raw * scale - totals)
        if masked:
            key_places = key_begin + lax.broadcasted_iota(jnp.int32, (key_rows, 1), 0)
            allowed = (key_places >= begins) & (key_places <= places)
            probs = jnp.where(allowed, probs, 0.0)
        kv_sum[place, head_dim:] += matmul(probs.astype(jnp.bfloat16), g_two[...], NN)
        grad_probs = matmul(values, g_two[...], NT)
        grad_scores = (probs * (grad_probs - delta)).astype(jnp.bfloat16)
        kv_sum[place, :head_dim] += matmul(grad_scores, q_two[...], NN)
        dq_two[...] += matmul(grad_scores, keys, TN)

    def either(index, carry):
        key_begin = index * key_rows
        plain = (key_begin >= begin_last) & (key_begin + key_rows - 1 <= first)

        @pl.when(plain)
        def _():
            step(False, index)

        @pl.when(jnp.logical_not(plain))
        def _():
            step(True, index)

        return carry

    low = begin_first // key_rows
    high = (first + rows - 1) // key_rows + 1
    lax.fori_loop(low, high, either, 0)
    grad_q_ref[:, :head_dim] = (dq_two[:rows] * unit).astype(grad_q_ref.dtype)
    grad_q_ref[:, head_dim:] = (dq_two[rows:] * unit).astype(grad_q_ref.dtype)

    @pl.when(block == pl.num_programs(0) - 1)
    def _():
        grad_kv_ref[:, :head_dim] = (kv_sum[:, :head_dim] * unit).astype(grad_kv_ref.dtype)
        grad_kv_ref[:, head_dim:] = kv_sum[:, head_dim:].astype(grad_kv_ref.dtype)

def attend_back(bounds, queries, grads, outs, totals, begin_rows, kv_all, group, head_dim, query_rows, key_rows):
    rows = queries.shape[0]
    blocks = rows // query_rows
    wide = pl.BlockSpec((query_rows, 2 * head_dim), lambda i, *_: (i, 0))
    kv_shape = (kv_all.shape[0], 2 * head_dim)
    whole = pl.BlockSpec(kv_shape, lambda i, *_: (0, 0))
    return pl.pallas_call(
        functools.partial(attend_back_kernel, head_dim, key_rows),
        out_shape=(jax.ShapeDtypeStruct(queries.shape, jnp.float32), jax.ShapeDtypeStruct(kv_shape, jnp.bfloat16)),
        grid_spec=pltpu.PrefetchScalarGridSpec(
            num_scalar_prefetch=1,
            grid=(blocks,),
            in_specs=[wide, wide, wide,
                pl.BlockSpec((1, 1, 2 * query_rows), lambda i, *_: (i, 0, 0)),
                pl.BlockSpec((1, 1, query_rows), lambda i, *_: (i, 0, 0)),
                pl.BlockSpec(kv_shape, lambda i, *_: (0, group))],
            out_specs=[wide, whole],
            scratch_shapes=[pltpu.VMEM((2 * query_rows, head_dim), jnp.bfloat16)] * 2
            + [pltpu.VMEM((2 * query_rows, head_dim), jnp.float32), pltpu.VMEM(kv_shape, jnp.float32)],
        ),
        compiler_params=pltpu.CompilerParams(vmem_limit_bytes=60 * MIB),
        cost_estimate=pl.CostEstimate(flops=20 * rows * kv_all.shape[0] * head_dim, bytes_accessed=2 * kv_all.size, transcendentals=2 * rows * kv_all.shape[0]),
    )(bounds, queries, grads, outs, totals, begin_rows, kv_all)


from jax.sharding import PartitionSpec as P

EPSILON = 1e-06
ROPE_BASE = 1000000.0
MOMENTUM = 0.5
EMA_DECAY = 0.5
LR_MATRIX = 0.08
LR_GAIN = 0.5
FF_BLOCK = 256
CHUNK_ENDS = (0, 1, 3)


def mlp_kernel(normed_ref, cot_ref, normed_t_ref, cot_t_ref, weight_ref, hidden_ref, gate_grad_ref, up_grad_ref, grads_ref, wide):
    ways, kinds, shard, _ = weight_ref.shape
    rows = normed_ref.shape[0]
    row_tile = min(512, rows)

    for at in range(ways):
        wide[:, at * shard : (at + 1) * shard, :] = weight_ref[at]

    @pl.loop(0, rows // row_tile)
    def _(tile):
        place = pl.ds(pl.multiple_of(tile * row_tile, row_tile), row_tile)
        x = normed_ref[place, :]
        gate = matmul(x, wide[0], NN)
        up = matmul(x, wide[1], NN)
        grad_hidden = matmul(cot_ref[place, :], wide[2], NN)
        sigmoid = 1.0 / (1.0 + jnp.exp(-gate))
        silu = gate * sigmoid
        hidden_ref[place, :] = (silu * up).astype(hidden_ref.dtype)
        gate_grad_ref[place, :] = (
            grad_hidden * up * (sigmoid * (1.0 + gate * (1.0 - sigmoid)))
        ).astype(gate_grad_ref.dtype)
        up_grad_ref[place, :] = (grad_hidden * silu).astype(up_grad_ref.dtype)

    for at in range(ways):
        place = slice(at * shard, (at + 1) * shard)
        left = normed_t_ref[place, :]
        grads_ref[at, 0] = matmul(left, gate_grad_ref[...], NN).astype(grads_ref.dtype)
        grads_ref[at, 1] = matmul(left, up_grad_ref[...], NN).astype(grads_ref.dtype)
        grads_ref[at, 2] = matmul(cot_t_ref[place, :], hidden_ref[...], NN).astype(grads_ref.dtype)


def mlp_chunk(normed, cotangent, normed_t, cotangent_t, weights):
    ways, _, shard, width = weights.shape
    rows, depth = normed.shape
    block = min(FF_BLOCK, width)

    def held(array):
        return pl.BlockSpec(array.shape, lambda i: (0, 0), pipeline_mode=pl.Buffered(1))

    weight_spec = pl.BlockSpec((ways, 3, shard, block), lambda i: (0, 0, 0, i))
    row_spec = pl.BlockSpec((rows, block), lambda i: (0, i))
    row_shape = jax.ShapeDtypeStruct((rows, width), jnp.bfloat16)
    return pl.pallas_call(
        mlp_kernel,
        grid=(width // block,),
        in_specs=[held(normed), held(cotangent), held(normed_t), held(cotangent_t), weight_spec],
        out_specs=[row_spec, row_spec, row_spec, weight_spec],
        out_shape=(row_shape, row_shape, row_shape, jax.ShapeDtypeStruct((ways, 3, shard, width), jnp.bfloat16)),
        scratch_shapes=[pltpu.VMEM((3, depth, block), jnp.bfloat16)],
        compiler_params=pltpu.CompilerParams(vmem_limit_bytes=60 * MIB),
        cost_estimate=pl.CostEstimate(flops=24 * rows * depth * width, bytes_accessed=12 * depth * width, transcendentals=rows * width),
    )(normed, cotangent, normed_t, cotangent_t, weights)


def back_product_kernel(kinds, *refs):
    out_ref = refs[-1]
    total = None
    chunks = (len(refs) - 1) // (kinds + 1)
    for chunk in range(chunks):
        weight_ref = refs[chunk * (kinds + 1) + kinds]
        for kind in range(kinds):
            part = matmul(refs[chunk * (kinds + 1) + kind][...], weight_ref[0, kind], NT)
            total = part if total is None else total + part
    out_ref[0] = total.astype(out_ref.dtype)


def back_product(groups_of, weights, kind_begin, pieces):
    kinds = len(groups_of[0])
    ways, _, shard, width = weights[0].shape
    rows = groups_of[0][0].shape[0]
    per_piece = ways // pieces
    args, specs = [], []
    for lefts, weight in zip(groups_of, weights):
        for left in lefts:
            args.append(left)
            specs.append(pl.BlockSpec(left.shape, lambda i: (0, 0), pipeline_mode=pl.Buffered(1)))
        args.append(weight)
        specs.append(pl.BlockSpec((1, kinds, shard, weight.shape[3]), lambda i: (i, kind_begin // kinds, 0, 0)))
    return pl.pallas_call(
        functools.partial(back_product_kernel, kinds),
        grid=(ways,),
        in_specs=specs,
        out_specs=pl.BlockSpec((1, rows, shard), lambda i: (i // per_piece, 0, i % per_piece)),
        out_shape=jax.ShapeDtypeStruct((pieces, rows, per_piece * shard), jnp.bfloat16),
        compiler_params=pltpu.CompilerParams(vmem_limit_bytes=60 * MIB),
        cost_estimate=pl.CostEstimate(flops=2 * len(weights) * kinds * rows * width * ways * shard, bytes_accessed=2 * len(weights) * kinds * width * ways * shard, transcendentals=0),
    )(*args)


MESH = pl.DeviceIdType.MESH
SUM_BLOCKS = 4


def flip(index, bit):
    unit = 1 << bit
    return index + unit - 2 * unit * ((index // unit) % 2)


def picks(index, fixed, free):
    base = 0
    for bit in fixed:
        unit = 1 << bit
        base = base + unit * ((index // unit) % 2)
    found = []
    for choice in range(1 << len(free)):
        offset = sum((1 << bit) for at, bit in enumerate(free) if (choice >> at) & 1)
        found.append(base + offset)
    return found


def tensor_sum_kernel(bits, whole, part_ref, out_ref, sums, landed, send_sem, recv_sem, send_out, recv_out):
    row_at = lax.axis_index("dp")
    me = lax.axis_index("tensor")
    barrier = pltpu.get_barrier_semaphore()
    for bit in range(bits):
        pl.semaphore_signal(barrier, inc=1, device_id=(row_at, flip(me, bit)), device_id_type=MESH)
    pl.semaphore_wait(barrier, bits)
    tensor_sum_steps(bits, whole, part_ref, out_ref, sums, landed, send_sem, recv_sem, send_out, recv_out)


def tensor_sum_steps(bits, whole, part_ref, out_ref, sums, landed, send_sem, recv_sem, send_out, recv_out):
    row_at = lax.axis_index("dp")
    me = lax.axis_index("tensor")
    rows = part_ref.shape[1] // SUM_BLOCKS
    orders = [list(range(bits)) if b % 2 == 0 else list(range(bits))[::-1] for b in range(SUM_BLOCKS)]

    def place(block):
        return pl.ds(block * rows, rows)

    def scatter(block, step):
        order = orders[block]
        bit = order[step]
        there = flip(me, bit)
        free = order[step + 1 :]
        source = part_ref if step == 0 else sums
        base = (1 << bits) - (1 << (bits - step))
        copies = []
        for at, piece in enumerate(picks(there, order[: step + 1], free)):
            slot = base + at
            copies.append(
                pltpu.make_async_remote_copy(
                    src_ref=source.at[piece, place(block)],
                    dst_ref=landed.at[slot, place(block)],
                    send_sem=send_sem.at[slot, block],
                    recv_sem=recv_sem.at[slot, block],
                    device_id=(row_at, there),
                    device_id_type=MESH,
                )
            )
        return copies

    def gather(block, step):
        order = orders[block][::-1]
        bit = order[step]
        there = flip(me, bit)
        base = (1 << step) - 1
        copies = []
        for at, piece in enumerate(picks(me, order[step:], order[:step])):
            slot = base + at
            copies.append(
                pltpu.make_async_remote_copy(
                    src_ref=out_ref.at[piece, place(block)],
                    dst_ref=out_ref.at[piece, place(block)],
                    send_sem=send_out.at[slot, block],
                    recv_sem=recv_out.at[slot, block],
                    device_id=(row_at, there),
                    device_id_type=MESH,
                )
            )
        return copies

    every = []
    flying = []
    for block in range(SUM_BLOCKS):
        copies = scatter(block, 0)
        for copy in copies:
            copy.start()
        flying.append(copies)
    for step in range(bits):
        for block in range(SUM_BLOCKS):
            order = orders[block]
            base = (1 << bits) - (1 << (bits - step))
            for copy in flying[block]:
                copy.wait_recv()
            every += flying[block]
            source = part_ref if step == 0 else sums
            last = step == bits - 1
            for at, piece in enumerate(picks(me, order[: step + 1], order[step + 1 :])):
                total = source[piece, place(block)].astype(jnp.float32) + landed[base + at, place(block)].astype(jnp.float32)
                if not last:
                    sums[piece, place(block)] = total.astype(sums.dtype)
                elif whole:
                    out_ref[piece, place(block)] = total.astype(out_ref.dtype)
                else:
                    out_ref[place(block)] = total.astype(out_ref.dtype)
            if not last:
                flying[block] = scatter(block, step + 1)
            elif whole:
                flying[block] = gather(block, 0)
            if not last or whole:
                for copy in flying[block]:
                    copy.start()
    if whole:
        for step in range(bits):
            for block in range(SUM_BLOCKS):
                for copy in flying[block]:
                    copy.wait_recv()
                every += flying[block]
                if step < bits - 1:
                    flying[block] = gather(block, step + 1)
                    for copy in flying[block]:
                        copy.start()
    for copy in every:
        copy.wait_send()


def tensor_sum(part, collective_id, whole=True):
    ways, rows, width = part.shape
    bits = ways.bit_length() - 1
    return pl.pallas_call(
        functools.partial(tensor_sum_kernel, bits, whole),
        out_shape=jax.ShapeDtypeStruct(part.shape if whole else part.shape[1:], part.dtype),
        in_specs=[pl.BlockSpec(memory_space=pltpu.VMEM)],
        out_specs=pl.BlockSpec(memory_space=pltpu.VMEM),
        scratch_shapes=[
            pltpu.VMEM(part.shape, part.dtype),
            pltpu.VMEM((ways - 1, rows, width), part.dtype),
            *[pltpu.SemaphoreType.DMA((ways - 1, SUM_BLOCKS))] * 4,
        ],
        compiler_params=pltpu.CompilerParams(
            collective_id=collective_id, has_side_effects=True, vmem_limit_bytes=32 * MIB
        ),
        cost_estimate=pl.CostEstimate(flops=0, bytes_accessed=(256 if whole else 128) * MIB, transcendentals=0),
    )(part)


def spread_kernel(source, slots, me, ways, place, send_sem, recv_sem):
    copies = []
    for step in range(1, ways):
        there = lax.rem(me + step, ways)
        copies.append(
            pltpu.make_async_remote_copy(
                src_ref=source,
                dst_ref=slots.at[me],
                send_sem=send_sem.at[step - 1],
                recv_sem=recv_sem.at[step - 1],
                device_id=place(there),
                device_id_type=MESH,
            )
        )
    for copy in copies:
        copy.start()
    return copies


def total_of(slots, ways):
    total = slots[0]
    for at in range(1, ways):
        total = total + slots[at]
    return total


def last_sum_kernel(
    bits, ways, part_ref, dots_ref, gains_ref, out_ref, dots_out_ref, gains_out_ref,
    sums, landed, dots_land, gains_land, gains_far, gains_mid, send_sem, recv_sem, dots_send, dots_recv,
    near_send, near_recv, far_send, far_recv,
):
    row_at = lax.axis_index("dp")
    me = lax.axis_index("tensor")
    pieces = 1 << bits

    def beside(there):
        return (row_at, there)

    def along(there):
        return (there, me)

    barrier = pltpu.get_barrier_semaphore()
    for step in range(1, pieces):
        pl.semaphore_signal(barrier, inc=1, device_id=beside(lax.rem(me + step, pieces)), device_id_type=MESH)
    for step in range(1, ways):
        pl.semaphore_signal(barrier, inc=1, device_id=along(lax.rem(row_at + step, ways)), device_id_type=MESH)
    pl.semaphore_wait(barrier, pieces + ways - 2)
    gains_land[me] = gains_ref[...]
    dots_land[me] = dots_ref[...]
    near = spread_kernel(gains_ref, gains_land, me, pieces, beside, near_send, near_recv)
    dots = spread_kernel(dots_ref, dots_land, me, pieces, beside, dots_send, dots_recv)
    for copy in near:
        copy.wait()
    gains_mid[...] = total_of(gains_land, pieces)
    gains_far[row_at] = gains_mid[...]
    far = spread_kernel(gains_mid, gains_far, row_at, ways, along, far_send, far_recv)
    tensor_sum_steps(bits, False, part_ref, out_ref, sums, landed, send_sem, recv_sem, None, None)
    for copy in dots:
        copy.wait()
    dots_out_ref[...] = total_of(dots_land, pieces)
    for copy in far:
        copy.wait()
    gains_out_ref[...] = total_of(gains_far, ways)


def last_sum(part, dots, gains, data_ways, collective_id):
    pieces, rows, width = part.shape
    bits = pieces.bit_length() - 1
    near = pltpu.SemaphoreType.DMA((pieces - 1,))
    far = pltpu.SemaphoreType.DMA((data_ways - 1,))
    return pl.pallas_call(
        functools.partial(last_sum_kernel, bits, data_ways),
        out_shape=(
            jax.ShapeDtypeStruct(part.shape[1:], part.dtype),
            jax.ShapeDtypeStruct(dots.shape, dots.dtype),
            jax.ShapeDtypeStruct(gains.shape, gains.dtype),
        ),
        in_specs=[pl.BlockSpec(memory_space=pltpu.VMEM)] * 3,
        out_specs=[pl.BlockSpec(memory_space=pltpu.VMEM)] * 3,
        scratch_shapes=[
            pltpu.VMEM(part.shape, part.dtype),
            pltpu.VMEM((pieces - 1, rows, width), part.dtype),
            pltpu.VMEM((pieces, *dots.shape), dots.dtype),
            pltpu.VMEM((pieces, *gains.shape), gains.dtype),
            pltpu.VMEM((data_ways, *gains.shape), gains.dtype),
            pltpu.VMEM(gains.shape, gains.dtype),
            *[pltpu.SemaphoreType.DMA((pieces - 1, SUM_BLOCKS))] * 2,
            near, near, near, near, far, far,
        ],
        compiler_params=pltpu.CompilerParams(
            collective_id=collective_id, has_side_effects=True, vmem_limit_bytes=32 * MIB
        ),
        cost_estimate=pl.CostEstimate(flops=0, bytes_accessed=128 * MIB, transcendentals=0),
    )(part, dots, gains)


def turned_by(values, signs):
    return pltpu.roll(values, values.shape[1] // 2, 1) * signs


def half_signs(head_dim, first):
    lanes = lax.broadcasted_iota(jnp.int32, (1, head_dim), 1)
    return jnp.where(lanes < head_dim // 2, first, -first)


def front_kernel(groups, head_dim, first, normed_ref, cos_ref, sin_ref, gains_ref, *refs):
    weights, raw_ref, outs = refs[:groups], refs[groups], refs[groups + 1 :]
    cosine = cos_ref[...]
    sine = sin_ref[...] * half_signs(head_dim, -1.0)
    for group in range(groups):
        pair = slice(group * 2 * head_dim, (group + 1) * 2 * head_dim)
        raw_ref[:, pair] = matmul(normed_ref[...], weights[group][...], NN)
        for at in range(2):
            base = (group * 2 + at) * head_dim
            raw = raw_ref[:, base : base + head_dim]
            if first + at < 3:
                gain = gains_ref[first // 2 : first // 2 + 1]
                scale = lax.rsqrt(jnp.mean(raw * raw, axis=1, keepdims=True) + EPSILON)
                raw = raw * scale * gain
                raw = raw * cosine + turned_by(raw, sine)
            out, place = (outs[group], at * head_dim) if first == 0 else (outs[0], base)
            out[:, place : place + head_dim] = raw.astype(out.dtype)


def front(normed, weight, groups, first, cosine, sine, gains, head_dim):
    rows, depth = normed.shape
    block = min(256, rows)
    width = groups * 2 * head_dim
    table = pl.BlockSpec((block, head_dim), lambda i: (i, 0))
    outs = [2 * head_dim] * groups if first == 0 else [width]

    def weight_spec(group):
        return pl.BlockSpec((depth, 2 * head_dim), lambda i: (0, 2 * group + first // 2), pipeline_mode=pl.Buffered(1))

    found = pl.pallas_call(
        functools.partial(front_kernel, groups, head_dim, first),
        grid=(rows // block,),
        in_specs=[pl.BlockSpec((block, depth), lambda i: (i, 0)), table, table, pl.BlockSpec(gains.shape, lambda i: (0, 0))]
        + [weight_spec(group) for group in range(groups)],
        out_specs=[pl.BlockSpec((block, columns), lambda i: (i, 0)) for columns in [width] + outs],
        out_shape=[jax.ShapeDtypeStruct((rows, width), jnp.float32)]
        + [jax.ShapeDtypeStruct((rows, columns), jnp.bfloat16) for columns in outs],
        compiler_params=pltpu.CompilerParams(vmem_limit_bytes=60 * MIB),
        cost_estimate=pl.CostEstimate(flops=2 * rows * depth * width, bytes_accessed=2 * depth * width, transcendentals=0),
    )(normed, cosine, sine, gains, *[weight] * groups)
    return found[0], found[1:]


def front_back_kernel(groups, head_dim, raw_query_ref, raw_key_ref, cos_ref, sin_ref, gains_ref, *refs):
    queries, keys = refs[:groups], refs[groups : 2 * groups]
    out_ref, sums_ref = refs[2 * groups :]

    @pl.when(pl.program_id(0) == 0)
    def _():
        sums_ref[...] = jnp.zeros_like(sums_ref)

    cosine = cos_ref[...]
    sine = sin_ref[...] * half_signs(head_dim, 1.0)
    for group in range(groups):
        for at in range(4):
            base = (group * 4 + at) * head_dim
            source = queries[group] if at < 2 else keys[group]
            grads = source[:, at % 2 * head_dim : (at % 2 + 1) * head_dim].astype(jnp.float32)
            if at < 3:
                gain = gains_ref[at // 2 : at // 2 + 1]
                place = (group * 2 + at % 2) * head_dim
                raw = (raw_query_ref if at < 2 else raw_key_ref)[:, place : place + head_dim]
                scale = lax.rsqrt(jnp.mean(raw * raw, axis=1, keepdims=True) + EPSILON)
                normal = raw * scale
                grads = grads * cosine + turned_by(grads, sine)
                sums_ref[at // 2 : at // 2 + 1] += jnp.sum(grads * normal, axis=0, keepdims=True)
                grads = grads * gain
                grads = scale * (grads - normal * jnp.mean(grads * normal, axis=1, keepdims=True))
            out_ref[:, base : base + head_dim] = grads.astype(out_ref.dtype)


def front_back(raw_queries, raw_keys, cosine, sine, gains, grad_queries, grad_kv, head_dim):
    rows, width = raw_queries.shape[0], 2 * raw_queries.shape[1]
    groups = width // (4 * head_dim)
    block = min(256, rows)
    half = pl.BlockSpec((block, width // 2), lambda i: (i, 0))
    narrow = pl.BlockSpec((block, 2 * head_dim), lambda i: (i, 0))
    table = pl.BlockSpec((block, head_dim), lambda i: (i, 0))
    wide = pl.BlockSpec((block, width), lambda i: (i, 0))
    return pl.pallas_call(
        functools.partial(front_back_kernel, groups, head_dim),
        grid=(rows // block,),
        in_specs=[half, half, table, table, pl.BlockSpec(gains.shape, lambda i: (0, 0))] + [narrow] * (2 * groups),
        out_specs=[wide, pl.BlockSpec((8, head_dim), lambda i: (0, 0))],
        out_shape=[
            jax.ShapeDtypeStruct((rows, width), jnp.bfloat16),
            jax.ShapeDtypeStruct((8, head_dim), jnp.float32),
        ],
        compiler_params=pltpu.CompilerParams(vmem_limit_bytes=60 * MIB),
        cost_estimate=pl.CostEstimate(flops=60 * rows * width, bytes_accessed=10 * rows * width, transcendentals=0),
    )(raw_queries, raw_keys, cosine, sine, gains, *grad_queries, *grad_kv)


def last_product_kernel(grad_ref, weight_ref, hidden_ref, scale_ref, gain_ref, out_ref, dots_ref, gain_out_ref):
    part = matmul(grad_ref[...], weight_ref[...], NT)
    out_ref[0] = part.astype(out_ref.dtype)
    product = part * (hidden_ref[...] * scale_ref[...])
    gain_out_ref[...] = jnp.sum(product, axis=0, keepdims=True)
    dots = jnp.sum(product * gain_ref[...], axis=1, keepdims=True)

    @pl.when(pl.program_id(0) == 0)
    def _():
        dots_ref[...] = dots

    @pl.when(pl.program_id(0) > 0)
    def _():
        dots_ref[...] += dots


def last_product(grads, weight, hidden, scale, gain, pieces):
    rows, width = grads.shape
    depth = weight.shape[0]
    block = depth // pieces // 2
    return pl.pallas_call(
        last_product_kernel,
        grid=(depth // block,),
        in_specs=[
            pl.BlockSpec((rows, width), lambda i: (0, 0), pipeline_mode=pl.Buffered(1)),
            pl.BlockSpec((block, width), lambda i: (i, 0)),
            pl.BlockSpec((rows, block), lambda i: (0, i)),
            pl.BlockSpec((rows, 1), lambda i: (0, 0)),
            pl.BlockSpec((1, block), lambda i: (0, i)),
        ],
        out_specs=[
            pl.BlockSpec((1, rows, block), lambda i: (i // 2, 0, i % 2)),
            pl.BlockSpec((rows, 1), lambda i: (0, 0)),
            pl.BlockSpec((1, block), lambda i: (0, i)),
        ],
        out_shape=[
            jax.ShapeDtypeStruct((pieces, rows, depth // pieces), jnp.bfloat16),
            jax.ShapeDtypeStruct((rows, 1), jnp.float32),
            jax.ShapeDtypeStruct((1, depth), jnp.float32),
        ],
        compiler_params=pltpu.CompilerParams(vmem_limit_bytes=60 * MIB),
        cost_estimate=pl.CostEstimate(flops=4 * rows * depth * width, bytes_accessed=2 * depth * width, transcendentals=0),
    )(grads, weight, hidden, scale, gain)


def resid_kernel(sum_ref, hidden_ref, gain_ref, resid_ref, normed_ref, normed_t_ref, scale_ref):
    total = jnp.concatenate([sum_ref[at] for at in range(sum_ref.shape[0])], axis=1)
    resid = hidden_ref[...] + total.astype(jnp.float32)
    scale = lax.rsqrt(jnp.mean(resid * resid, axis=1, keepdims=True) + EPSILON)
    normed = resid * scale * gain_ref[...]
    resid_ref[...] = resid
    scale_ref[...] = scale
    normed_ref[...] = normed.astype(normed_ref.dtype)
    normed_t_ref[...] = jnp.transpose(normed).astype(normed_t_ref.dtype)


def add_and_norm(total, hidden, gain):
    pieces, rows, width = total.shape
    depth = pieces * width
    block = min(256, rows)
    wide = pl.BlockSpec((block, depth), lambda i: (i, 0))
    return pl.pallas_call(
        resid_kernel,
        grid=(rows // block,),
        in_specs=[
            pl.BlockSpec((pieces, block, width), lambda i: (0, i, 0)),
            wide,
            pl.BlockSpec((1, depth), lambda i: (0, 0)),
        ],
        out_specs=[
            wide,
            wide,
            pl.BlockSpec((depth, block), lambda i: (0, i)),
            pl.BlockSpec((block, 1), lambda i: (i, 0)),
        ],
        out_shape=[
            jax.ShapeDtypeStruct((rows, depth), jnp.float32),
            jax.ShapeDtypeStruct((rows, depth), jnp.bfloat16),
            jax.ShapeDtypeStruct((depth, rows), jnp.bfloat16),
            jax.ShapeDtypeStruct((rows, 1), jnp.float32),
        ],
        compiler_params=pltpu.CompilerParams(vmem_limit_bytes=60 * MIB),
        cost_estimate=pl.CostEstimate(flops=10 * rows * depth, bytes_accessed=18 * rows * depth, transcendentals=0),
    )(total, hidden, gain)


def resid_back_kernel(sum_ref, cot_ref, resid_ref, scale_ref, gain_ref, grad_ref, rounded_ref, gain_out_ref):
    grads = jnp.concatenate([sum_ref[at] for at in range(sum_ref.shape[0])], axis=1).astype(jnp.float32)
    scale = scale_ref[...]
    normal = resid_ref[...] * scale
    sums = jnp.sum(grads * normal, axis=0, keepdims=True)
    grads = grads * gain_ref[...]
    grads = scale * (grads - normal * jnp.mean(grads * normal, axis=1, keepdims=True))
    grads = cot_ref[...].astype(jnp.float32) + grads
    grad_ref[...] = grads
    rounded_ref[...] = grads.astype(rounded_ref.dtype)

    @pl.when(pl.program_id(0) == 0)
    def _():
        gain_out_ref[...] = sums

    @pl.when(pl.program_id(0) > 0)
    def _():
        gain_out_ref[...] += sums


def norm_and_add_back(total, cotangent, resid, scale, gain):
    pieces, rows, width = total.shape
    depth = pieces * width
    block = min(256, rows)
    wide = pl.BlockSpec((block, depth), lambda i: (i, 0))
    whole = pl.BlockSpec((1, depth), lambda i: (0, 0))
    return pl.pallas_call(
        resid_back_kernel,
        grid=(rows // block,),
        in_specs=[
            pl.BlockSpec((pieces, block, width), lambda i: (0, i, 0)),
            wide,
            wide,
            pl.BlockSpec((block, 1), lambda i: (i, 0)),
            whole,
        ],
        out_specs=[wide, wide, whole],
        out_shape=[
            jax.ShapeDtypeStruct((rows, depth), jnp.float32),
            jax.ShapeDtypeStruct((rows, depth), jnp.bfloat16),
            jax.ShapeDtypeStruct((1, depth), jnp.float32),
        ],
        compiler_params=pltpu.CompilerParams(vmem_limit_bytes=60 * MIB),
        cost_estimate=pl.CostEstimate(flops=10 * rows * depth, bytes_accessed=16 * rows * depth, transcendentals=0),
    )(total, cotangent, resid, scale, gain)


def step_of(rate, weight, moment, average, gradient, outs):
    moment = MOMENTUM * moment + gradient
    weight = weight - rate * (gradient + MOMENTUM * moment)
    average = EMA_DECAY * average + (1.0 - EMA_DECAY) * weight
    for out, value in zip(outs, (weight, moment, average, average)):
        out[...] = value.astype(out.dtype)


def mlp_step_kernel(rate, steps_of, *refs):
    chunks = len(steps_of)
    grads, held, outs = refs[:chunks], refs[chunks : chunks + 6], refs[chunks + 6 :]
    begin = 0
    for chunk, steps in enumerate(steps_of):

        @pl.when((pl.program_id(0) >= begin) & (pl.program_id(0) < begin + steps))
        def _():
            both = grads[chunk][:2].astype(jnp.float32)
            step_of(rate, *(ref[...] for ref in held[:3]), both, outs[:4])
            down = jnp.transpose(grads[chunk][2].astype(jnp.float32))
            step_of(rate, *(ref[...] for ref in held[3:]), down, outs[4:])

        begin += steps


def mlp_step(rate, grads, gate_up, down):
    kinds, depth, _ = grads[0].shape
    block = min(FF_BLOCK, grads[0].shape[2])
    steps_of = [grad.shape[2] // block for grad in grads]

    def grad_spec(chunk):
        begin, last = sum(steps_of[:chunk]), steps_of[chunk] - 1
        return pl.BlockSpec((kinds, depth, block), lambda i: (0, 0, jnp.clip(i - begin, 0, last)))

    gate_up_spec = pl.BlockSpec((2, depth, block), lambda i: (0, 0, i))
    down_spec = pl.BlockSpec((block, depth), lambda i: (i, 0))
    types = (jnp.float32,) * 3 + (jnp.bfloat16,)
    return pl.pallas_call(
        functools.partial(mlp_step_kernel, rate, steps_of),
        grid=(sum(steps_of),),
        in_specs=[grad_spec(chunk) for chunk in range(len(grads))] + [gate_up_spec] * 3 + [down_spec] * 3,
        out_specs=[gate_up_spec] * 4 + [down_spec] * 4,
        out_shape=[jax.ShapeDtypeStruct(gate_up[0].shape, kind) for kind in types]
        + [jax.ShapeDtypeStruct(down[0].shape, kind) for kind in types],
        compiler_params=pltpu.CompilerParams(vmem_limit_bytes=40 * MIB),
        cost_estimate=pl.CostEstimate(flops=0, bytes_accessed=26 * sum(grad.size for grad in grads), transcendentals=0),
    )(*grads, *gate_up, *down)


def turned_step_kernel(rate, grad_ref, *refs):
    step_of(rate, *(ref[...] for ref in refs[:3]), jnp.transpose(grad_ref[...].astype(jnp.float32)), refs[3:])


def turned_step(rate, grad_t, held):
    types = (jnp.float32,) * 3 + (jnp.bfloat16,)
    return pl.pallas_call(
        functools.partial(turned_step_kernel, rate),
        in_specs=[pl.BlockSpec(memory_space=pltpu.VMEM)] * 4,
        out_specs=[pl.BlockSpec(memory_space=pltpu.VMEM)] * 4,
        out_shape=[jax.ShapeDtypeStruct(held[0].shape, kind) for kind in types],
        compiler_params=pltpu.CompilerParams(vmem_limit_bytes=60 * MIB),
        cost_estimate=pl.CostEstimate(flops=0, bytes_accessed=28 * grad_t.size, transcendentals=0),
    )(grad_t, *held)


def out_product_kernel(left_ref, weight_ref, out_ref):
    out_ref[0] = matmul(left_ref[...], weight_ref[...], NT).astype(out_ref.dtype)


def out_product(left, weight, column, pieces):
    rows, width = left.shape
    depth = weight.shape[0]
    block = depth // pieces // 2
    return pl.pallas_call(
        out_product_kernel,
        grid=(depth // block,),
        in_specs=[
            pl.BlockSpec((rows, width), lambda i: (0, 0), pipeline_mode=pl.Buffered(1)),
            pl.BlockSpec((block, width), lambda i: (i, column)),
        ],
        out_specs=pl.BlockSpec((1, rows, block), lambda i: (i // 2, 0, i % 2)),
        out_shape=jax.ShapeDtypeStruct((pieces, rows, depth // pieces), jnp.bfloat16),
        compiler_params=pltpu.CompilerParams(vmem_limit_bytes=60 * MIB),
        cost_estimate=pl.CostEstimate(flops=2 * rows * depth * width, bytes_accessed=2 * depth * width, transcendentals=0),
    )(left, weight)


def weight_products_kernel(normed_ref, grad_ref, left_ref, mixed_ref, out_ref):
    width = grad_ref.shape[1]
    out_ref[:, :width] = matmul(normed_ref[...], grad_ref[...], TN).astype(out_ref.dtype)
    out_ref[:, width:] = matmul(left_ref[...], mixed_ref[...], TN).astype(out_ref.dtype)


def weight_products(normed, grads, left, mixed):
    rows, depth = normed.shape
    block = min(256, depth)
    width = grads.shape[1] + mixed.shape[1]
    column = pl.BlockSpec((rows, block), lambda i: (0, i))

    def held(array):
        return pl.BlockSpec(array.shape, lambda i: (0, 0), pipeline_mode=pl.Buffered(1))

    return pl.pallas_call(
        weight_products_kernel,
        grid=(depth // block,),
        in_specs=[column, held(grads), column, held(mixed)],
        out_specs=pl.BlockSpec((block, width), lambda i: (i, 0)),
        out_shape=jax.ShapeDtypeStruct((depth, width), jnp.bfloat16),
        compiler_params=pltpu.CompilerParams(vmem_limit_bytes=60 * MIB),
        cost_estimate=pl.CostEstimate(flops=2 * rows * depth * width, bytes_accessed=2 * depth * width, transcendentals=0),
    )(normed, grads, left, mixed)


def rms_scale(values_in):
    return lax.rsqrt(jnp.mean(values_in * values_in, axis=-1, keepdims=True) + EPSILON)


def rope_tables(offsets, head_dim):
    half_dim = head_dim // 2
    frequency = 1.0 / ROPE_BASE ** (jnp.arange(half_dim, dtype=jnp.float32) * 2.0 / head_dim)
    angles = offsets.astype(jnp.float32)[:, None] * frequency[None, :]
    cosine = jnp.cos(angles)
    sine = jnp.sin(angles)
    return (jnp.concatenate([cosine, cosine], axis=-1), jnp.concatenate([sine, sine], axis=-1))


def nesterov(weight, moment, average, gradient, rate):
    new_moment = MOMENTUM * moment + gradient
    new_weight = weight - rate * (gradient + MOMENTUM * new_moment)
    new_average = EMA_DECAY * average + (1.0 - EMA_DECAY) * new_weight
    return (new_weight, new_moment, new_average, new_average.astype(jnp.bfloat16))


def dot(a, b, dims):
    return lax.dot_general(a, b, dims, preferred_element_type=jnp.float32)


def tie(*values):
    return lax.optimization_barrier(values)


def local(
    hidden_in,
    cotangent,
    doc_lengths,
    valid_mask,
    w_qkv,
    w_out,
    w_gate_up,
    w_down,
    norm_gains,
    m_qkv,
    m_out,
    m_gate_up,
    m_down,
    m_gains,
    a_qkv,
    a_out,
    a_gate_up,
    a_down,
    a_gains,
):
    row_count, model_dim = hidden_in.shape
    head_dim = (norm_gains.shape[0] - 2 * model_dim) // 2
    data_ways = lax.axis_size("dp")
    tensor_ways = lax.axis_size("tensor")
    tensor_at = lax.axis_index("tensor")
    tokens_all = row_count * data_ways
    width_cols = model_dim // tensor_ways
    col_begin = tensor_at * width_cols
    groups = w_qkv.shape[1] // (4 * head_dim)
    ff_local = w_down.shape[0]
    ff_unit = ff_local // CHUNK_ENDS[-1]
    bf16 = jnp.bfloat16
    f32 = jnp.float32

    def columns_of(values_in):
        return lax.dynamic_slice_in_dim(values_in, col_begin, width_cols, values_in.ndim - 1)

    qkv_cols, out_rows = w_qkv.shape[1], w_out.shape[0]
    qkv_out = lax.all_gather(jnp.concatenate([w_qkv, w_out.T], axis=1).astype(bf16), "dp", axis=0, tiled=True)

    ends_at = jnp.cumsum(doc_lengths)
    starts_at = ends_at - doc_lengths
    place_begin = lax.axis_index("dp") * row_count
    places = place_begin + jnp.arange(row_count, dtype=jnp.int32)
    doc_ids = jnp.sum((places[:, None] >= ends_at[None, :]).astype(jnp.int32), axis=1)
    owned = doc_ids[:, None] == jnp.arange(doc_lengths.shape[0], dtype=jnp.int32)[None, :]
    doc_begin = jnp.sum(jnp.where(owned, starts_at[None, :], 0), axis=1)
    cosine, sine = rope_tables(places - doc_begin, head_dim)
    query_rows = min(512, row_count)
    blocks = row_count // query_rows
    bounds = jnp.stack(
        [
            place_begin + jnp.arange(blocks, dtype=jnp.int32) * query_rows,
            doc_begin[::query_rows],
            doc_begin[query_rows - 1 :: query_rows],
        ]
    ).astype(jnp.int32)
    begin_rows = doc_begin.astype(jnp.int32).reshape(blocks, 1, query_rows)

    gain_attn = norm_gains[:model_dim]
    gain_mlp = norm_gains[model_dim : 2 * model_dim]
    gain_query = norm_gains[2 * model_dim : 2 * model_dim + head_dim]
    gain_key = norm_gains[2 * model_dim + head_dim :]
    scale_one = rms_scale(hidden_in)
    normal_one = hidden_in * scale_one
    normed_one_b = (normal_one * gain_attn).astype(bf16)
    gains_two = jnp.stack([gain_query, gain_key])
    raw_keys, (kv_local,) = front(
        normed_one_b, qkv_out, groups, 2, cosine, sine, gains_two, head_dim
    )
    normed_one_b, kv_local = tie(normed_one_b, kv_local)
    kv_every = lax.all_gather(kv_local, "dp", axis=0, tiled=True)
    raw_queries, queries = front(
        normed_one_b, qkv_out, groups, 0, cosine, sine, gains_two, head_dim
    )

    down_t = w_down.T

    def chunk_shard(chunk):
        units = slice(CHUNK_ENDS[chunk] * ff_unit, CHUNK_ENDS[chunk + 1] * ff_unit)
        return jnp.stack([w_gate_up[0, :, units], w_gate_up[1, :, units], down_t[:, units]]).astype(bf16)

    def chunk_gather(shard):
        return lax.all_gather(shard, "dp", axis=0)

    shard, kv_every, cotangent_t, queries = tie(chunk_shard(0), kv_every, cotangent.T, queries)
    chunk_weights = [chunk_gather(shard)]
    mixed, totals = [], []
    for group in range(groups):
        mixed_rows, total_rows = attend(
            bounds, queries[group], begin_rows, kv_every, group, head_dim, query_rows, min(1024, tokens_all)
        )
        mixed.append(mixed_rows)
        totals.append(total_rows)
    mixed_b = jnp.concatenate(mixed, axis=1)
    attn_part = out_product(mixed_b, qkv_out, qkv_cols // out_rows, tensor_ways)
    shard, chunk_weights[0], attn_part = tie(chunk_shard(1), chunk_weights[0], attn_part)
    chunk_weights.append(chunk_gather(shard))
    attn_sum = tensor_sum(attn_part, 0)
    resid_one, normed_two_b, normed_two_t, scale_two = add_and_norm(attn_sum, hidden_in, gain_mlp[None])

    mask_rows = valid_mask.astype(f32)[:, None]

    def squares_of(columns):
        return jnp.sum(mask_rows * columns * columns)

    stats_early, chunk_weights[1] = tie(
        jnp.stack(
            [
                squares_of(columns_of(hidden_in)),
                squares_of(lax.dynamic_index_in_dim(attn_sum, tensor_at, 0, False).astype(f32)),
                jnp.where(tensor_at == 0, jnp.sum(valid_mask.astype(f32)), 0.0),
            ]
        ),
        chunk_weights[1],
    )
    weight_grads, hiddens, back_pairs = [], [], []
    for weights in chunk_weights:
        hidden_b, gate_grad, up_grad, weight_grad = mlp_chunk(
            normed_two_b, cotangent, normed_two_t, cotangent_t, weights
        )
        hiddens.append((hidden_b,))
        back_pairs.append((gate_grad, up_grad))
        weight_grads.append(lax.psum_scatter(weight_grad, "dp", scatter_dimension=0))

    part_two = back_product(back_pairs, chunk_weights, 0, tensor_ways)
    part_two_sum, weight_grads[0] = tie(tensor_sum(part_two, 1), weight_grads[0])
    grad_resid, grad_attn_b, gain_mlp_part = norm_and_add_back(
        part_two_sum, cotangent, resid_one, scale_two, gain_mlp[None]
    )
    grad_mixed_b = dot(grad_attn_b, qkv_out[:, qkv_cols:], NN).astype(bf16)

    grad_queries, kv_sums = [], []
    for group in range(groups):
        grad_rows = grad_mixed_b[:, group * 2 * head_dim : (group + 1) * 2 * head_dim]
        if group and group == groups - 1:
            grad_rows, weight_grads[1], kv_sums[-1] = tie(grad_rows, weight_grads[1], kv_sums[-1])
        grad_query, kv_sum = attend_back(
            bounds,
            queries[group],
            grad_rows,
            mixed[group],
            totals[group],
            begin_rows,
            kv_every,
            group,
            head_dim,
            query_rows,
            min(512, tokens_all),
        )
        grad_queries.append(grad_query)
        kv_sums.append(kv_sum)
    kv_grads = []
    for group in range(groups):
        if group:
            kv_grads[-1], kv_sums[group] = tie(kv_grads[-1], kv_sums[group])
        kv_grads.append(lax.psum_scatter(kv_sums[group], "dp", scatter_dimension=0, tiled=True))
    hidden_b, grad_queries[-1] = tie(hiddens[0][0], grad_queries[-1])
    mlp_part = back_product([(hidden_b,), *hiddens[1:]], chunk_weights, 2, tensor_ways)
    rate_matrix = LR_MATRIX / math.sqrt(tokens_all)
    mlp_sum, kv_grads[-1], updates = tie(
        tensor_sum(mlp_part, 2, False),
        kv_grads[-1],
        mlp_step(rate_matrix, weight_grads, (w_gate_up, m_gate_up, a_gate_up), (w_down, m_down, a_down)),
    )
    grad_projected_b, gains_found = front_back(
        raw_queries, raw_keys, cosine, sine, gains_two, grad_queries, kv_grads, head_dim
    )
    both_grads, grad_projected_b, mlp_sum = tie(
        weight_products(normed_one_b, grad_projected_b, grad_attn_b, mixed_b), grad_projected_b, mlp_sum
    )
    both_shard = lax.psum_scatter(both_grads, "dp", scatter_dimension=0, tiled=True)
    qkv_shard = both_shard[:, :qkv_cols].astype(f32)
    part_one, dots_part, gain_attn_part = last_product(
        grad_projected_b, qkv_out, hidden_in, scale_one, gain_attn[None], tensor_ways
    )

    mlp_cols = mlp_sum.astype(f32)
    mixed_cols = columns_of(resid_one) + mlp_cols
    stats_part = jnp.concatenate([stats_early[:2], squares_of(mlp_cols)[None], stats_early[2:]])
    gain_mlp_wide = lax.dynamic_update_slice_in_dim(
        jnp.zeros((model_dim,), f32), columns_of(gain_mlp_part[0]), col_begin, 0
    )
    gains_part = jnp.concatenate(
        [gain_attn_part[0], gain_mlp_wide, gains_found[0], gains_found[1], stats_part]
    )
    gains_count = gains_part.shape[0]
    gains_rows = -(-gains_count // 1024) * 8
    gains_part = jnp.pad(gains_part, (0, gains_rows * 128 - gains_count)).reshape(gains_rows, 128)
    grad_one_cols, row_dots, gains_sum = last_sum(
        part_one, dots_part.reshape(row_count // 128, 128), gains_part, data_ways, 3
    )
    gains_sum = gains_sum.reshape(-1)[:gains_count]
    grad_cols = columns_of(grad_resid) + scale_one * (
        grad_one_cols.astype(f32) * columns_of(gain_attn)
        - columns_of(normal_one) * (row_dots.reshape(row_count, 1) / model_dim)
    )
    grad_gains = gains_sum[: norm_gains.shape[0]]
    stats_sum = gains_sum[norm_gains.shape[0] :]
    branch_rms = jnp.sqrt(stats_sum[:3] / (stats_sum[3] * model_dim))

    rate_gain = LR_GAIN / math.sqrt(tokens_all)
    return (
        mixed_cols,
        grad_cols,
        branch_rms,
        *nesterov(w_qkv, m_qkv, a_qkv, qkv_shard, rate_matrix),
        *turned_step(rate_matrix, both_shard[:, qkv_cols:], (w_out, m_out, a_out)),
        *updates,
        *nesterov(norm_gains, m_gains, a_gains, grad_gains, rate_gain),
    )


def solution(mesh):
    rows = P("dp", None)
    spread = P("dp", "tensor")
    turned = P("tensor", "dp")
    stacked = P(None, "dp", "tensor")
    matrices = (spread, turned, stacked, turned, P())
    in_specs = (rows, rows, P(), P("dp"), *matrices, *matrices, *matrices)
    out_specs = (spread, spread, P(), *(spec for spec in matrices for _ in range(4)))
    return jax.shard_map(local, mesh=mesh, in_specs=in_specs, out_specs=out_specs, check_vma=False)
```
